128 devices in a mesh: ctx: 8 (over z, y_lo), fsdp: 16 (over y_hi, x, core).
Axes of the slice: x: 4, y: 4 (y_hi: 2, y_lo: 2; y = y_hi * 2 + y_lo), z: 4, core: 2. Of those that a mesh axis runs over, the one named last changes fastest.
Arguments:
- tokens: bfloat16 [2048, 2880], P(('ctx', 'fsdp')), may hold values from -6 to 6
- attn_gain: float32 [2880], replicated, may hold values from 0.1 to 1.9
- query_weight: bfloat16 [2880, 4096], P(None, 'fsdp'), may hold values from -4 to 4
- keyval_weight: bfloat16 [1024, 2880], P('fsdp'), may hold values from -0.109375 to 0.109375
- sink_logits: float32 [64], P('fsdp'), may hold values from 1 to 6
- out_weight: bfloat16 [4096, 2880], P('fsdp'), may hold values from -0.09375 to 0.09375
- mlp_gain: float32 [2880], replicated, may hold values from 0.1 to 1.9
- routes: int32 [2048, 4], P(('ctx', 'fsdp')), may hold values from 0 to 63, all different within a row; in each aligned block of 16 rows (0 to 15, 16 to 31, ...) at most 2 rows name the same one
- gate_fixed: int32 [2048, 4], P(('ctx', 'fsdp')), may hold values from 1 to 65533, as said below
- gate_weight: bfloat16 [64, 1440, 2880], P('fsdp', 'ctx'), may hold values from -0.109375 to 0.109375
- up_weight: bfloat16 [64, 1440, 2880], P('fsdp', 'ctx'), may hold values from -0.109375 to 0.109375
- down_weight: bfloat16 [64, 1440, 2880], P('fsdp', 'ctx'), may hold values from -0.15625 to 0.15625
Outputs:
- layer_out: bfloat16 [2048, 2880], P(('ctx', 'fsdp'))
The draws below stay inside these ranges and needn't reach their ends.
Inputs may be any that keep to these rules, and one draw needn't show every extreme that they name: `routes`: each row names 4 different experts; within the rows of one device (aligned blocks of 16 rows) no expert is named by more than 2 rows, a bound that some block reaches. `gate_fixed`: the 4 values of each row are positive and add up to 65536.
All inputs are finite; a program needn't handle non-finite values.
Results may differ from the reference program's by a relative error of at most 0.018.
Values may be sent and summed in bfloat16 or wider, within the bound.
A program may use at most 128 MiB of HBM per device.

```python
import math
import jax
import jax.numpy as jnp
import numpy as np
from jax import lax

D = 2880
HEADS = 64
KV_HEADS = 8
HEAD_DIM = 64
WINDOW = 128
TOP = 4
EXP_F = 4
HID = 1440
TOK_DEV = 16
TOKENS = 2048
MOST = 2
N_CTX = 8
N_FSDP = 16


def draw_query_weight(key, part):
    key = jax.random.fold_in(key, 11)
    base_key, head_key = jax.random.split(key)
    base = jax.random.truncated_normal(base_key, -6.0, 6.0, (D, HEADS * HEAD_DIM), jnp.float32) * D ** (-0.5)
    factor = jnp.exp(jax.random.uniform(head_key, (HEADS,), jnp.float32, math.log(0.7), math.log(1.4)))
    scaled = jnp.clip(base * jnp.repeat(factor, HEAD_DIM)[None, :], -4.0, 4.0)
    return scaled.astype(jnp.bfloat16)


def draw_gate_fixed(key, part):
    key = jax.random.fold_in(key, 23)
    raw_key, row_key = jax.random.split(key)
    raw = jax.random.randint(raw_key, (TOKENS, TOP), 1, 1000, dtype=jnp.int32)
    row_total = jnp.sum(raw, axis=1, keepdims=True)
    base = raw * 65536 // row_total
    missing = 65536 - jnp.sum(base, axis=1)
    filled = base.at[:, 0].add(missing).astype(jnp.int32)
    picked_row = jax.random.randint(row_key, (), 0, TOKENS, dtype=jnp.int32)
    extreme = jnp.ones((TOP,), jnp.int32).at[0].set(65537 - TOP)
    marker = (jnp.arange(TOKENS, dtype=jnp.int32) == picked_row)[:, None]
    return jnp.where(marker, extreme[None, :], filled).astype(jnp.int32)


def steps_of(rng, extent, cuts, low, top_value):
    level = 1.0
    for position, blocks in cuts:
        draws = jax.random.uniform(jax.random.fold_in(jax.random.fold_in(rng, 6), position), (blocks,), jnp.float32, low / len(cuts), top_value / len(cuts))
        level = level * jnp.repeat(jnp.exp(draws), extent[position] // blocks).reshape((-1,) + (1,) * (len(extent) - 1 - position))
    return level


def shared_out(rng, own, number, rows, count, top, limit, slope):
    order = jax.random.permutation(rng, count)
    heavy_load, common = load_shares(count, rows * top, limit, slope, True), load_shares(count, rows * top, limit, slope, False)
    places = jnp.arange(count)

    def named(tallies, turn):
        used = int((tallies > 0).sum())
        fixed = max(1, used // 4)
        moved = fixed + (places - fixed + turn * (used - fixed)) % max(1, count - fixed)
        return jnp.zeros((count,), jnp.int32).at[order[jnp.where(places < fixed, places, moved)]].set(jnp.asarray(tallies, jnp.int32))

    tallies = jnp.where(number % 4 == 0, named(heavy_load, number // 4), named(common, number - number // 4 - 1))
    mixed = jax.random.permutation(jax.random.fold_in(own, 3), count)
    donor, taker = mixed[0:count // 2 * 2:2], mixed[1:count // 2 * 2:2]
    margin = jnp.minimum(tallies[donor] - 1, limit - tallies[taker]) // 2
    margin = jnp.where((donor == order[0]) | (taker == order[0]) | (tallies[taker] == 0), 0, jnp.maximum(margin, 0))
    moved = jax.random.randint(jax.random.fold_in(own, 4), (count // 2,), 0, 1 << 20) % (margin + 1)
    tallies = tallies.at[donor].add(-moved).at[taker].add(moved)
    labels = jnp.searchsorted(jnp.cumsum(tallies), jnp.arange(rows * top), side="right").astype(jnp.int32)
    grid = labels.reshape(top, rows).T
    grid = grid[jax.random.permutation(jax.random.fold_in(own, 1), rows)]
    turn = jax.random.randint(jax.random.fold_in(own, 2), (rows, 1), 0, top)
    return jnp.take_along_axis(grid, (jnp.arange(top)[None, :] + turn) % top, axis=1)


def load_shares(number_of, total, bound, lean, full):
    weights = [(1 << 20) // math.isqrt(standing ** lean) + 1 for standing in range(1, number_of + 1)]
    largest = bound if full else min(bound, max(-(-total // number_of), total * weights[0] // sum(weights)))
    least = 1 if total - largest >= number_of - 1 else 0
    given, rest = [largest] + [least] * (number_of - 1), total - largest - least * (number_of - 1)
    while rest > 0:
        free = [i for i in range(1, number_of) if given[i] < largest] or [i for i in range(1, number_of) if given[i] < bound]
        pool, left = sum([weights[i] for i in free]), rest
        for i in free:
            extra = min(bound - given[i], max(1, left * weights[i] // pool), rest)
            given[i] = given[i] + extra
            rest = rest - extra
    return np.array(given)


def scatter_about(stream_key, dims, width, limit, shards=(), held_as=jnp.bfloat16):
    drawn = jax.random.normal(stream_key, dims, jnp.float32) * width
    if len(shards) > 0:
        drawn = steps_of(stream_key, dims, shards, -0.22, 0.18) * drawn
    return jnp.clip(drawn, min=-limit, max=limit).astype(held_as)


def setup_inputs(seed: int = 0) -> dict:
    key_of = jax.random.split(jax.random.key(seed), 13)
    tokens = scatter_about(key_of[0], (TOKENS, D), 1.0, 6.0, ((0, 128),))
    attn_gain = jnp.clip(1.0 + 0.18 * jax.random.normal(key_of[1], (D,), jnp.float32), 0.1, 1.9)
    query_weight = draw_query_weight(jax.random.fold_in(key_of[12], 71), 0)
    keyval_weight = scatter_about(key_of[3], (2 * KV_HEADS * HEAD_DIM, D), D ** -0.5, 0.109375, ((0, 16),))
    sink_logits = jnp.clip(1.0 + 5.0 * jax.random.uniform(key_of[4], (HEADS,), jnp.float32) ** steps_of(key_of[4], (HEADS,), ((0, 16),), -0.2, 0.2), 1.0, 6.0)
    out_weight = scatter_about(key_of[5], (HEADS * HEAD_DIM, D), (HEADS * HEAD_DIM) ** -0.5, 0.09375, ((0, 16),))
    mlp_gain = jnp.clip(1.0 + 0.18 * jax.random.normal(key_of[6], (D,), jnp.float32), 0.1, 1.9)
    routes_keys = jax.random.split(jax.random.fold_in(key_of[7], 1), TOKENS // TOK_DEV)
    routes_turns = jax.random.permutation(jax.random.fold_in(key_of[7], 3), TOKENS // TOK_DEV)
    routes = jax.vmap(lambda own, number: shared_out(jax.random.fold_in(key_of[7], 2), own, number, TOK_DEV, EXP_F * N_FSDP, TOP, MOST, 2))(routes_keys, routes_turns).reshape((TOKENS, TOP))
    gate_fixed = draw_gate_fixed(jax.random.fold_in(key_of[12], 71), 0)
    gate_weight = scatter_about(key_of[9], (EXP_F * N_FSDP, HID, D), D ** -0.5, 0.109375, ((0, 16), (1, 8)))
    up_weight = scatter_about(key_of[10], (EXP_F * N_FSDP, HID, D), D ** -0.5, 0.109375, ((0, 16), (1, 8)))
    down_weight = scatter_about(key_of[11], (EXP_F * N_FSDP, HID, D), HID ** -0.5, 0.15625, ((0, 16), (1, 8)))
    return {"tokens": tokens, "attn_gain": attn_gain, "query_weight": query_weight, "keyval_weight": keyval_weight, "sink_logits": sink_logits, "out_weight": out_weight, "mlp_gain": mlp_gain, "routes": routes, "gate_fixed": gate_fixed, "gate_weight": gate_weight, "up_weight": up_weight, "down_weight": down_weight}


rope_theta = 150000.0
norm_eps = 1e-05
glu_alpha = 1.702
fixed_scale = 65536.0

def rms_scale(values, gain):
    mean_sq = lax.optimization_barrier(jnp.mean(values * values, axis=-1, keepdims=True))
    return values * lax.rsqrt(mean_sq + norm_eps) * gain

def rotate(tensor, positions):
    half_dim = tensor.shape[-1] // 2
    freqs = rope_theta ** (-(jnp.arange(half_dim, dtype=jnp.float32) * 2.0 / tensor.shape[-1]))
    angles = positions[:, None] * freqs[None, :]
    cosine = jnp.cos(angles)[:, None, :]
    sine = jnp.sin(angles)[:, None, :]
    first = tensor[..., :half_dim]
    second = tensor[..., half_dim:]
    return jnp.concatenate([first * cosine - second * sine, second * cosine + first * sine], axis=-1)

def rounded(values):
    narrow = lax.optimization_barrier(values.astype(jnp.bfloat16))
    return narrow.astype(jnp.float32)

def dot_rows(left, right):
    return lax.dot_general(left, right, (((1,), (1,)), ((), ())), preferred_element_type=jnp.float32)

def expert_slots(route_block, num_experts, capacity):
    flat_ids = route_block.reshape(-1).astype(jnp.int32)
    onehot = (flat_ids[:, None] == jnp.arange(num_experts, dtype=jnp.int32)[None, :]).astype(jnp.int32)
    before = jnp.cumsum(onehot, axis=0) - onehot
    slot = lax.optimization_barrier(jnp.sum(before * onehot, axis=1)).astype(jnp.int32)
    return (flat_ids * capacity + slot).astype(jnp.int32)

def reference(tokens, attn_gain, query_weight, keyval_weight, sink_logits, out_weight, mlp_gain, routes, gate_fixed, gate_weight, up_weight, down_weight):
    token_vals = tokens.astype(jnp.float32)
    normed = rms_scale(token_vals, attn_gain).astype(jnp.bfloat16)
    positions = jnp.arange(TOKENS, dtype=jnp.float32)
    query_all = jnp.dot(normed, query_weight, preferred_element_type=jnp.float32).reshape(TOKENS, HEADS, HEAD_DIM)
    query_all = rotate(query_all, positions).astype(jnp.bfloat16)
    keyval = dot_rows(normed, keyval_weight)
    key_all = rotate(keyval[:, :KV_HEADS * HEAD_DIM].reshape(TOKENS, KV_HEADS, HEAD_DIM), positions).astype(jnp.bfloat16)
    value_all = keyval[:, KV_HEADS * HEAD_DIM:].reshape(TOKENS, KV_HEADS, HEAD_DIM).astype(jnp.bfloat16)
    group = HEADS // KV_HEADS
    key_pad = jnp.concatenate([jnp.zeros((WINDOW, KV_HEADS, HEAD_DIM), jnp.bfloat16), key_all], axis=0)
    value_pad = jnp.concatenate([jnp.zeros((WINDOW, KV_HEADS, HEAD_DIM), jnp.bfloat16), value_all], axis=0)

    def band_block(block_index):
        start = (block_index * WINDOW).astype(jnp.int32)
        query_rows = lax.dynamic_slice_in_dim(query_all, start, WINDOW, 0)
        key_rows = jnp.repeat(lax.dynamic_slice_in_dim(key_pad, start, 2 * WINDOW, 0), group, axis=1)
        value_rows = jnp.repeat(lax.dynamic_slice_in_dim(value_pad, start, 2 * WINDOW, 0), group, axis=1)
        scores = jnp.einsum('qhd,khd->hqk', query_rows.astype(jnp.float32), key_rows.astype(jnp.float32)) * HEAD_DIM ** (-0.5)
        query_pos = start + jnp.arange(WINDOW, dtype=jnp.int32)
        key_pos = start - WINDOW + jnp.arange(2 * WINDOW, dtype=jnp.int32)
        allowed = (key_pos[None, :] <= query_pos[:, None]) & (key_pos[None, :] > query_pos[:, None] - WINDOW) & (key_pos[None, :] >= 0)
        masked = jnp.where(allowed[None], scores, -1e+30)
        top_score = jnp.maximum(lax.optimization_barrier(jnp.max(masked, axis=-1)), sink_logits[:, None])
        expd = jnp.exp(masked - top_score[..., None])
        total = jnp.exp(sink_logits[:, None] - top_score) + lax.optimization_barrier(jnp.sum(expd, axis=-1))
        probs = rounded(expd / total[..., None])
        mixed = jnp.einsum('hqk,khd->qhd', probs, value_rows.astype(jnp.float32))
        return mixed.astype(jnp.bfloat16).reshape(WINDOW, HEADS * HEAD_DIM)
    attended = lax.map(band_block, jnp.arange(TOKENS // WINDOW, dtype=jnp.int32)).reshape(TOKENS, HEADS * HEAD_DIM)
    resid = token_vals + jnp.dot(attended, out_weight, preferred_element_type=jnp.float32)
    ffn_in = rms_scale(resid, mlp_gain).astype(jnp.bfloat16)
    num_experts = EXP_F * N_FSDP
    blocks = TOKENS // TOK_DEV
    route_blocks = routes.reshape(blocks, TOK_DEV, TOP)
    slot_pos = jax.vmap(lambda route_block: expert_slots(route_block, num_experts, MOST))(route_blocks)
    block_ids = jnp.broadcast_to(jnp.arange(blocks, dtype=jnp.int32)[:, None], slot_pos.shape)
    route_rows = jnp.repeat(ffn_in.reshape(blocks, TOK_DEV, D), TOP, axis=1)
    buffer = jnp.zeros((blocks, num_experts * MOST, D), jnp.bfloat16).at[block_ids, slot_pos].set(route_rows)
    expert_rows = buffer.reshape(blocks, num_experts, MOST, D).transpose(1, 0, 2, 3).reshape(num_experts, blocks * MOST, D)
    part_width = HID // N_CTX

    def run_expert(operands):
        rows, gate_mat, up_mat, down_mat = operands
        gate_val = dot_rows(rows, gate_mat)
        up_val = dot_rows(rows, up_mat)
        hidden = rounded(gate_val * jax.nn.sigmoid(glu_alpha * gate_val) * (up_val + 1.0))
        pieces = jnp.einsum('nch,chd->cnd', hidden.reshape(-1, N_CTX, part_width), down_mat.reshape(N_CTX, part_width, D).astype(jnp.float32))
        return lax.optimization_barrier(jnp.sum(rounded(pieces), axis=0)).astype(jnp.bfloat16)
    expert_out = lax.map(run_expert, (expert_rows, gate_weight, up_weight, down_weight)).reshape(num_experts, blocks, MOST, D)
    picked = expert_out[slot_pos // MOST, block_ids, slot_pos % MOST].reshape(TOKENS, TOP, D).astype(jnp.float32)
    route_weights = gate_fixed.astype(jnp.float32) / fixed_scale
    moe_sum = lax.optimization_barrier(jnp.sum(picked * route_weights[..., None], axis=1))
    return (resid + moe_sum).astype(jnp.bfloat16)
```

```python
import jax
import jax.numpy as jnp
from jax import lax
from jax.sharding import PartitionSpec as P

HEADS = 64
KV_HEADS = 8
HEAD_DIM = 64
WINDOW = 128
TOP = 4


rope_theta = 150000.0
norm_eps = 1e-05
glu_alpha = 1.702
fixed_scale = 65536.0


def from_behind(x, axis, by):
    count = lax.axis_size(axis)
    pairs = [(i, i + by) for i in range(count) if 0 <= i + by < count]
    return lax.ppermute(x, axis, pairs)


def rms_scale(values, gain):
    mean_sq = jnp.mean(values * values, axis=-1, keepdims=True)
    return values * lax.rsqrt(mean_sq + norm_eps) * gain


def rotate(tensor, positions):
    half_dim = tensor.shape[-1] // 2
    freqs = rope_theta ** (-(jnp.arange(half_dim, dtype=jnp.float32) * 2.0 / tensor.shape[-1]))
    angles = positions[:, None] * freqs[None, :]
    cosine = jnp.cos(angles)[:, None, :]
    sine = jnp.sin(angles)[:, None, :]
    first = tensor[..., :half_dim]
    second = tensor[..., half_dim:]
    return jnp.concatenate(
        [first * cosine - second * sine, second * cosine + first * sine], axis=-1
    )


def expert_slots(route_block, num_experts, capacity):
    flat_ids = route_block.reshape(-1)
    order = jnp.arange(flat_ids.shape[0], dtype=jnp.int32)
    earlier = (order[None, :] < order[:, None]) & (flat_ids[None, :] == flat_ids[:, None])
    slot = jnp.sum(earlier.astype(jnp.int32), axis=1)
    return flat_ids * capacity + slot


def shards(
    tokens,
    attn_gain,
    query_weight,
    keyval_weight,
    sink_logits,
    out_weight,
    mlp_gain,
    routes,
    gate_fixed,
    gate_weight,
    up_weight,
    down_weight,
):
    ctx_size = lax.axis_size("ctx")
    fsdp_size = lax.axis_size("fsdp")
    ctx_index = lax.axis_index("ctx")
    fsdp_index = lax.axis_index("fsdp")
    local_rows = tokens.shape[0]
    width = tokens.shape[1]
    shard_len = local_rows * fsdp_size
    heads_here = query_weight.shape[1] // HEAD_DIM
    kv_blocks = keyval_weight.shape[0] // HEAD_DIM
    block_ids = fsdp_index * kv_blocks + jnp.arange(kv_blocks, dtype=jnp.int32)
    rope_flag = jnp.concatenate(
        [jnp.ones((heads_here,), jnp.float32), (block_ids < KV_HEADS).astype(jnp.float32)]
    )
    piece = lax.all_gather(tokens, "fsdp", axis=0, tiled=True)
    count = piece.shape[0]
    normed = rms_scale(piece.astype(jnp.float32), attn_gain).astype(jnp.bfloat16)
    query_val = jnp.dot(normed, query_weight, preferred_element_type=jnp.float32)
    kv_val = lax.dot_general(
        normed, keyval_weight, (((1,), (1,)), ((), ())), preferred_element_type=jnp.float32
    )
    mixed = jnp.concatenate([query_val, kv_val], axis=1).reshape(
        count, heads_here + kv_blocks, HEAD_DIM
    )
    positions = (ctx_index * shard_len + jnp.arange(count, dtype=jnp.int32)).astype(jnp.float32)
    turned = rotate(mixed, positions)
    chosen = jnp.where(rope_flag[None, :, None] > 0.5, turned, mixed)
    projected = chosen.astype(jnp.bfloat16).reshape(count, (heads_here + kv_blocks) * HEAD_DIM)
    query_part = projected[:, : heads_here * HEAD_DIM].reshape(shard_len, heads_here, HEAD_DIM)
    kv_mine = projected[:, heads_here * HEAD_DIM :]
    own_head = fsdp_index * heads_here // (HEADS // KV_HEADS)
    kv_all = lax.all_gather(kv_mine, "fsdp", axis=1, tiled=True)
    key_cols = lax.dynamic_slice_in_dim(kv_all, own_head * HEAD_DIM, HEAD_DIM, 1)
    value_cols = lax.dynamic_slice_in_dim(
        kv_all, KV_HEADS * HEAD_DIM + own_head * HEAD_DIM, HEAD_DIM, 1
    )
    own_rows = jnp.concatenate([key_cols, value_cols], axis=1)
    rim_rows = from_behind(own_rows[shard_len - WINDOW :], "ctx", 1)
    extended = jnp.concatenate([rim_rows, own_rows], axis=0)
    key_ext = extended[:, :HEAD_DIM]
    value_ext = extended[:, HEAD_DIM:]
    scores = jnp.einsum(
        "rhd,kd->hrk", query_part, key_ext, preferred_element_type=jnp.float32
    ) * HEAD_DIM ** (-0.5)
    query_pos = ctx_index * shard_len + jnp.arange(shard_len, dtype=jnp.int32)
    key_pos = ctx_index * shard_len - WINDOW + jnp.arange(shard_len + WINDOW, dtype=jnp.int32)
    allowed = (
        (key_pos[None, :] <= query_pos[:, None])
        & (key_pos[None, :] > query_pos[:, None] - WINDOW)
        & (key_pos[None, :] >= 0)
    )
    masked = jnp.where(allowed[None], scores, -1e30)
    top_score = jnp.maximum(jnp.max(masked, axis=-1), sink_logits[:, None])
    expd = jnp.exp(masked - top_score[..., None])
    total = jnp.exp(sink_logits[:, None] - top_score) + jnp.sum(expd, axis=-1)
    probs = (expd / total[..., None]).astype(jnp.bfloat16)
    attended = jnp.einsum("hrk,kd->rhd", probs, value_ext, preferred_element_type=jnp.float32)
    attended = attended.astype(jnp.bfloat16).reshape(shard_len, heads_here * HEAD_DIM)
    attn_delta = lax.psum_scatter(
        jnp.dot(attended, out_weight, preferred_element_type=jnp.float32).astype(jnp.bfloat16),
        "fsdp",
        scatter_dimension=0,
        tiled=True,
    ).astype(jnp.float32)
    resid = tokens.astype(jnp.float32) + attn_delta
    ffn_in = rms_scale(resid, mlp_gain).astype(jnp.bfloat16)
    experts_here = gate_weight.shape[0]
    num_experts = experts_here * fsdp_size
    capacity = max(2, 3 * local_rows * TOP // (2 * num_experts))
    slot_pos = expert_slots(routes, num_experts, capacity)
    table = jnp.any(
        slot_pos.reshape(local_rows, TOP)[None, :, :]
        == jnp.arange(num_experts * capacity, dtype=jnp.int32)[:, None, None],
        axis=-1,
    )
    send_rows = jnp.dot(
        table.astype(jnp.bfloat16), ffn_in, preferred_element_type=jnp.float32
    ).astype(jnp.bfloat16)
    send_rows = send_rows.reshape(fsdp_size, experts_here * capacity, width)
    fanned = jnp.broadcast_to(send_rows[None], (ctx_size,) + send_rows.shape)
    fanned = fanned.reshape(ctx_size * fsdp_size, experts_here * capacity, width)
    arrived = lax.all_to_all(fanned, ("ctx", "fsdp"), split_axis=0, concat_axis=0, tiled=True)
    count = arrived.shape[0]
    grouped = arrived.reshape(count, experts_here, capacity, width)
    gate_val = jnp.einsum(
        "aemd,ehd->aemh", grouped, gate_weight, preferred_element_type=jnp.float32
    )
    up_val = jnp.einsum("aemd,ehd->aemh", grouped, up_weight, preferred_element_type=jnp.float32)
    hidden = (gate_val * jax.nn.sigmoid(glu_alpha * gate_val) * (up_val + 1.0)).astype(jnp.bfloat16)
    partial_value = jnp.einsum(
        "aemh,ehd->aemd", hidden, down_weight, preferred_element_type=jnp.float32
    )
    partial_value = partial_value.reshape(count, experts_here * capacity, width).astype(
        jnp.bfloat16
    )
    returned = lax.all_to_all(
        partial_value, ("ctx", "fsdp"), split_axis=0, concat_axis=0, tiled=True
    )
    returned = returned.reshape(ctx_size, fsdp_size * experts_here * capacity, width).astype(
        jnp.float32
    )
    expert_out = jnp.sum(returned, axis=0).astype(jnp.bfloat16)
    picked = (
        jnp.take(expert_out, slot_pos, axis=0).reshape(local_rows, TOP, width).astype(jnp.float32)
    )
    route_weights = gate_fixed.astype(jnp.float32) / fixed_scale
    moe_sum = jnp.sum(picked * route_weights[..., None], axis=1)
    return (resid + moe_sum).astype(jnp.bfloat16)


def solution(mesh):
    in_specs = (
        P(("ctx", "fsdp"), None),
        P(),
        P(None, "fsdp"),
        P("fsdp", None),
        P("fsdp"),
        P("fsdp", None),
        P(),
        P(("ctx", "fsdp"), None),
        P(("ctx", "fsdp"), None),
        P("fsdp", "ctx", None),
        P("fsdp", "ctx", None),
        P("fsdp", "ctx", None),
    )
    out_specs = P(("ctx", "fsdp"), None)
    return jax.shard_map(shards, mesh=mesh, in_specs=in_specs, out_specs=out_specs, check_vma=False)
```

```python
import functools
import jax
import jax.numpy as jnp
from jax import lax
from jax.experimental import pallas as pl
from jax.experimental.pallas import tpu as pltpu
from jax.sharding import PartitionSpec as P

PARTS = ((0, 1024, 1024), (1024, 1024, 1024), (2048, 832, 896))
ORDERS = ((0, 1, 2), (1, 2, 0), (2, 0, 1))
HALF = 512
GROUPS = 8
GLU = 1.702


def moe_kernel(
    xin, resid, gate_hbm, up_hbm, down_hbm, out,
    x0, x1, x2, d0, d1, d2, s0, s1, s2,
    gate_w, up_w, down_w, table, lower,
    ra0, ra1, ra2, rb0, rb1, rb2, rc0, rc1, rc2,
    wsem, ag_send, ag_recv, sib_send, sib_recv,
    rs_send, rs_recv, sx_send, sx_recv,
):
    xs, ds, ss = (x0, x1, x2), (d0, d1, d2), (s0, s1, s2)
    rbufs = ((ra0, ra1, ra2), (rb0, rb1, rb2), (rc0, rc1, rc2))
    ctx = lax.axis_index("ctx")
    fsdp = lax.axis_index("fsdp")
    core = fsdp % 2
    me = (ctx // 2, (fsdp // 8) * 2 + ctx % 2, (fsdp // 2) % 4)

    def device(z, y, x, c):
        return (z * 2 + y % 2, ((y // 2) * 4 + x) * 2 + c)

    def neighbour(axis, by):
        at = list(me)
        at[axis] = (at[axis] + by + 4) % 4
        return device(*at, core)

    sibling = device(*me, 1 - core)

    def copy(src, dst, ss_, rs_, to):
        return pltpu.make_async_remote_copy(
            src_ref=src, dst_ref=dst, send_sem=ss_, recv_sem=rs_,
            device_id=to, device_id_type=pl.DeviceIdType.MESH,
        )

    weights = [
        pltpu.make_async_copy(h, v, wsem.at[i])
        for i, (h, v) in enumerate(((gate_hbm, gate_w), (up_hbm, up_w), (down_hbm, down_w)))
    ]
    for w in weights:
        w.start()

    barrier = pltpu.get_barrier_semaphore()
    partners = [neighbour(a, b) for a in range(3) for b in (1, -1)] + [sibling]
    for p in partners:
        pl.semaphore_signal(barrier, inc=1, device_id=p, device_id_type=pl.DeviceIdType.MESH)

    for p, (lo, n, held) in enumerate(PARTS):
        xs[p][me[0], me[1], me[2], core] = xin[:, lo : lo + held]

    r = lax.broadcasted_iota(jnp.int32, (256, 256), 0)
    c = lax.broadcasted_iota(jnp.int32, (256, 256), 1)
    lower[...] = jnp.where((r // 16 == c // 16) & (c < r), 1.0, 0.0).astype(jnp.bfloat16)
    pl.semaphore_wait(barrier, len(partners))

    def view(ref, p, stage, by, cols, which=None):
        axis = ORDERS[p][stage]
        free = ORDERS[p][:stage]
        idx = []
        for a in range(3):
            if a in free:
                idx.append(slice(None))
            elif a == axis:
                idx.append((me[a] + by + 4) % 4)
            else:
                idx.append(me[a])
        if which is not None:
            idx.append(which)
        return ref.at[tuple(idx) + (slice(None), cols)]

    def halves(p):
        return pl.ds(0, HALF), pl.ds(HALF, PARTS[p][2] - HALF)

    def whole(p):
        return pl.ds(0, PARTS[p][2])

    pending = []
    for p in range(3):
        v = view(xs[p], p, 0, 0, whole(p), core)
        cp = copy(v, v, sib_send.at[p, 0, 3], sib_recv.at[p, 0, 3], sibling)
        cp.start()
        pending.append(cp)

    def ag(p, st, by, half, k, to):
        v = view(xs[p], p, st, by, halves(p)[half], core)
        cp = copy(v, v, ag_send.at[p, st, k], ag_recv.at[p, st, k], to)
        cp.start()
        pending.append(cp)

    def ag_wait(p, st, by, half, k):
        v = view(xs[p], p, st, by, halves(p)[half], core)
        copy(v, v, ag_send.at[p, st, k], ag_recv.at[p, st, k], sibling).wait_recv()

    def forward(p, st, by, k):
        v = view(xs[p], p, st, by, whole(p), core)
        cp = copy(v, v, sib_send.at[p, st, k], sib_recv.at[p, st, k], sibling)
        cp.start()
        pending.append(cp)

    for st in range(3):
        for p in range(3):
            a = ORDERS[p][st]
            up, dn = neighbour(a, 1), neighbour(a, -1)
            ag(p, st, 0, 0, 0, up)
            ag(p, st, 0, 1, 1, dn)
            ag(p, st, 0, 1, 2, up)
            ag(p, st, 0, 0, 3, dn)
        for p in range(3):
            a = ORDERS[p][st]
            up, dn = neighbour(a, 1), neighbour(a, -1)
            ag_wait(p, st, -1, 0, 0)
            ag(p, st, -1, 0, 4, up)
            ag_wait(p, st, 1, 1, 1)
            ag(p, st, 1, 1, 5, dn)
        for p in range(3):
            ag_wait(p, st, -1, 1, 2)
            forward(p, st, -1, 0)
            ag_wait(p, st, 1, 0, 3)
            forward(p, st, 1, 1)
        for p in range(3):
            ag_wait(p, st, 2, 0, 4)
            ag_wait(p, st, 2, 1, 5)
            forward(p, st, 2, 2)
    for p in range(3):
        v = view(xs[p], p, 0, 0, whole(p), 1 - core)
        copy(v, v, sib_send.at[p, 0, 3], sib_recv.at[p, 0, 3], sibling).wait_recv()
        for st in range(3):
            for k, by in enumerate((-1, 1, 2)):
                v = view(xs[p], p, st, by, whole(p), 1 - core)
                copy(v, v, sib_send.at[p, st, k], sib_recv.at[p, st, k], sibling).wait_recv()
    for cp in pending:
        cp.wait_send()

    first_expert = fsdp * 4
    lane = lax.broadcasted_iota(jnp.int32, (256, 128), 1)
    row = lax.broadcasted_iota(jnp.int32, (256, 128), 0)
    lane_expert = (first_expert + lane // 32).astype(jnp.float32)
    lane_slot = ((lane % 32) // 16).astype(jnp.float32)
    same_source = row // 16 == lane % 16

    def dispatch(g, _):
        z, yh = g // 2, g % 2

        def rows(p):
            return xs[p][z, pl.ds(yh * 2, 2)].reshape(256, PARTS[p][2])

        last = rows(2)
        ids = last[:, 768:896].astype(jnp.float32)
        hit = jnp.zeros((256, 128), jnp.float32)
        for k in range(4):
            hit = hit + jnp.where(ids[:, 64 + k : 65 + k] == lane_expert, 1.0, 0.0)
        rank = jnp.dot(lower[...], hit.astype(jnp.bfloat16), preferred_element_type=jnp.float32)
        t = jnp.where((rank == lane_slot) & same_source, hit, 0.0)
        table[g] = t.astype(jnp.bfloat16)
        pick = t.T.astype(jnp.bfloat16)
        for p in range(3):
            src = last if p == 2 else rows(p)
            got = jnp.dot(pick, src, preferred_element_type=jnp.float32).astype(jnp.bfloat16)
            for e in range(4):
                ds[p][e, pl.ds(g * 32, 32), :] = got[e * 32 : (e + 1) * 32]
        return 0

    lax.fori_loop(0, GROUPS, dispatch, 0)

    for w in weights:
        w.wait()

    def expert(e, _):
        gate = jnp.zeros((256, 180), jnp.float32)
        upv = jnp.zeros((256, 180), jnp.float32)
        for p, (lo, n, held) in enumerate(PARTS):
            y = ds[p][e, :, 0:n]
            nt = (((1,), (1,)), ((), ()))
            gate = gate + lax.dot_general(y, gate_w[e, :, lo : lo + n], nt, preferred_element_type=jnp.float32)
            upv = upv + lax.dot_general(y, up_w[e, :, lo : lo + n], nt, preferred_element_type=jnp.float32)
        meta = ds[2][e, :, 768:896].astype(jnp.float32)
        weight = jnp.zeros((256, 1), jnp.float32)
        number = (first_expert + e).astype(jnp.float32)
        for k in range(4):
            value = meta[:, 68 + k : 69 + k] * 256.0 + meta[:, 72 + k : 73 + k]
            weight = weight + jnp.where(meta[:, 64 + k : 65 + k] == number, value, 0.0)
        hidden = gate * jax.nn.sigmoid(GLU * gate) * (upv + 1.0)
        hidden = (hidden * (weight * (1.0 / 65536.0))).astype(jnp.bfloat16)
        for p, (lo, n, held) in enumerate(PARTS):
            ds[p][e, :, 0:n] = jnp.dot(
                hidden, down_w[e, :, lo : lo + n], preferred_element_type=jnp.float32
            ).astype(jnp.bfloat16)
        return 0

    lax.fori_loop(0, 4, expert, 0)

    pending = []
    for p in range(3):
        n = PARTS[p][1]

        def combine(g, _, p=p, n=n):
            z, yh = g // 2, g % 2
            y = jnp.concatenate([ds[p][e, pl.ds(g * 32, 32), :] for e in range(4)], axis=0)
            got = jnp.dot(table[g], y, preferred_element_type=jnp.float32).astype(jnp.bfloat16)
            xs[p][z, pl.ds(yh * 2, 2)] = got.reshape(2, 4, 2, 16, PARTS[p][2])
            return 0

        lax.fori_loop(0, GROUPS, combine, 0)
        for k, by in enumerate((2, 1, -1, 0)):
            cp = copy(
                view(xs[p], p, 2, by, whole(p), 1 - core), view(ss[p], p, 2, by, whole(p)),
                sx_send.at[p, k], sx_recv.at[p, k], sibling,
            )
            cp.start()
            pending.append(cp)

    def add(dst, *others):
        lead = dst.shape[:-2]
        count = 1
        for s in lead:
            count *= s

        def one(i, _):
            idx = () if not lead else ((i,) if len(lead) == 1 else (i // 4, i % 4))
            total = dst[idx].astype(jnp.float32)
            for o in others:
                total = total + o[idx].astype(jnp.float32)
            dst[idx] = total.astype(jnp.bfloat16)
            return 0

        if lead:
            lax.fori_loop(0, count, one, 0)
        else:
            one(0, 0)

    def rs(p, st, k, src, dst, to):
        cp = copy(src, dst, rs_send.at[p, st, k], rs_recv.at[p, st, k], to)
        cp.start()
        pending.append(cp)

    def rs_wait(p, st, k, dst):
        copy(dst, dst, rs_send.at[p, st, k], rs_recv.at[p, st, k], sibling).wait_recv()

    def sib_wait(p, k, by):
        v = view(ss[p], p, 2, by, whole(p))
        copy(v, v, sx_send.at[p, k], sx_recv.at[p, k], sibling).wait_recv()

    for st in (2, 1, 0):
        for p in range(3):
            a = ORDERS[p][st]
            up, dn = neighbour(a, 1), neighbour(a, -1)
            ha, hb = halves(p)
            r = rbufs[p][st]
            if st == 2:
                sib_wait(p, 0, 2)
                add(view(xs[p], p, st, 2, whole(p), core), view(ss[p], p, st, 2, whole(p)))
            rs(p, st, 0, view(xs[p], p, st, 2, ha, core), r.at[2, ..., ha], up)
            rs(p, st, 1, view(xs[p], p, st, 2, hb, core), r.at[2, ..., hb], dn)
        for p in range(3):
            a = ORDERS[p][st]
            up, dn = neighbour(a, 1), neighbour(a, -1)
            ha, hb = halves(p)
            r = rbufs[p][st]
            if st == 2:
                sib_wait(p, 1, 1)
                add(view(xs[p], p, st, 1, whole(p), core), view(ss[p], p, st, 1, whole(p)))
            rs(p, st, 2, view(xs[p], p, st, 1, hb, core), r.at[0, ..., hb], up)
            if st == 2:
                sib_wait(p, 2, -1)
                add(view(xs[p], p, st, -1, whole(p), core), view(ss[p], p, st, -1, whole(p)))
            rs(p, st, 3, view(xs[p], p, st, -1, ha, core), r.at[1, ..., ha], dn)
        for p in range(3):
            a = ORDERS[p][st]
            up, dn = neighbour(a, 1), neighbour(a, -1)
            ha, hb = halves(p)
            r = rbufs[p][st]
            rs_wait(p, st, 0, r.at[2, ..., ha])
            add(view(xs[p], p, st, 1, ha, core), r.at[2, ..., ha])
            rs(p, st, 4, view(xs[p], p, st, 1, ha, core), r.at[0, ..., ha], up)
            rs_wait(p, st, 1, r.at[2, ..., hb])
            add(view(xs[p], p, st, -1, hb, core), r.at[2, ..., hb])
            rs(p, st, 5, view(xs[p], p, st, -1, hb, core), r.at[1, ..., hb], dn)
        for p in range(3):
            ha, hb = halves(p)
            r = rbufs[p][st]
            own = view(xs[p], p, st, 0, whole(p), core)
            others = [r.at[0], r.at[1]]
            if st == 2:
                sib_wait(p, 3, 0)
                others.append(view(ss[p], p, st, 0, whole(p)))
            rs_wait(p, st, 2, r.at[0, ..., hb])
            rs_wait(p, st, 3, r.at[1, ..., ha])
            rs_wait(p, st, 4, r.at[0, ..., ha])
            rs_wait(p, st, 5, r.at[1, ..., hb])
            if st:
                add(own, *others)
            else:
                lo, n, held = PARTS[p]
                total = own[...].astype(jnp.float32) + r[0].astype(jnp.float32) + r[1].astype(jnp.float32)
                out[:, lo : lo + n] = (resid[:, lo : lo + n] + total[:, :n]).astype(jnp.bfloat16)
    for cp in pending:
        cp.wait_send()


def moe(xin, resid, gate_weight, up_weight, down_weight):
    bf = jnp.bfloat16
    held = [p[2] for p in PARTS]
    scratch = (
        [pltpu.VMEM((4, 4, 4, 2, 16, h), bf) for h in held]
        + [pltpu.VMEM((4, 256, h), bf) for h in held]
        + [pltpu.VMEM((4, 4, 4, 16, h), bf) for h in held]
        + [pltpu.VMEM(w.shape, bf) for w in (gate_weight, up_weight, down_weight)]
        + [pltpu.VMEM((GROUPS, 256, 128), bf), pltpu.VMEM((256, 256), bf)]
        + [pltpu.VMEM((3,) + (4,) * s + (16, h), bf) for h in held for s in range(3)]
        + [
            pltpu.SemaphoreType.DMA((3,)),
            pltpu.SemaphoreType.DMA((3, 3, 6)),
            pltpu.SemaphoreType.DMA((3, 3, 6)),
            pltpu.SemaphoreType.DMA((3, 3, 4)),
            pltpu.SemaphoreType.DMA((3, 3, 4)),
            pltpu.SemaphoreType.DMA((3, 3, 6)),
            pltpu.SemaphoreType.DMA((3, 3, 6)),
            pltpu.SemaphoreType.DMA((3, 4)),
            pltpu.SemaphoreType.DMA((3, 4)),
        ]
    )
    vm = pl.BlockSpec(memory_space=pltpu.VMEM)
    anym = pl.BlockSpec(memory_space=pl.ANY)
    return pl.pallas_call(
        moe_kernel,
        out_shape=jax.ShapeDtypeStruct(resid.shape, bf),
        in_specs=[vm, vm, anym, anym, anym],
        out_specs=vm,
        scratch_shapes=scratch,
        compiler_params=pltpu.CompilerParams(
            collective_id=1, has_side_effects=True, vmem_limit_bytes=60 * 1024 * 1024
        ),
        name="moe",
    )(xin, resid, gate_weight, up_weight, down_weight)


HEADS = 64
KV_HEADS = 8
HEAD_DIM = 64
WINDOW = 128
TOP = 4


rope_theta = 150000.0
norm_eps = 1e-05
glu_alpha = 1.702
fixed_scale = 65536.0


def from_behind(x, axis, by):
    count = lax.axis_size(axis)
    pairs = [(i, i + by) for i in range(count) if 0 <= i + by < count]
    return lax.ppermute(x, axis, pairs)


def rms_scale(values, gain):
    mean_sq = jnp.mean(values * values, axis=-1, keepdims=True)
    return values * lax.rsqrt(mean_sq + norm_eps) * gain


def rotate(tensor, positions):
    half_dim = tensor.shape[-1] // 2
    freqs = rope_theta ** (-(jnp.arange(half_dim, dtype=jnp.float32) * 2.0 / tensor.shape[-1]))
    angles = positions[:, None] * freqs[None, :]
    cosine = jnp.cos(angles)[:, None, :]
    sine = jnp.sin(angles)[:, None, :]
    first = tensor[..., :half_dim]
    second = tensor[..., half_dim:]
    return jnp.concatenate(
        [first * cosine - second * sine, second * cosine + first * sine], axis=-1
    )


def shards(
    tokens,
    attn_gain,
    query_weight,
    keyval_weight,
    sink_logits,
    out_weight,
    mlp_gain,
    routes,
    gate_fixed,
    gate_weight,
    up_weight,
    down_weight,
):
    ctx_size = lax.axis_size("ctx")
    fsdp_size = lax.axis_size("fsdp")
    ctx_index = lax.axis_index("ctx")
    fsdp_index = lax.axis_index("fsdp")
    local_rows = tokens.shape[0]
    width = tokens.shape[1]
    shard_len = local_rows * fsdp_size
    heads_here = query_weight.shape[1] // HEAD_DIM
    kv_blocks = keyval_weight.shape[0] // HEAD_DIM
    block_ids = fsdp_index * kv_blocks + jnp.arange(kv_blocks, dtype=jnp.int32)
    rope_flag = jnp.concatenate(
        [jnp.ones((heads_here,), jnp.float32), (block_ids < KV_HEADS).astype(jnp.float32)]
    )
    piece = lax.all_gather(tokens, "fsdp", axis=0, tiled=True)
    count = piece.shape[0]
    normed = rms_scale(piece.astype(jnp.float32), attn_gain).astype(jnp.bfloat16)
    query_val = jnp.dot(normed, query_weight, preferred_element_type=jnp.float32)
    kv_val = lax.dot_general(
        normed, keyval_weight, (((1,), (1,)), ((), ())), preferred_element_type=jnp.float32
    )
    mixed = jnp.concatenate([query_val, kv_val], axis=1).reshape(
        count, heads_here + kv_blocks, HEAD_DIM
    )
    positions = (ctx_index * shard_len + jnp.arange(count, dtype=jnp.int32)).astype(jnp.float32)
    turned = rotate(mixed, positions)
    chosen = jnp.where(rope_flag[None, :, None] > 0.5, turned, mixed)
    projected = chosen.astype(jnp.bfloat16).reshape(count, (heads_here + kv_blocks) * HEAD_DIM)
    query_part = projected[:, : heads_here * HEAD_DIM].reshape(shard_len, heads_here, HEAD_DIM)
    kv_mine = projected[:, heads_here * HEAD_DIM :]
    own_head = fsdp_index * heads_here // (HEADS // KV_HEADS)
    kv_all = lax.all_gather(kv_mine, "fsdp", axis=1, tiled=True)
    key_cols = lax.dynamic_slice_in_dim(kv_all, own_head * HEAD_DIM, HEAD_DIM, 1)
    value_cols = lax.dynamic_slice_in_dim(
        kv_all, KV_HEADS * HEAD_DIM + own_head * HEAD_DIM, HEAD_DIM, 1
    )
    own_rows = jnp.concatenate([key_cols, value_cols], axis=1)
    rim_rows = from_behind(own_rows[shard_len - WINDOW :], "ctx", 1)
    extended = jnp.concatenate([rim_rows, own_rows], axis=0)
    key_ext = extended[:, :HEAD_DIM]
    value_ext = extended[:, HEAD_DIM:]
    scores = jnp.einsum(
        "rhd,kd->hrk", query_part, key_ext, preferred_element_type=jnp.float32
    ) * HEAD_DIM ** (-0.5)
    query_pos = ctx_index * shard_len + jnp.arange(shard_len, dtype=jnp.int32)
    key_pos = ctx_index * shard_len - WINDOW + jnp.arange(shard_len + WINDOW, dtype=jnp.int32)
    allowed = (
        (key_pos[None, :] <= query_pos[:, None])
        & (key_pos[None, :] > query_pos[:, None] - WINDOW)
        & (key_pos[None, :] >= 0)
    )
    masked = jnp.where(allowed[None], scores, -1e30)
    top_score = jnp.maximum(jnp.max(masked, axis=-1), sink_logits[:, None])
    expd = jnp.exp(masked - top_score[..., None])
    total = jnp.exp(sink_logits[:, None] - top_score) + jnp.sum(expd, axis=-1)
    probs = (expd / total[..., None]).astype(jnp.bfloat16)
    attended = jnp.einsum("hrk,kd->rhd", probs, value_ext, preferred_element_type=jnp.float32)
    attended = attended.astype(jnp.bfloat16).reshape(shard_len, heads_here * HEAD_DIM)
    attn_delta = lax.psum_scatter(
        jnp.dot(attended, out_weight, preferred_element_type=jnp.float32).astype(jnp.bfloat16),
        "fsdp",
        scatter_dimension=0,
        tiled=True,
    ).astype(jnp.float32)
    resid = tokens.astype(jnp.float32) + attn_delta
    ffn_in = rms_scale(resid, mlp_gain).astype(jnp.bfloat16)
    high = gate_fixed // 256
    meta = jnp.concatenate([routes, high, gate_fixed - high * 256], axis=1).astype(jnp.bfloat16)
    xin = jnp.concatenate(
        [ffn_in, meta, jnp.zeros((local_rows, 2944 - width - meta.shape[1]), jnp.bfloat16)], axis=1
    )
    return moe(xin, resid, gate_weight, up_weight, down_weight)


def solution(mesh):
    in_specs = (
        P(("ctx", "fsdp"), None),
        P(),
        P(None, "fsdp"),
        P("fsdp", None),
        P("fsdp"),
        P("fsdp", None),
        P(),
        P(("ctx", "fsdp"), None),
        P(("ctx", "fsdp"), None),
        P("fsdp", "ctx", None),
        P("fsdp", "ctx", None),
        P("fsdp", "ctx", None),
    )
    out_specs = P(("ctx", "fsdp"), None)
    return jax.shard_map(shards, mesh=mesh, in_specs=in_specs, out_specs=out_specs, check_vma=False)
```

```python
import functools
import jax
import jax.numpy as jnp
from jax import lax
from jax.experimental import pallas as pl
from jax.experimental.pallas import tpu as pltpu
from jax.sharding import PartitionSpec as P

PARTS = ((0, 1024, 1024), (1024, 1024, 1024), (2048, 832, 896))
ORDERS = ((0, 1, 2), (1, 2, 0), (2, 0, 1))
HALF = 512
GROUPS = 8
GLU = 1.702


def layer_kernel(
    tokens, attn_gain, mlp_gain, cos_ref, sin_ref, sinks, meta,
    query_hbm, keyval_hbm, outw_hbm, gate_hbm, up_hbm, down_hbm, out,
    x0, x1, x2, d0, d1, d2, s0, s1, s2,
    gate_w, up_w, down_w, table, lower,
    ra0, ra1, ra2, rb0, rb1, rb2, rc0, rc1, rc2,
    query_w, keyval_w, outw_w, gathered, normed, kv_mine, kv_all, queries, attended,
    part, part_sib, part_in, part_last, resid,
    wsem, ag_send, ag_recv, sib_send, sib_recv,
    rs_send, rs_recv, sx_send, sx_recv,
    ta_send, ta_recv, kv_send, kv_recv, tr_send, tr_recv,
):
    xs, ds, ss = (x0, x1, x2), (d0, d1, d2), (s0, s1, s2)
    rbufs = ((ra0, ra1, ra2), (rb0, rb1, rb2), (rc0, rc1, rc2))
    ctx = lax.axis_index("ctx")
    fsdp = lax.axis_index("fsdp")
    core = fsdp % 2
    me = (ctx // 2, (fsdp // 8) * 2 + ctx % 2, (fsdp // 2) % 4)

    def device(z, y, x, c):
        return (z * 2 + y % 2, ((y // 2) * 4 + x) * 2 + c)

    def neighbour(axis, by):
        at = list(me)
        at[axis] = (at[axis] + by + 4) % 4
        return device(*at, core)

    sibling = device(*me, 1 - core)

    def copy(src, dst, ss_, rs_, to):
        return pltpu.make_async_remote_copy(
            src_ref=src, dst_ref=dst, send_sem=ss_, recv_sem=rs_,
            device_id=to, device_id_type=pl.DeviceIdType.MESH,
        )

    loads = [
        pltpu.make_async_copy(h, v, wsem.at[i])
        for i, (h, v) in enumerate(
            (
                (keyval_hbm, keyval_w), (query_hbm, query_w), (outw_hbm, outw_w),
                (gate_hbm, gate_w), (up_hbm, up_w), (down_hbm, down_w),
            )
        )
    ]
    for w in loads:
        w.start()
    weights = loads[3:]

    def signal(to):
        pl.semaphore_signal(barrier, inc=1, device_id=to, device_id_type=pl.DeviceIdType.MESH)

    barrier = pltpu.get_barrier_semaphore()
    across = device(me[0], (me[1] + 2) % 4, me[2], core)
    partners = [neighbour(a, b) for a in range(3) for b in (1, -1)] + [sibling, across]
    for to in partners:
        signal(to)
    behind = (ctx + 7) % 8
    ahead = (ctx + 1) % 8
    key_from, value_from = fsdp // 2, 8 + fsdp // 2
    signal((behind, key_from))
    signal((behind, value_from))

    @pl.when(fsdp != 0)
    def _():
        signal((ctx, key_from))

    @pl.when(fsdp != 15)
    def _():
        signal((ctx, value_from))

    yh = me[1] // 2
    gathered[yh, me[2], core] = tokens[...]
    r = lax.broadcasted_iota(jnp.int32, (256, 256), 0)
    c = lax.broadcasted_iota(jnp.int32, (256, 256), 1)
    lower[...] = jnp.where((r // 16 == c // 16) & (c < r), 1.0, 0.0).astype(jnp.bfloat16)
    alone = jnp.where((fsdp == 0) | (fsdp == 15), 1, 0)
    pl.semaphore_wait(barrier, len(partners) + 4 - alone)

    started = []

    def send(src, dst, send_sem, recv_sem, to):
        cp = copy(src, dst, send_sem, recv_sem, to)
        cp.start()
        started.append(cp)

    left, right = neighbour(2, -1), neighbour(2, 1)
    halves_of = (pl.ds(0, 1408), pl.ds(1408, 1472))

    def held(b, by, which, half=None):
        at = gathered.at[(yh + b) % 2, (me[2] + by + 4) % 4, which]
        return at if half is None else at.at[:, halves_of[half]]

    def pass_on(b, by, half, k, to):
        v = held(b, by, core, half)
        send(v, v, ta_send.at[b, k], ta_recv.at[b, k], to)

    def arrived(b, by, half, k):
        v = held(b, by, core, half)
        copy(v, v, ta_send.at[b, k], ta_recv.at[b, k], sibling).wait_recv()

    def to_sibling(b, by, k):
        v = held(b, by, core)
        send(v, v, ta_send.at[b, k], ta_recv.at[b, k], sibling)

    def norm_block(b, by, which):
        y_, x_ = (yh + b) % 2, (me[2] + by + 4) % 4
        v = gathered[y_, x_, which].astype(jnp.float32)
        scale = lax.rsqrt(jnp.sum(v * v, axis=-1, keepdims=True) * (1.0 / 2880.0) + 1e-05)
        row = ((y_ * 4 + x_) * 2 + which) * 16
        normed[pl.ds(pl.multiple_of(row, 16), 16), :] = (v * scale * attn_gain[...]).astype(jnp.bfloat16)

    send(held(0, 0, core), held(0, 0, core), ta_send.at[0, 10], ta_recv.at[0, 10], across)
    for b in range(2):
        if b == 1:
            v = held(1, 0, core)
            copy(v, v, ta_send.at[0, 10], ta_recv.at[0, 10], sibling).wait_recv()
        pass_on(b, 0, 0, 0, right)
        pass_on(b, 0, 1, 1, left)
        pass_on(b, 0, 1, 2, right)
        pass_on(b, 0, 0, 3, left)
        to_sibling(b, 0, 6)
        norm_block(b, 0, core)
    for b in range(2):
        arrived(b, -1, 0, 0)
        pass_on(b, -1, 0, 4, right)
        arrived(b, 1, 1, 1)
        pass_on(b, 1, 1, 5, left)
    for b in range(2):
        arrived(b, -1, 1, 2)
        to_sibling(b, -1, 7)
        arrived(b, 1, 0, 3)
        to_sibling(b, 1, 8)
        norm_block(b, -1, core)
        norm_block(b, 1, core)
    for b in range(2):
        arrived(b, 2, 0, 4)
        arrived(b, 2, 1, 5)
        to_sibling(b, 2, 9)
        norm_block(b, 2, core)
    for k, by in ((6, 0), (7, -1), (8, 1), (9, 2)):
        for b in range(2):
            v = held(b, by, 1 - core)
            copy(v, v, ta_send.at[b, k], ta_recv.at[b, k], sibling).wait_recv()
            norm_block(b, by, 1 - core)

    nt = (((1,), (1,)), ((), ()))
    cosine, sine = cos_ref[...], sin_ref[...]
    early = lax.broadcasted_iota(jnp.int32, (256, 128), 1) % 64 < 32

    def turn(v, c_, s_):
        return v * c_ + jnp.where(early, pltpu.roll(v, 96, 1), pltpu.roll(v, 32, 1)) * s_

    loads[0].wait()
    kv = lax.dot_general(normed[...], keyval_w[...], nt, preferred_element_type=jnp.float32)
    kv = jnp.concatenate([kv, kv], axis=1)
    kv = jnp.where(fsdp < 8, turn(kv, cosine, sine), kv)
    kv_mine[...] = kv[:, :64].astype(jnp.bfloat16)
    which = fsdp // 8
    main, rim = pl.ds(128, 256), pl.ds(0, 128)
    wait_main = []
    for i in range(2):
        to = 2 * (fsdp % 8) + i
        cp = copy(kv_mine, kv_all.at[which, main], kv_send.at[i], kv_recv.at[which * 2], (ctx, to))
        own = fsdp == 15 * i

        @pl.when(jnp.logical_not(own))
        def _(cp=cp):
            cp.start()

        @pl.when(own)
        def _():
            kv_all[which, main] = kv_mine[...]

        wait_main.append((own, cp))
        send(
            kv_mine.at[pl.ds(128, 128)], kv_all.at[which, rim],
            kv_send.at[2 + i], kv_recv.at[which * 2 + 1], (ahead, to),
        )
    loads[1].wait()
    query = jnp.dot(normed[...], query_w[...], preferred_element_type=jnp.float32)
    for i in range(2):
        cols = slice(i * 128, i * 128 + 128)
        queries[:, cols] = turn(query[:, cols], cosine, sine).astype(jnp.bfloat16)
    for w in range(2):
        v = kv_all.at[w, main]

        @pl.when(fsdp != 15 * w)
        def _(v=v, w=w):
            copy(v, v, kv_send.at[0], kv_recv.at[w * 2], sibling).wait_recv()

        v = kv_all.at[w, rim]
        copy(v, v, kv_send.at[0], kv_recv.at[w * 2 + 1], sibling).wait_recv()
    for own, cp in wait_main:

        @pl.when(jnp.logical_not(own))
        def _(cp=cp):
            cp.wait_send()

    row = lax.broadcasted_iota(jnp.int32, (128, 256), 0)
    col = lax.broadcasted_iota(jnp.int32, (128, 256), 1)
    for b in range(2):
        allowed = (col <= row + 128) & (col > row) & (ctx * 256 + b * 128 - 128 + col >= 0)
        keys = kv_all[0, b * 128 : b * 128 + 256]
        values = kv_all[1, b * 128 : b * 128 + 256]
        for h in range(4):
            q = queries[b * 128 : b * 128 + 128, h * 64 : h * 64 + 64]
            score = lax.dot_general(q, keys, nt, preferred_element_type=jnp.float32) * 0.125
            score = jnp.where(allowed, score, -1e30)
            sink = sinks[h]
            top = jnp.maximum(jnp.max(score, axis=-1, keepdims=True), sink)
            expd = jnp.exp(score - top)
            total = jnp.exp(sink - top) + jnp.sum(expd, axis=-1, keepdims=True)
            probs = (expd / total).astype(jnp.bfloat16)
            mixed = jnp.dot(probs, values, preferred_element_type=jnp.float32)
            attended[b * 128 : b * 128 + 128, h * 64 : h * 64 + 64] = mixed.astype(jnp.bfloat16)

    loads[2].wait()
    for lo, n in ((0, 1024), (1024, 1024), (2048, 832)):
        got = lax.dot_general(
            attended[...], outw_w[lo : lo + n, :], nt, preferred_element_type=jnp.float32
        ).astype(jnp.bfloat16)
        part[:, :, :, :, lo : lo + n] = got.reshape(2, 4, 2, 16, n)

    def piece(by, half=None):
        cols = slice(None) if half is None else halves_of[half]
        return part.at[:, (me[2] + by + 4) % 4, core, :, cols]

    def landed(slot, half):
        return part_in.at[slot, :, :, halves_of[half]]

    def from_sibling(by):
        return part_sib.at[:, (me[2] + by + 4) % 4]

    def tr_wait(k, v):
        copy(v, v, tr_send.at[k], tr_recv.at[k], sibling).wait_recv()

    def plus(dst, *others):
        for i in range(2):
            total = dst[i].astype(jnp.float32)
            for o in others:
                total = total + o[i].astype(jnp.float32)
            dst[i] = total.astype(jnp.bfloat16)

    for k, by in enumerate((2, 1, -1, 0)):
        send(
            part.at[:, (me[2] + by + 4) % 4, 1 - core], from_sibling(by),
            tr_send.at[k], tr_recv.at[k], sibling,
        )
    tr_wait(0, from_sibling(2))
    plus(piece(2), from_sibling(2))
    send(piece(2, 0), landed(2, 0), tr_send.at[4], tr_recv.at[4], right)
    send(piece(2, 1), landed(2, 1), tr_send.at[5], tr_recv.at[5], left)
    tr_wait(1, from_sibling(1))
    plus(piece(1), from_sibling(1))
    send(piece(1, 1), landed(0, 1), tr_send.at[6], tr_recv.at[6], right)
    tr_wait(2, from_sibling(-1))
    plus(piece(-1), from_sibling(-1))
    send(piece(-1, 0), landed(1, 0), tr_send.at[7], tr_recv.at[7], left)
    tr_wait(4, landed(2, 0))
    plus(piece(1, 0), landed(2, 0))
    send(piece(1, 0), landed(0, 0), tr_send.at[8], tr_recv.at[8], right)
    tr_wait(5, landed(2, 1))
    plus(piece(-1, 1), landed(2, 1))
    send(piece(-1, 1), landed(1, 1), tr_send.at[9], tr_recv.at[9], left)
    tr_wait(3, from_sibling(0))
    plus(piece(0), from_sibling(0))
    tr_wait(6, landed(0, 1))
    tr_wait(7, landed(1, 0))
    tr_wait(8, landed(0, 0))
    tr_wait(9, landed(1, 1))
    plus(piece(0), part_in.at[0], part_in.at[1])
    send(part.at[1 - yh, me[2], core], part_last, tr_send.at[10], tr_recv.at[10], across)
    tr_wait(10, part_last)
    total = part[yh, me[2], core].astype(jnp.float32) + part_last[...].astype(jnp.float32)
    resid[:, 2816:2944] = jnp.zeros((16, 128), jnp.float32)
    resid[:, 0:2880] = tokens[...].astype(jnp.float32) + total
    v = resid[...]
    scale = lax.rsqrt(jnp.sum(v * v, axis=-1, keepdims=True) * (1.0 / 2880.0) + 1e-05)
    v = v * scale * mlp_gain[...]
    for p, (lo, n, wide) in enumerate(PARTS):
        w = v[:, lo : lo + wide]
        if p == 2:
            w = jnp.concatenate([w[:, :768], w[:, 768:] + meta[...]], axis=1)
        xs[p][me[0], me[1], me[2], core] = w.astype(jnp.bfloat16)
    for cp in started:
        cp.wait_send()

    def view(ref, p, stage, by, cols, which=None):
        axis = ORDERS[p][stage]
        free = ORDERS[p][:stage]
        idx = []
        for a in range(3):
            if a in free:
                idx.append(slice(None))
            elif a == axis:
                idx.append((me[a] + by + 4) % 4)
            else:
                idx.append(me[a])
        if which is not None:
            idx.append(which)
        return ref.at[tuple(idx) + (slice(None), cols)]

    def halves(p):
        return pl.ds(0, HALF), pl.ds(HALF, PARTS[p][2] - HALF)

    def whole(p):
        return pl.ds(0, PARTS[p][2])

    pending = []
    for p in range(3):
        v = view(xs[p], p, 0, 0, whole(p), core)
        cp = copy(v, v, sib_send.at[p, 0, 3], sib_recv.at[p, 0, 3], sibling)
        cp.start()
        pending.append(cp)

    def ag(p, st, by, half, k, to):
        v = view(xs[p], p, st, by, halves(p)[half], core)
        cp = copy(v, v, ag_send.at[p, st, k], ag_recv.at[p, st, k], to)
        cp.start()
        pending.append(cp)

    def ag_wait(p, st, by, half, k):
        v = view(xs[p], p, st, by, halves(p)[half], core)
        copy(v, v, ag_send.at[p, st, k], ag_recv.at[p, st, k], sibling).wait_recv()

    def forward(p, st, by, k):
        v = view(xs[p], p, st, by, whole(p), core)
        cp = copy(v, v, sib_send.at[p, st, k], sib_recv.at[p, st, k], sibling)
        cp.start()
        pending.append(cp)

    for st in range(3):
        for p in range(3):
            a = ORDERS[p][st]
            up, dn = neighbour(a, 1), neighbour(a, -1)
            ag(p, st, 0, 0, 0, up)
            ag(p, st, 0, 1, 1, dn)
            ag(p, st, 0, 1, 2, up)
            ag(p, st, 0, 0, 3, dn)
        for p in range(3):
            a = ORDERS[p][st]
            up, dn = neighbour(a, 1), neighbour(a, -1)
            ag_wait(p, st, -1, 0, 0)
            ag(p, st, -1, 0, 4, up)
            ag_wait(p, st, 1, 1, 1)
            ag(p, st, 1, 1, 5, dn)
        for p in range(3):
            ag_wait(p, st, -1, 1, 2)
            forward(p, st, -1, 0)
            ag_wait(p, st, 1, 0, 3)
            forward(p, st, 1, 1)
        for p in range(3):
            ag_wait(p, st, 2, 0, 4)
            ag_wait(p, st, 2, 1, 5)
            forward(p, st, 2, 2)
    for p in range(3):
        v = view(xs[p], p, 0, 0, whole(p), 1 - core)
        copy(v, v, sib_send.at[p, 0, 3], sib_recv.at[p, 0, 3], sibling).wait_recv()
        for st in range(3):
            for k, by in enumerate((-1, 1, 2)):
                v = view(xs[p], p, st, by, whole(p), 1 - core)
                copy(v, v, sib_send.at[p, st, k], sib_recv.at[p, st, k], sibling).wait_recv()
    for cp in pending:
        cp.wait_send()

    first_expert = fsdp * 4
    lane = lax.broadcasted_iota(jnp.int32, (256, 128), 1)
    row = lax.broadcasted_iota(jnp.int32, (256, 128), 0)
    lane_expert = (first_expert + lane // 32).astype(jnp.float32)
    lane_slot = ((lane % 32) // 16).astype(jnp.float32)
    same_source = row // 16 == lane % 16

    def dispatch(g, _):
        z, yh = g // 2, g % 2

        def rows(p):
            return xs[p][z, pl.ds(yh * 2, 2)].reshape(256, PARTS[p][2])

        last = rows(2)
        ids = last[:, 768:896].astype(jnp.float32)
        hit = jnp.zeros((256, 128), jnp.float32)
        for k in range(4):
            hit = hit + jnp.where(ids[:, 64 + k : 65 + k] == lane_expert, 1.0, 0.0)
        rank = jnp.dot(lower[...], hit.astype(jnp.bfloat16), preferred_element_type=jnp.float32)
        t = jnp.where((rank == lane_slot) & same_source, hit, 0.0)
        table[g] = t.astype(jnp.bfloat16)
        pick = t.T.astype(jnp.bfloat16)
        for p in range(3):
            src = last if p == 2 else rows(p)
            got = jnp.dot(pick, src, preferred_element_type=jnp.float32).astype(jnp.bfloat16)
            for e in range(4):
                ds[p][e, pl.ds(g * 32, 32), :] = got[e * 32 : (e + 1) * 32]
        return 0

    lax.fori_loop(0, GROUPS, dispatch, 0)

    for w in weights:
        w.wait()

    def expert(e, _):
        gate = jnp.zeros((256, 180), jnp.float32)
        upv = jnp.zeros((256, 180), jnp.float32)
        for p, (lo, n, held) in enumerate(PARTS):
            y = ds[p][e, :, 0:n]
            nt = (((1,), (1,)), ((), ()))
            gate = gate + lax.dot_general(y, gate_w[e, :, lo : lo + n], nt, preferred_element_type=jnp.float32)
            upv = upv + lax.dot_general(y, up_w[e, :, lo : lo + n], nt, preferred_element_type=jnp.float32)
        meta = ds[2][e, :, 768:896].astype(jnp.float32)
        weight = jnp.zeros((256, 1), jnp.float32)
        number = (first_expert + e).astype(jnp.float32)
        for k in range(4):
            value = meta[:, 68 + k : 69 + k] * 256.0 + meta[:, 72 + k : 73 + k]
            weight = weight + jnp.where(meta[:, 64 + k : 65 + k] == number, value, 0.0)
        hidden = gate * jax.nn.sigmoid(GLU * gate) * (upv + 1.0)
        hidden = (hidden * (weight * (1.0 / 65536.0))).astype(jnp.bfloat16)
        for p, (lo, n, held) in enumerate(PARTS):
            ds[p][e, :, 0:n] = jnp.dot(
                hidden, down_w[e, :, lo : lo + n], preferred_element_type=jnp.float32
            ).astype(jnp.bfloat16)
        return 0

    lax.fori_loop(0, 4, expert, 0)

    pending = []
    for p in range(3):
        n = PARTS[p][1]

        def combine(g, _, p=p, n=n):
            z, yh = g // 2, g % 2
            y = jnp.concatenate([ds[p][e, pl.ds(g * 32, 32), :] for e in range(4)], axis=0)
            got = jnp.dot(table[g], y, preferred_element_type=jnp.float32).astype(jnp.bfloat16)
            xs[p][z, pl.ds(yh * 2, 2)] = got.reshape(2, 4, 2, 16, PARTS[p][2])
            return 0

        lax.fori_loop(0, GROUPS, combine, 0)
        for k, by in enumerate((2, 1, -1, 0)):
            cp = copy(
                view(xs[p], p, 2, by, whole(p), 1 - core), view(ss[p], p, 2, by, whole(p)),
                sx_send.at[p, k], sx_recv.at[p, k], sibling,
            )
            cp.start()
            pending.append(cp)

    def add(dst, *others):
        lead = dst.shape[:-2]
        count = 1
        for s in lead:
            count *= s

        def one(i, _):
            idx = () if not lead else ((i,) if len(lead) == 1 else (i // 4, i % 4))
            total = dst[idx].astype(jnp.float32)
            for o in others:
                total = total + o[idx].astype(jnp.float32)
            dst[idx] = total.astype(jnp.bfloat16)
            return 0

        if lead:
            lax.fori_loop(0, count, one, 0)
        else:
            one(0, 0)

    def rs(p, st, k, src, dst, to):
        cp = copy(src, dst, rs_send.at[p, st, k], rs_recv.at[p, st, k], to)
        cp.start()
        pending.append(cp)

    def rs_wait(p, st, k, dst):
        copy(dst, dst, rs_send.at[p, st, k], rs_recv.at[p, st, k], sibling).wait_recv()

    def sib_wait(p, k, by):
        v = view(ss[p], p, 2, by, whole(p))
        copy(v, v, sx_send.at[p, k], sx_recv.at[p, k], sibling).wait_recv()

    for st in (2, 1, 0):
        for p in range(3):
            a = ORDERS[p][st]
            up, dn = neighbour(a, 1), neighbour(a, -1)
            ha, hb = halves(p)
            r = rbufs[p][st]
            if st == 2:
                sib_wait(p, 0, 2)
                add(view(xs[p], p, st, 2, whole(p), core), view(ss[p], p, st, 2, whole(p)))
            rs(p, st, 0, view(xs[p], p, st, 2, ha, core), r.at[2, ..., ha], up)
            rs(p, st, 1, view(xs[p], p, st, 2, hb, core), r.at[2, ..., hb], dn)
        for p in range(3):
            a = ORDERS[p][st]
            up, dn = neighbour(a, 1), neighbour(a, -1)
            ha, hb = halves(p)
            r = rbufs[p][st]
            if st == 2:
                sib_wait(p, 1, 1)
                add(view(xs[p], p, st, 1, whole(p), core), view(ss[p], p, st, 1, whole(p)))
            rs(p, st, 2, view(xs[p], p, st, 1, hb, core), r.at[0, ..., hb], up)
            if st == 2:
                sib_wait(p, 2, -1)
                add(view(xs[p], p, st, -1, whole(p), core), view(ss[p], p, st, -1, whole(p)))
            rs(p, st, 3, view(xs[p], p, st, -1, ha, core), r.at[1, ..., ha], dn)
        for p in range(3):
            a = ORDERS[p][st]
            up, dn = neighbour(a, 1), neighbour(a, -1)
            ha, hb = halves(p)
            r = rbufs[p][st]
            rs_wait(p, st, 0, r.at[2, ..., ha])
            add(view(xs[p], p, st, 1, ha, core), r.at[2, ..., ha])
            rs(p, st, 4, view(xs[p], p, st, 1, ha, core), r.at[0, ..., ha], up)
            rs_wait(p, st, 1, r.at[2, ..., hb])
            add(view(xs[p], p, st, -1, hb, core), r.at[2, ..., hb])
            rs(p, st, 5, view(xs[p], p, st, -1, hb, core), r.at[1, ..., hb], dn)
        for p in range(3):
            ha, hb = halves(p)
            r = rbufs[p][st]
            own = view(xs[p], p, st, 0, whole(p), core)
            others = [r.at[0], r.at[1]]
            if st == 2:
                sib_wait(p, 3, 0)
                others.append(view(ss[p], p, st, 0, whole(p)))
            rs_wait(p, st, 2, r.at[0, ..., hb])
            rs_wait(p, st, 3, r.at[1, ..., ha])
            rs_wait(p, st, 4, r.at[0, ..., ha])
            rs_wait(p, st, 5, r.at[1, ..., hb])
            if st:
                add(own, *others)
            else:
                lo, n, held = PARTS[p]
                total = own[...].astype(jnp.float32) + r[0].astype(jnp.float32) + r[1].astype(jnp.float32)
                out[:, lo : lo + n] = (resid[:, lo : lo + n] + total[:, :n]).astype(jnp.bfloat16)
    for cp in pending:
        cp.wait_send()


def layer(tokens, attn_gain, mlp_gain, cosine, sine, sinks, meta, weights):
    bf = jnp.bfloat16
    wide = [p[2] for p in PARTS]
    width = tokens.shape[1]
    dma = pltpu.SemaphoreType.DMA
    scratch = (
        [pltpu.VMEM((4, 4, 4, 2, 16, h), bf) for h in wide]
        + [pltpu.VMEM((4, 256, h), bf) for h in wide]
        + [pltpu.VMEM((4, 4, 4, 16, h), bf) for h in wide]
        + [pltpu.VMEM(w.shape, bf) for w in weights[3:]]
        + [pltpu.VMEM((GROUPS, 256, 128), bf), pltpu.VMEM((256, 256), bf)]
        + [pltpu.VMEM((3,) + (4,) * s + (16, h), bf) for h in wide for s in range(3)]
        + [pltpu.VMEM(w.shape, bf) for w in (weights[0], weights[1], weights[2])]
        + [
            pltpu.VMEM((2, 4, 2, 16, width), bf),
            pltpu.VMEM((256, width), bf),
            pltpu.VMEM((256, 64), bf),
            pltpu.VMEM((2, 384, 64), bf),
            pltpu.VMEM((256, 256), bf),
            pltpu.VMEM((256, 256), bf),
            pltpu.VMEM((2, 4, 2, 16, width), bf),
            pltpu.VMEM((2, 4, 16, width), bf),
            pltpu.VMEM((3, 2, 16, width), bf),
            pltpu.VMEM((16, width), bf),
            pltpu.VMEM((16, 2944), jnp.float32),
        ]
        + [
            dma((6,)), dma((3, 3, 6)), dma((3, 3, 6)), dma((3, 3, 4)), dma((3, 3, 4)),
            dma((3, 3, 6)), dma((3, 3, 6)), dma((3, 4)), dma((3, 4)),
            dma((2, 11)), dma((2, 11)), dma((4,)), dma((4,)), dma((11,)), dma((11,)),
        ]
    )
    vm = pl.BlockSpec(memory_space=pltpu.VMEM)
    sm = pl.BlockSpec(memory_space=pltpu.SMEM)
    anym = pl.BlockSpec(memory_space=pl.ANY)
    return pl.pallas_call(
        layer_kernel,
        out_shape=jax.ShapeDtypeStruct(tokens.shape, bf),
        in_specs=[vm] * 5 + [sm, vm] + [anym] * 6,
        out_specs=vm,
        scratch_shapes=scratch,
        compiler_params=pltpu.CompilerParams(
            collective_id=1, has_side_effects=True, vmem_limit_bytes=62 * 1024 * 1024
        ),
        name="layer",
    )(tokens, attn_gain, mlp_gain, cosine, sine, sinks, meta, *weights)


HEAD_DIM = 64
rope_theta = 150000.0


def shards(
    tokens, attn_gain, query_weight, keyval_weight, sink_logits, out_weight,
    mlp_gain, routes, gate_fixed, gate_weight, up_weight, down_weight,
):
    ctx_index = lax.axis_index("ctx")
    shard_len = tokens.shape[0] * lax.axis_size("fsdp")
    half_dim = HEAD_DIM // 2
    freqs = rope_theta ** (-(jnp.arange(half_dim, dtype=jnp.float32) * 2.0 / HEAD_DIM))
    positions = (ctx_index * shard_len + jnp.arange(shard_len, dtype=jnp.int32)).astype(jnp.float32)
    angles = positions[:, None] * freqs[None, :]
    cosine = jnp.tile(jnp.cos(angles), (1, 4))
    sine = jnp.sin(angles)
    sine = jnp.concatenate([-sine, sine, -sine, sine], axis=1)
    high = gate_fixed // 256
    meta = jnp.concatenate([routes, high, gate_fixed - high * 256], axis=1).astype(jnp.float32)
    meta = jnp.pad(meta, ((0, 0), (64, 64 - meta.shape[1])))
    weights = (query_weight, keyval_weight, out_weight.T, gate_weight, up_weight, down_weight)
    return layer(
        tokens, attn_gain[None, :], jnp.pad(mlp_gain, (0, 64))[None, :],
        cosine, sine, sink_logits, meta, weights,
    )


def solution(mesh):
    in_specs = (
        P(("ctx", "fsdp"), None),
        P(),
        P(None, "fsdp"),
        P("fsdp", None),
        P("fsdp"),
        P("fsdp", None),
        P(),
        P(("ctx", "fsdp"), None),
        P(("ctx", "fsdp"), None),
        P("fsdp", "ctx", None),
        P("fsdp", "ctx", None),
        P("fsdp", "ctx", None),
    )
    out_specs = P(("ctx", "fsdp"), None)
    return jax.shard_map(shards, mesh=mesh, in_specs=in_specs, out_specs=out_specs, check_vma=False)
```

```python
import math
import jax
import jax.numpy as jnp
from jax import lax
from jax.experimental import pallas as pl
from jax.experimental.pallas import tpu as pltpu
from jax.sharding import PartitionSpec as P

PARTS = ((0, 1024, 1024), (1024, 1024, 1024), (2048, 832, 896))
ORDERS = ((0, 1, 2), (1, 2, 0), (2, 0, 1))
HALF = 512
GROUPS = 8
GLU = 1.702


def layer_kernel(
    tokens, attn_gain, mlp_gain, sinks, routes, fixed,
    query_hbm, keyval_hbm, outw_hbm, gate_hbm, up_hbm, down_hbm, out,
    x0, x1, x2, d0, d1, d2, s0, s1, s2,
    gate_w, up_w, down_w, stage, hidden_all, gain_pad, table, lower,
    ra0, ra1, ra2, rb0, rb1, rb2, rc0, rc1, rc2,
    query_w, keyval_w, outw_w, gathered, normed, kv_mine, kv_all, queries, attended,
    part, part_sib, part_in, part_last, resid,
    wsem, ag_send, ag_recv, sib_send, sib_recv,
    rs_send, rs_recv, sx_send, sx_recv,
    ta_send, ta_recv, kv_send, kv_recv, tr_send, tr_recv,
):
    xs, ds, ss = (x0, x1, x2), (d0, d1, d2), (s0, s1, s2)
    rbufs = ((ra0, ra1, ra2), (rb0, rb1, rb2), (rc0, rc1, rc2))
    ctx = lax.axis_index("ctx")
    fsdp = lax.axis_index("fsdp")
    core = fsdp % 2
    me = (ctx // 2, (fsdp // 8) * 2 + ctx % 2, (fsdp // 2) % 4)

    def device(z, y, x, c):
        return (z * 2 + y % 2, ((y // 2) * 4 + x) * 2 + c)

    def neighbour(axis, by):
        at = list(me)
        at[axis] = (at[axis] + by + 4) % 4
        return device(*at, core)

    sibling = device(*me, 1 - core)

    def copy(src, dst, ss_, rs_, to):
        return pltpu.make_async_remote_copy(
            src_ref=src, dst_ref=dst, send_sem=ss_, recv_sem=rs_,
            device_id=to, device_id_type=pl.DeviceIdType.MESH,
        )

    loads = [
        pltpu.make_async_copy(h, v, wsem.at[i])
        for i, (h, v) in enumerate(((keyval_hbm, keyval_w), (query_hbm, query_w), (outw_hbm, outw_w)))
    ]
    for w in loads:
        w.start()

    def chunk(i):
        src = (gate_hbm, up_hbm, down_hbm)[i // 4]
        n = 36 if i % 4 == 3 else 48
        return pltpu.make_async_copy(
            src.at[pl.ds((i % 4) * 48, n)], stage.at[i % 2, pl.ds(0, n)], wsem.at[3 + i % 2]
        )

    turned = [0]

    def turn_weights(count):
        for i in range(turned[0], min(turned[0] + count, 12)):
            chunk(i).wait()
            dst = (gate_w, up_w, down_w)[i // 4]
            rows = pl.ds((i % 4) * 48, 48)
            if i % 4 == 3:
                stage[i % 2, 36:48] = jnp.zeros((12, 4, 2880), jnp.bfloat16)

            def tile(t, _):
                cols = pl.ds(pl.multiple_of(t * 256, 256), 256)
                dst[:, rows, cols] = jnp.swapaxes(stage[i % 2, :, :, cols], 0, 1)
                return 0

            lax.fori_loop(0, 11, tile, 0)
            dst[:, rows, 2816:2880] = jnp.swapaxes(stage[i % 2, :, :, 2816:2880], 0, 1)
            if i + 2 < 12:
                chunk(i + 2).start()
            turned[0] = i + 1

    chunk(0).start()
    chunk(1).start()

    def signal(to):
        pl.semaphore_signal(barrier, inc=1, device_id=to, device_id_type=pl.DeviceIdType.MESH)

    barrier = pltpu.get_barrier_semaphore()
    across = neighbour(1, 2)
    partners = [neighbour(a, b) for a in range(3) for b in (1, -1, 2)] + [sibling]
    for to in partners:
        signal(to)
    behind = (ctx + 7) % 8
    ahead = (ctx + 1) % 8
    key_from, value_from = fsdp // 2, 8 + fsdp // 2
    signal((behind, key_from))
    signal((behind, value_from))

    @pl.when(fsdp != 0)
    def _():
        signal((ctx, key_from))

    @pl.when(fsdp != 15)
    def _():
        signal((ctx, value_from))

    yh = me[1] // 2
    gathered[yh, me[2], core] = tokens[...]
    r = lax.broadcasted_iota(jnp.int32, (256, 256), 0)
    c = lax.broadcasted_iota(jnp.int32, (256, 256), 1)
    lower[...] = jnp.where((r // 16 == c // 16) & (c < r), 1.0, 0.0).astype(jnp.bfloat16)
    alone = jnp.where((fsdp == 0) | (fsdp == 15), 1, 0)
    pl.semaphore_wait(barrier, len(partners) + 4 - alone)

    started = []

    def send(src, dst, send_sem, recv_sem, to):
        cp = copy(src, dst, send_sem, recv_sem, to)
        cp.start()
        started.append(cp)

    left, right = neighbour(2, -1), neighbour(2, 1)
    halves_of = (pl.ds(0, 1408), pl.ds(1408, 1472))

    def held(b, by, which, half=None):
        at = gathered.at[(yh + b) % 2, (me[2] + by + 4) % 4, which]
        return at if half is None else at.at[:, halves_of[half]]

    def pass_on(b, by, half, k, to):
        v = held(b, by, core, half)
        send(v, v, ta_send.at[b, k], ta_recv.at[b, k], to)

    def arrived(b, by, half, k):
        v = held(b, by, core, half)
        copy(v, v, ta_send.at[b, k], ta_recv.at[b, k], sibling).wait_recv()

    def to_sibling(b, by, k):
        v = held(b, by, core)
        send(v, v, ta_send.at[b, k], ta_recv.at[b, k], sibling)

    def norm_block(b, by, which):
        y_, x_ = (yh + b) % 2, (me[2] + by + 4) % 4
        v = gathered[y_, x_, which].astype(jnp.float32)
        scale = lax.rsqrt(jnp.sum(v * v, axis=-1, keepdims=True) * (1.0 / 2880.0) + 1e-05)
        row = ((y_ * 4 + x_) * 2 + which) * 16
        normed[pl.ds(pl.multiple_of(row, 16), 16), :] = (v * scale * attn_gain[...].reshape(1, 2880)).astype(jnp.bfloat16)

    lanes = lax.broadcasted_iota(jnp.int32, (256, 128), 1)
    early = lanes % 64 < 32
    freqs = jnp.exp((lanes % 32).astype(jnp.float32) * (-2.0 / 64 * math.log(150000.0)))
    angles = (ctx * 256 + lax.broadcasted_iota(jnp.int32, (256, 128), 0)).astype(jnp.float32) * freqs

    send(held(0, 0, core), held(0, 0, core), ta_send.at[0, 10], ta_recv.at[0, 10], across)
    for b in range(2):
        if b == 1:
            v = held(1, 0, core)
            copy(v, v, ta_send.at[0, 10], ta_recv.at[0, 10], sibling).wait_recv()
        pass_on(b, 0, 0, 0, right)
        pass_on(b, 0, 1, 1, left)
        pass_on(b, 0, 1, 2, right)
        pass_on(b, 0, 0, 3, left)
        to_sibling(b, 0, 6)
        norm_block(b, 0, core)
        if b == 0:
            cosine = jnp.cos(angles)
            sine = jnp.sin(angles)
            sine = jnp.where(early, -sine, sine)
    for b in range(2):
        arrived(b, -1, 0, 0)
        pass_on(b, -1, 0, 4, right)
        arrived(b, 1, 1, 1)
        pass_on(b, 1, 1, 5, left)
    for b in range(2):
        arrived(b, -1, 1, 2)
        to_sibling(b, -1, 7)
        arrived(b, 1, 0, 3)
        to_sibling(b, 1, 8)
        norm_block(b, -1, core)
        norm_block(b, 1, core)
    for b in range(2):
        arrived(b, 2, 0, 4)
        arrived(b, 2, 1, 5)
        to_sibling(b, 2, 9)
        norm_block(b, 2, core)
    for k, by in ((6, 0), (7, -1), (8, 1), (9, 2)):
        for b in range(2):
            v = held(b, by, 1 - core)
            copy(v, v, ta_send.at[b, k], ta_recv.at[b, k], sibling).wait_recv()
            norm_block(b, by, 1 - core)

    nt = (((1,), (1,)), ((), ()))

    def turn(v, c_, s_):
        return v * c_ + jnp.where(early, pltpu.roll(v, 96, 1), pltpu.roll(v, 32, 1)) * s_

    loads[0].wait()
    kv = lax.dot_general(normed[...], keyval_w[...], nt, preferred_element_type=jnp.float32)
    kv = jnp.concatenate([kv, kv], axis=1)
    kv = jnp.where(fsdp < 8, turn(kv, cosine, sine), kv)
    kv_mine[...] = kv[:, :64].astype(jnp.bfloat16)
    which = fsdp // 8
    main, rim = pl.ds(128, 256), pl.ds(0, 128)
    wait_main = []
    for i in range(2):
        to = 2 * (fsdp % 8) + i
        cp = copy(kv_mine, kv_all.at[which, main], kv_send.at[i], kv_recv.at[which * 2], (ctx, to))
        own = fsdp == 15 * i

        @pl.when(jnp.logical_not(own))
        def _(cp=cp):
            cp.start()

        @pl.when(own)
        def _():
            kv_all[which, main] = kv_mine[...]

        wait_main.append((own, cp))
        send(
            kv_mine.at[pl.ds(128, 128)], kv_all.at[which, rim],
            kv_send.at[2 + i], kv_recv.at[which * 2 + 1], (ahead, to),
        )
    loads[1].wait()
    query = jnp.dot(normed[...], query_w[...], preferred_element_type=jnp.float32)
    for i in range(2):
        cols = slice(i * 128, i * 128 + 128)
        queries[:, cols] = turn(query[:, cols], cosine, sine).astype(jnp.bfloat16)
    for w in range(2):
        v = kv_all.at[w, main]

        @pl.when(fsdp != 15 * w)
        def _(v=v, w=w):
            copy(v, v, kv_send.at[0], kv_recv.at[w * 2], sibling).wait_recv()

        v = kv_all.at[w, rim]
        copy(v, v, kv_send.at[0], kv_recv.at[w * 2 + 1], sibling).wait_recv()
    for own, cp in wait_main:

        @pl.when(jnp.logical_not(own))
        def _(cp=cp):
            cp.wait_send()

    row = lax.broadcasted_iota(jnp.int32, (128, 256), 0)
    col = lax.broadcasted_iota(jnp.int32, (128, 256), 1)
    for b in range(2):
        allowed = (col <= row + 128) & (col > row) & (ctx * 256 + b * 128 - 128 + col >= 0)
        keys = kv_all[0, b * 128 : b * 128 + 256]
        values = kv_all[1, b * 128 : b * 128 + 256]
        for h in range(4):
            q = queries[b * 128 : b * 128 + 128, h * 64 : h * 64 + 64]
            score = lax.dot_general(q, keys, nt, preferred_element_type=jnp.float32) * 0.125
            score = jnp.where(allowed, score, -1e30)
            sink = sinks[h]
            top = jnp.maximum(jnp.max(score, axis=-1, keepdims=True), sink)
            expd = jnp.exp(score - top)
            total = jnp.exp(sink - top) + jnp.sum(expd, axis=-1, keepdims=True)
            probs = (expd / total).astype(jnp.bfloat16)
            mixed = jnp.dot(probs, values, preferred_element_type=jnp.float32)
            attended[b * 128 : b * 128 + 128, h * 64 : h * 64 + 64] = mixed.astype(jnp.bfloat16)

    loads[2].wait()
    for lo, n in ((0, 1024), (1024, 1024), (2048, 832)):
        got = lax.dot_general(
            attended[...], outw_w[lo : lo + n, :], nt, preferred_element_type=jnp.float32
        ).astype(jnp.bfloat16)
        part[:, :, :, :, lo : lo + n] = got.reshape(2, 4, 2, 16, n)

    def piece(by, half=None):
        cols = slice(None) if half is None else halves_of[half]
        return part.at[:, (me[2] + by + 4) % 4, core, :, cols]

    def landed(slot, half):
        return part_in.at[slot, :, :, halves_of[half]]

    def from_sibling(by):
        return part_sib.at[:, (me[2] + by + 4) % 4]

    def tr_wait(k, v):
        copy(v, v, tr_send.at[k], tr_recv.at[k], sibling).wait_recv()

    def plus(dst, *others):
        for i in range(2):
            total = dst[i].astype(jnp.float32)
            for o in others:
                total = total + o[i].astype(jnp.float32)
            dst[i] = total.astype(jnp.bfloat16)

    for k, by in enumerate((2, 1, -1, 0)):
        send(
            part.at[:, (me[2] + by + 4) % 4, 1 - core], from_sibling(by),
            tr_send.at[k], tr_recv.at[k], sibling,
        )
    tr_wait(0, from_sibling(2))
    plus(piece(2), from_sibling(2))
    send(piece(2, 0), landed(2, 0), tr_send.at[4], tr_recv.at[4], right)
    send(piece(2, 1), landed(2, 1), tr_send.at[5], tr_recv.at[5], left)
    tr_wait(1, from_sibling(1))
    plus(piece(1), from_sibling(1))
    send(piece(1, 1), landed(0, 1), tr_send.at[6], tr_recv.at[6], right)
    tr_wait(2, from_sibling(-1))
    plus(piece(-1), from_sibling(-1))
    send(piece(-1, 0), landed(1, 0), tr_send.at[7], tr_recv.at[7], left)
    tr_wait(4, landed(2, 0))
    plus(piece(1, 0), landed(2, 0))
    send(piece(1, 0), landed(0, 0), tr_send.at[8], tr_recv.at[8], right)
    tr_wait(5, landed(2, 1))
    plus(piece(-1, 1), landed(2, 1))
    send(piece(-1, 1), landed(1, 1), tr_send.at[9], tr_recv.at[9], left)
    tr_wait(3, from_sibling(0))
    plus(piece(0), from_sibling(0))
    tr_wait(6, landed(0, 1))
    tr_wait(7, landed(1, 0))
    tr_wait(8, landed(0, 0))
    tr_wait(9, landed(1, 1))
    plus(piece(0), part_in.at[0], part_in.at[1])
    send(part.at[1 - yh, me[2], core], part_last, tr_send.at[10], tr_recv.at[10], across)
    tr_wait(10, part_last)
    total = part[yh, me[2], core].astype(jnp.float32) + part_last[...].astype(jnp.float32)
    resid[:, 2816:2944] = jnp.zeros((16, 128), jnp.float32)
    resid[:, 0:2880] = tokens[...].astype(jnp.float32) + total
    v = resid[...]
    scale = lax.rsqrt(jnp.sum(v * v, axis=-1, keepdims=True) * (1.0 / 2880.0) + 1e-05)
    gain_pad[...] = jnp.zeros((1, 2944), jnp.float32)
    gain_pad[:, 0:2880] = mlp_gain[...].reshape(1, 2880)
    v = v * scale * gain_pad[...]
    high = fixed[...] // 256
    low = fixed[...] - high * 256
    meta = jnp.concatenate([routes[...], high, low, jnp.zeros((4, 16), jnp.int32)], axis=0)
    meta = meta.astype(jnp.float32).T.astype(jnp.bfloat16)
    spot = lax.broadcasted_iota(jnp.int32, (16, 128), 0) + 64 == lax.broadcasted_iota(jnp.int32, (16, 128), 1)
    meta = jnp.dot(meta, jnp.where(spot, 1.0, 0.0).astype(jnp.bfloat16), preferred_element_type=jnp.float32)
    for p, (lo, n, wide) in enumerate(PARTS):
        w = v[:, lo : lo + wide]
        if p == 2:
            w = jnp.concatenate([w[:, :768], w[:, 768:] + meta], axis=1)
        xs[p][me[0], me[1], me[2], core] = w.astype(jnp.bfloat16)
    for cp in started:
        cp.wait_send()

    ALL = "all"

    def where_(p, offsets, drop=()):
        idx = [None] * 3
        for s, o in enumerate(offsets):
            a = ORDERS[p][s]
            idx[a] = slice(None) if o is ALL else (me[a] + o + 4) % 4
        return tuple(idx[a] for a in range(3) if a not in [ORDERS[p][s] for s in drop])

    def cols_of(p, half):
        if half is None:
            return pl.ds(0, PARTS[p][2])
        return (pl.ds(0, HALF), pl.ds(HALF, PARTS[p][2] - HALF))[half]

    def mine(p, offsets, half=None, which=None):
        which = core if which is None else which
        return xs[p].at[where_(p, offsets) + (which, slice(None), cols_of(p, half))]

    def ways(p, s):
        return neighbour(ORDERS[p][s], 1), neighbour(ORDERS[p][s], -1)

    pending = []

    def ag(p, k, v, to):
        cp = copy(v, v, ag_send.at[p, k], ag_recv.at[p, k], to)
        cp.start()
        pending.append(cp)

    def ag_wait(p, k, v):
        copy(v, v, ag_send.at[p, k], ag_recv.at[p, k], sibling).wait_recv()

    forwards = []

    def forward(p, offsets):
        k = len([f for f in forwards if f[0] == p])
        forwards.append((p, k, offsets))
        v = mine(p, offsets)
        cp = copy(v, v, sib_send.at[p, k], sib_recv.at[p, k], sibling)
        cp.start()
        pending.append(cp)

    def third(p, j):
        up, dn = ways(p, 2)
        k = 9 + (j % 4) * 4
        ag(p, k, mine(p, (ALL, j, 0)), up)
        ag(p, k + 1, mine(p, (ALL, j, 0)), dn)

    def third_relay(p, j):
        up, dn = ways(p, 2)
        k = 9 + (j % 4) * 4
        ag_wait(p, k, mine(p, (ALL, j, -1)))
        ag(p, k + 2, mine(p, (ALL, j, -1), 0), up)
        ag_wait(p, k + 1, mine(p, (ALL, j, 1)))
        ag(p, k + 3, mine(p, (ALL, j, 1), 1), dn)
        forward(p, (ALL, j, -1))
        forward(p, (ALL, j, 1))

    def third_end(p, j):
        k = 9 + (j % 4) * 4
        ag_wait(p, k + 2, mine(p, (ALL, j, 2), 0))
        ag_wait(p, k + 3, mine(p, (ALL, j, 2), 1))
        forward(p, (ALL, j, 2))

    for p in range(3):
        own = mine(p, (0, 0, 0))
        up, dn = ways(p, 0)
        ag(p, 0, own, up)
        ag(p, 1, own, dn)
        ag(p, 2, own, neighbour(ORDERS[p][0], 2))
    turn_weights(2)
    for p in range(3):
        ag_wait(p, 0, mine(p, (-1, 0, 0)))
        ag_wait(p, 1, mine(p, (1, 0, 0)))
        ag_wait(p, 2, mine(p, (2, 0, 0)))
        up, dn = ways(p, 1)
        ag(p, 3, mine(p, (ALL, 0, 0), 0), up)
        ag(p, 4, mine(p, (ALL, 0, 0), 1), dn)
        ag(p, 5, mine(p, (ALL, 0, 0), 1), up)
        ag(p, 6, mine(p, (ALL, 0, 0), 0), dn)
        third(p, 0)
        forward(p, (ALL, 0, 0))
    turn_weights(2)
    for p in range(3):
        up, dn = ways(p, 1)
        ag_wait(p, 3, mine(p, (ALL, -1, 0), 0))
        ag(p, 7, mine(p, (ALL, -1, 0), 0), up)
        ag_wait(p, 4, mine(p, (ALL, 1, 0), 1))
        ag(p, 8, mine(p, (ALL, 1, 0), 1), dn)
    for p in range(3):
        ag_wait(p, 5, mine(p, (ALL, -1, 0), 1))
        third(p, -1)
        ag_wait(p, 6, mine(p, (ALL, 1, 0), 0))
        third(p, 1)
        forward(p, (ALL, -1, 0))
        forward(p, (ALL, 1, 0))
    turn_weights(1)
    for p in range(3):
        third_relay(p, 0)
    turn_weights(1)
    for p in range(3):
        ag_wait(p, 7, mine(p, (ALL, 2, 0), 0))
        ag_wait(p, 8, mine(p, (ALL, 2, 0), 1))
        third(p, 2)
        forward(p, (ALL, 2, 0))
    turn_weights(1)
    for p in range(3):
        third_end(p, 0)
        third_relay(p, -1)
    turn_weights(2)
    for p in range(3):
        third_relay(p, 1)
        third_end(p, -1)
    turn_weights(2)
    for p in range(3):
        third_relay(p, 2)
        third_end(p, 1)
    turn_weights(12)
    for p in range(3):
        third_end(p, 2)
    for p, k, offsets in forwards:
        v = mine(p, offsets, None, 1 - core)
        copy(v, v, sib_send.at[p, k], sib_recv.at[p, k], sibling).wait_recv()
    for cp in pending:
        cp.wait_send()

    first_expert = fsdp * 4
    lane = lax.broadcasted_iota(jnp.int32, (256, 128), 1)
    row = lax.broadcasted_iota(jnp.int32, (256, 128), 0)
    lane_expert = (first_expert + lane // 32).astype(jnp.float32)
    lane_slot = ((lane % 32) // 16).astype(jnp.float32)
    same_source = row // 16 == lane % 16

    def dispatch(g, _):
        z, yh = g // 2, g % 2

        def rows(p):
            return xs[p][z, pl.ds(yh * 2, 2)].reshape(256, PARTS[p][2])

        last = rows(2)
        ids = last[:, 768:896].astype(jnp.float32)
        hit = jnp.zeros((256, 128), jnp.float32)
        for k in range(4):
            hit = hit + jnp.where(ids[:, 64 + k : 65 + k] == lane_expert, 1.0, 0.0)
        rank = jnp.dot(lower[...], hit.astype(jnp.bfloat16), preferred_element_type=jnp.float32)
        t = jnp.where((rank == lane_slot) & same_source, hit, 0.0)
        table[g] = t.astype(jnp.bfloat16)
        pick = t.T.astype(jnp.bfloat16)
        for p in range(3):
            src = last if p == 2 else rows(p)
            got = jnp.dot(pick, src, preferred_element_type=jnp.float32).astype(jnp.bfloat16)
            for e in range(4):
                ds[p][e, pl.ds(g * 32, 32), :] = got[e * 32 : (e + 1) * 32]
        return 0

    lax.fori_loop(0, GROUPS, dispatch, 0)

    def expert(e, _):
        gate = jnp.zeros((256, 192), jnp.float32)
        upv = jnp.zeros((256, 192), jnp.float32)
        for p, (lo, n, held) in enumerate(PARTS):
            y = ds[p][e, :, 0:n]
            gate = gate + lax.dot_general(y, gate_w[e, :, lo : lo + n], nt, preferred_element_type=jnp.float32)
            upv = upv + lax.dot_general(y, up_w[e, :, lo : lo + n], nt, preferred_element_type=jnp.float32)
        about = ds[2][e, :, 768:896].astype(jnp.float32)
        weight = jnp.zeros((256, 1), jnp.float32)
        number = (first_expert + e).astype(jnp.float32)
        for k in range(4):
            value = about[:, 68 + k : 69 + k] * 256.0 + about[:, 72 + k : 73 + k]
            weight = weight + jnp.where(about[:, 64 + k : 65 + k] == number, value, 0.0)
        hidden = gate * jax.nn.sigmoid(GLU * gate) * (upv + 1.0)
        hidden_all[e] = (hidden * (weight * (1.0 / 65536.0))).astype(jnp.bfloat16)
        return 0

    lax.fori_loop(0, 4, expert, 0)

    pending = []
    turns = (2, 1, -1, 0)

    def other(p, offsets):
        return ss[p].at[where_(p, offsets)]

    def land3(p, slot, j, half=None):
        return rbufs[p][2].at[(slot,) + where_(p, (ALL, j, 0), (2,)) + (slice(None), cols_of(p, half))]

    def land2(p, slot, half=None):
        return rbufs[p][1].at[slot, :, :, cols_of(p, half)]

    def rs(p, k, src, dst, to):
        cp = copy(src, dst, rs_send.at[p, k], rs_recv.at[p, k], to)
        cp.start()
        pending.append(cp)

    def rs_wait(p, k, dst):
        copy(dst, dst, rs_send.at[p, k], rs_recv.at[p, k], sibling).wait_recv()

    def add(dst, *others):
        def one(i, _):
            total = dst[i].astype(jnp.float32)
            for o in others:
                total = total + o[i].astype(jnp.float32)
            dst[i] = total.astype(jnp.bfloat16)
            return 0

        lax.fori_loop(0, 4, one, 0)

    def half_of(ref, p, half):
        return ref.at[:, :, cols_of(p, half)]

    def first(p, j):
        v = other(p, (ALL, j, ALL))
        copy(v, v, sx_send.at[p, j % 4], sx_recv.at[p, j % 4], sibling).wait_recv()
        up, dn = ways(p, 2)
        k = 9 + (j % 4) * 4
        add(mine(p, (ALL, j, 2)), other(p, (ALL, j, 2)))
        rs(p, k, mine(p, (ALL, j, 2), 0), land3(p, 2, j, 0), up)
        rs(p, k + 1, mine(p, (ALL, j, 2), 1), land3(p, 2, j, 1), dn)

    def mid(p, j):
        up, dn = ways(p, 2)
        k = 9 + (j % 4) * 4
        add(mine(p, (ALL, j, 1), 1), half_of(other(p, (ALL, j, 1)), p, 1))
        add(mine(p, (ALL, j, -1), 0), half_of(other(p, (ALL, j, -1)), p, 0))
        rs_wait(p, k, land3(p, 2, j, 0))
        add(mine(p, (ALL, j, 1), 0), half_of(other(p, (ALL, j, 1)), p, 0), land3(p, 2, j, 0))
        rs(p, k + 2, mine(p, (ALL, j, 1)), land3(p, 0, j), up)
        rs_wait(p, k + 1, land3(p, 2, j, 1))
        add(mine(p, (ALL, j, -1), 1), half_of(other(p, (ALL, j, -1)), p, 1), land3(p, 2, j, 1))
        rs(p, k + 3, mine(p, (ALL, j, -1)), land3(p, 1, j), dn)

    def last(p, j):
        k = 9 + (j % 4) * 4
        rs_wait(p, k + 2, land3(p, 0, j))
        rs_wait(p, k + 3, land3(p, 1, j))
        add(mine(p, (ALL, j, 0)), other(p, (ALL, j, 0)), land3(p, 0, j), land3(p, 1, j))
        up, dn = ways(p, 1)
        if j == 2:
            rs(p, 3, mine(p, (ALL, 2, 0), 0), land2(p, 2, 0), up)
            rs(p, 4, mine(p, (ALL, 2, 0), 1), land2(p, 2, 1), dn)
        if j == 1:
            rs(p, 5, mine(p, (ALL, 1, 0), 1), land2(p, 0, 1), up)
        if j == -1:
            rs(p, 6, mine(p, (ALL, -1, 0), 0), land2(p, 1, 0), dn)

    def second(p):
        up, dn = ways(p, 1)
        rs_wait(p, 3, land2(p, 2, 0))
        add(mine(p, (ALL, 1, 0), 0), land2(p, 2, 0))
        rs(p, 7, mine(p, (ALL, 1, 0), 0), land2(p, 0, 0), up)
        rs_wait(p, 4, land2(p, 2, 1))
        add(mine(p, (ALL, -1, 0), 1), land2(p, 2, 1))
        rs(p, 8, mine(p, (ALL, -1, 0), 1), land2(p, 1, 1), dn)

    def second_end(p):
        rs_wait(p, 5, land2(p, 0, 1))
        rs_wait(p, 6, land2(p, 1, 0))
        rs_wait(p, 7, land2(p, 0, 0))
        rs_wait(p, 8, land2(p, 1, 1))
        add(mine(p, (ALL, 0, 0)), land2(p, 0), land2(p, 1))
        up, dn = ways(p, 0)
        rs(p, 0, mine(p, (1, 0, 0)), rbufs[p][0].at[0], up)
        rs(p, 1, mine(p, (-1, 0, 0)), rbufs[p][0].at[1], dn)
        rs(p, 2, mine(p, (2, 0, 0)), rbufs[p][0].at[2], neighbour(ORDERS[p][0], 2))

    def produce(p):
        lo, n, wide = PARTS[p]

        def down(e, _):
            ds[p][e, :, 0:n] = jnp.dot(
                hidden_all[e], down_w[e, :, lo : lo + n], preferred_element_type=jnp.float32
            ).astype(jnp.bfloat16)
            return 0

        lax.fori_loop(0, 4, down, 0)

        def combine(g, _):
            z, yh_ = g // 2, g % 2
            y = jnp.concatenate([ds[p][e, pl.ds(g * 32, 32), :] for e in range(4)], axis=0)
            got = jnp.dot(table[g], y, preferred_element_type=jnp.float32).astype(jnp.bfloat16)
            xs[p][z, pl.ds(yh_ * 2, 2)] = got.reshape(2, 4, 2, 16, wide)
            return 0

        lax.fori_loop(0, GROUPS, combine, 0)
        for j in turns:
            cp = copy(
                mine(p, (ALL, j, ALL), None, 1 - core), other(p, (ALL, j, ALL)),
                sx_send.at[p, j % 4], sx_recv.at[p, j % 4], sibling,
            )
            cp.start()
            pending.append(cp)

    produce(0)
    produce(1)
    first(0, 2)
    first(0, 1)
    produce(2)
    first(1, 2)
    first(1, 1)
    first(0, -1)
    first(0, 0)
    mid(0, 2)
    first(2, 2)
    first(2, 1)
    mid(1, 2)
    first(1, -1)
    first(1, 0)
    mid(0, 1)
    mid(2, 2)
    first(2, -1)
    first(2, 0)
    mid(1, 1)
    mid(2, 1)
    for p in range(3):
        last(p, 2)
        mid(p, -1)
    for p in range(3):
        last(p, 1)
        mid(p, 0)
    for p in range(3):
        last(p, -1)
        second(p)
    for p in range(3):
        last(p, 0)
    for p in range(3):
        second_end(p)
    for p, (lo, n, wide) in enumerate(PARTS):
        total = mine(p, (0, 0, 0))[...].astype(jnp.float32)
        for s in range(3):
            rs_wait(p, s, rbufs[p][0].at[s])
            total = total + rbufs[p][0][s].astype(jnp.float32)
        out[:, lo : lo + n] = (resid[:, lo : lo + n] + total[:, :n]).astype(jnp.bfloat16)
    for cp in pending:
        cp.wait_send()


def layer(tokens, attn_gain, mlp_gain, sinks, routes, fixed, weights):
    bf = jnp.bfloat16
    wide = [p[2] for p in PARTS]
    width = tokens.shape[1]
    dma = pltpu.SemaphoreType.DMA
    scratch = (
        [pltpu.VMEM((4, 4, 4, 2, 16, h), bf) for h in wide]
        + [pltpu.VMEM((4, 256, h), bf) for h in wide]
        + [pltpu.VMEM((4, 4, 4, 16, h), bf) for h in wide]
        + [pltpu.VMEM((4, 192, width), bf)] * 3
        + [
            pltpu.VMEM((2, 48, 4, width), bf),
            pltpu.VMEM((4, 256, 192), bf),
            pltpu.VMEM((1, 2944), jnp.float32),
        ]
        + [pltpu.VMEM((GROUPS, 256, 128), bf), pltpu.VMEM((256, 256), bf)]
        + [pltpu.VMEM((3,) + (4,) * s + (16, h), bf) for h in wide for s in range(3)]
        + [pltpu.VMEM(w.shape, bf) for w in (weights[0], weights[1], weights[2])]
        + [
            pltpu.VMEM((2, 4, 2, 16, width), bf),
            pltpu.VMEM((256, width), bf),
            pltpu.VMEM((256, 64), bf),
            pltpu.VMEM((2, 384, 64), bf),
            pltpu.VMEM((256, 256), bf),
            pltpu.VMEM((256, 256), bf),
            pltpu.VMEM((2, 4, 2, 16, width), bf),
            pltpu.VMEM((2, 4, 16, width), bf),
            pltpu.VMEM((3, 2, 16, width), bf),
            pltpu.VMEM((16, width), bf),
            pltpu.VMEM((16, 2944), jnp.float32),
        ]
        + [
            dma((5,)), dma((3, 25)), dma((3, 25)), dma((3, 16)), dma((3, 16)),
            dma((3, 25)), dma((3, 25)), dma((3, 4)), dma((3, 4)),
            dma((2, 11)), dma((2, 11)), dma((4,)), dma((4,)), dma((11,)), dma((11,)),
        ]
    )
    vm = pl.BlockSpec(memory_space=pltpu.VMEM)
    sm = pl.BlockSpec(memory_space=pltpu.SMEM)
    anym = pl.BlockSpec(memory_space=pl.ANY)
    return pl.pallas_call(
        layer_kernel,
        out_shape=jax.ShapeDtypeStruct(tokens.shape, bf),
        in_specs=[vm] * 3 + [sm] + [vm] * 2 + [anym] * 6,
        out_specs=vm,
        scratch_shapes=scratch,
        compiler_params=pltpu.CompilerParams(
            collective_id=1, has_side_effects=True, vmem_limit_bytes=62 * 1024 * 1024
        ),
        name="layer",
    )(tokens, attn_gain, mlp_gain, sinks, routes, fixed, *weights)


def shards(
    tokens, attn_gain, query_weight, keyval_weight, sink_logits, out_weight,
    mlp_gain, routes, gate_fixed, gate_weight, up_weight, down_weight,
):
    experts = [jnp.transpose(w, (1, 0, 2)) for w in (gate_weight, up_weight, down_weight)]
    weights = (query_weight, keyval_weight, out_weight.T, *experts)
    return layer(tokens, attn_gain, mlp_gain, sink_logits, routes.T, gate_fixed.T, weights)


def solution(mesh):
    in_specs = (
        P(("ctx", "fsdp"), None),
        P(),
        P(None, "fsdp"),
        P("fsdp", None),
        P("fsdp"),
        P("fsdp", None),
        P(),
        P(("ctx", "fsdp"), None),
        P(("ctx", "fsdp"), None),
        P("fsdp", "ctx", None),
        P("fsdp", "ctx", None),
        P("fsdp", "ctx", None),
    )
    out_specs = P(("ctx", "fsdp"), None)
    return jax.shard_map(shards, mesh=mesh, in_specs=in_specs, out_specs=out_specs, check_vma=False)
```

```python
import math
import jax
import jax.numpy as jnp
from jax import lax
from jax.experimental import pallas as pl
from jax.experimental.pallas import tpu as pltpu
from jax.sharding import PartitionSpec as P

PARTS = ((0, 1024, 1024), (1024, 1024, 1024), (2048, 832, 896))
ORDERS = ((0, 1, 2), (1, 2, 0), (2, 0, 1))
HALF = 512
GROUPS = 8
GLU = 1.702


def layer_kernel(
    tokens, attn_gain, mlp_gain, sinks, routes, fixed,
    query_hbm, keyval_hbm, outw_hbm, gate_hbm, up_hbm, down_hbm, out,
    x0, x1, x2, d0, d1, d2, s0, s1, s2,
    gate_w, up_w, down_w, stage, hidden_all, gain_pad, table, lower,
    ra0, ra1, ra2, rb0, rb1, rb2, rc0, rc1, rc2,
    query_w, keyval_w, outw_w, gathered, normed, kv_mine, kv_all, queries, attended,
    part, part_sib, part_in, part_last, resid,
    wsem, ag_send, ag_recv, sib_send, sib_recv,
    rs_send, rs_recv, sx_send, sx_recv,
    ta_send, ta_recv, kv_send, kv_recv, tr_send, tr_recv,
):
    xs, ds, ss = (x0, x1, x2), (d0, d1, d2), (s0, s1, s2)
    rbufs = ((ra0, ra1, ra2), (rb0, rb1, rb2), (rc0, rc1, rc2))
    ctx = lax.axis_index("ctx")
    fsdp = lax.axis_index("fsdp")
    core = lax.rem(fsdp, 2)
    me = (lax.div(ctx, 2), lax.div(fsdp, 8) * 2 + lax.rem(ctx, 2), lax.rem(lax.div(fsdp, 2), 4))
    shifted = [[me[a]] + [lax.rem(me[a] + by, 4) for by in (1, 2, 3)] for a in range(3)]

    def device(z, y, x, c):
        return (z * 2 + lax.rem(y, 2), (lax.div(y, 2) * 4 + x) * 2 + c)

    def neighbour(axis, by):
        at = list(me)
        at[axis] = shifted[axis][by % 4]
        return device(*at, core)

    sibling = device(*me, 1 - core)

    def copy(src, dst, ss_, rs_, to):
        return pltpu.make_async_remote_copy(
            src_ref=src, dst_ref=dst, send_sem=ss_, recv_sem=rs_,
            device_id=to, device_id_type=pl.DeviceIdType.MESH,
        )

    loads = [
        pltpu.make_async_copy(h, v, wsem.at[i])
        for i, (h, v) in enumerate(((keyval_hbm, keyval_w), (query_hbm, query_w), (outw_hbm, outw_w)))
    ]
    for w in loads:
        w.start()

    def chunk(i):
        src = (gate_hbm, up_hbm, down_hbm)[i // 4]
        n = 36 if i % 4 == 3 else 48
        return pltpu.make_async_copy(
            src.at[pl.ds((i % 4) * 48, n)], stage.at[i % 2, pl.ds(0, n)], wsem.at[3 + i % 2]
        )

    turned = [0]

    def turn_weights(count):
        for i in range(turned[0], min(turned[0] + count, 12)):
            chunk(i).wait()
            dst = (gate_w, up_w, down_w)[i // 4]
            rows = pl.ds((i % 4) * 48, 48)
            if i % 4 == 3:
                stage[i % 2, 36:48] = jnp.zeros((12, 4, 2880), jnp.bfloat16)

            def tile(t, _):
                cols = pl.ds(pl.multiple_of(t * 256, 256), 256)
                dst[:, rows, cols] = jnp.swapaxes(stage[i % 2, :, :, cols], 0, 1)
                return 0

            lax.fori_loop(0, 11, tile, 0)
            dst[:, rows, 2816:2880] = jnp.swapaxes(stage[i % 2, :, :, 2816:2880], 0, 1)
            if i + 2 < 12:
                chunk(i + 2).start()
            turned[0] = i + 1

    chunk(0).start()
    chunk(1).start()

    def signal(to):
        pl.semaphore_signal(barrier, inc=1, device_id=to, device_id_type=pl.DeviceIdType.MESH)

    barrier = pltpu.get_barrier_semaphore()
    across = neighbour(1, 2)
    diagonal = [device(me[0], shifted[1][2], shifted[2][by % 4], core) for by in range(4)]
    partners = [neighbour(a, b) for a in range(3) for b in (1, -1, 2)] + [sibling] + diagonal[1:]
    for to in partners:
        signal(to)
    behind = (ctx + 7) % 8
    ahead = (ctx + 1) % 8
    key_from, value_from = fsdp // 2, 8 + fsdp // 2
    signal((behind, key_from))
    signal((behind, value_from))

    @pl.when(fsdp != 0)
    def _():
        signal((ctx, key_from))

    @pl.when(fsdp != 15)
    def _():
        signal((ctx, value_from))

    yh = lax.div(me[1], 2)
    ys = (yh, 1 - yh)
    gathered[yh, me[2], core] = tokens[...]
    r = lax.broadcasted_iota(jnp.int32, (256, 256), 0)
    c = lax.broadcasted_iota(jnp.int32, (256, 256), 1)
    lower[...] = jnp.where((r // 16 == c // 16) & (c < r), 1.0, 0.0).astype(jnp.bfloat16)
    alone = jnp.where((fsdp == 0) | (fsdp == 15), 1, 0)
    pl.semaphore_wait(barrier, len(partners) + 4 - alone)

    started = []

    def send(src, dst, send_sem, recv_sem, to):
        cp = copy(src, dst, send_sem, recv_sem, to)
        cp.start()
        started.append(cp)

    left, right = neighbour(2, -1), neighbour(2, 1)
    halves_of = (pl.ds(0, 1408), pl.ds(1408, 1472))

    def held(b, by, which):
        return gathered.at[ys[b], shifted[2][by % 4], which]

    def norm_block(b, by, which):
        y_, x_ = ys[b], shifted[2][by % 4]
        v = gathered[y_, x_, which].astype(jnp.float32)
        scale = lax.rsqrt(jnp.sum(v * v, axis=-1, keepdims=True) * (1.0 / 2880.0) + 1e-05)
        row = ((y_ * 4 + x_) * 2 + which) * 16
        normed[pl.ds(pl.multiple_of(row, 16), 16), :] = (v * scale * attn_gain[...].reshape(1, 2880)).astype(jnp.bfloat16)

    lanes = lax.broadcasted_iota(jnp.int32, (256, 128), 1)
    early = lanes % 64 < 32
    freqs = jnp.exp((lanes % 32).astype(jnp.float32) * (-2.0 / 64 * math.log(150000.0)))
    angles = (ctx * 256 + lax.broadcasted_iota(jnp.int32, (256, 128), 0)).astype(jnp.float32) * freqs

    mates = ((1, 2), (1, 1), (1, -1), (0, 2), (1, 0), (0, 1), (0, -1))
    own = held(0, 0, core)
    for b, by in mates:
        to = diagonal[by % 4] if b else neighbour(2, by)
        copy(own, own, ta_send.at[0], ta_recv.at[b * 4 + by % 4], to).start()
    copy(own, own, ta_send.at[1], ta_recv.at[8], sibling).start()
    norm_block(0, 0, core)
    cosine = jnp.cos(angles)
    sine = jnp.sin(angles)
    sine = jnp.where(early, -sine, sine)
    turn_weights(4)
    for b, by in ((0, -1), (0, 1), (1, 0), (0, 2), (1, -1), (1, 1), (1, 2)):
        v = held(b, by, core)
        copy(v, v, ta_send.at[0], ta_recv.at[b * 4 + -by % 4], sibling).wait_recv()
        copy(v, v, ta_send.at[1], ta_recv.at[8], sibling).start()
        norm_block(b, by, core)
    v = gathered.at[:, :, 1 - core]
    copy(v, v, ta_send.at[1], ta_recv.at[8], sibling).wait_recv()
    for b in range(2):
        for by in range(4):
            norm_block(b, by, 1 - core)

    nt = (((1,), (1,)), ((), ()))

    def turn(v, c_, s_):
        return v * c_ + jnp.where(early, pltpu.roll(v, 96, 1), pltpu.roll(v, 32, 1)) * s_

    loads[0].wait()
    kv = lax.dot_general(normed[...], keyval_w[...], nt, preferred_element_type=jnp.float32)
    kv = jnp.concatenate([kv, kv], axis=1)
    kv = jnp.where(fsdp < 8, turn(kv, cosine, sine), kv)
    kv_mine[...] = kv[:, :64].astype(jnp.bfloat16)
    which = fsdp // 8
    main, rim = pl.ds(128, 256), pl.ds(0, 128)
    wait_main = []
    for i in range(2):
        to = 2 * (fsdp % 8) + i
        cp = copy(kv_mine, kv_all.at[which, main], kv_send.at[i], kv_recv.at[which * 2], (ctx, to))
        own = fsdp == 15 * i

        @pl.when(jnp.logical_not(own))
        def _(cp=cp):
            cp.start()

        @pl.when(own)
        def _():
            kv_all[which, main] = kv_mine[...]

        wait_main.append((own, cp))
        send(
            kv_mine.at[pl.ds(128, 128)], kv_all.at[which, rim],
            kv_send.at[2 + i], kv_recv.at[which * 2 + 1], (ahead, to),
        )
    loads[1].wait()
    query = jnp.dot(normed[...], query_w[...], preferred_element_type=jnp.float32)
    for i in range(2):
        cols = slice(i * 128, i * 128 + 128)
        queries[:, cols] = turn(query[:, cols], cosine, sine).astype(jnp.bfloat16)
    turn_weights(1)
    for w in range(2):
        v = kv_all.at[w, main]

        @pl.when(fsdp != 15 * w)
        def _(v=v, w=w):
            copy(v, v, kv_send.at[0], kv_recv.at[w * 2], sibling).wait_recv()

        v = kv_all.at[w, rim]
        copy(v, v, kv_send.at[0], kv_recv.at[w * 2 + 1], sibling).wait_recv()
    for own, cp in wait_main:

        @pl.when(jnp.logical_not(own))
        def _(cp=cp):
            cp.wait_send()

    row = lax.broadcasted_iota(jnp.int32, (128, 256), 0)
    col = lax.broadcasted_iota(jnp.int32, (128, 256), 1)
    for b in range(2):
        allowed = (col <= row + 128) & (col > row) & (ctx * 256 + b * 128 - 128 + col >= 0)
        keys = kv_all[0, b * 128 : b * 128 + 256]
        values = kv_all[1, b * 128 : b * 128 + 256]
        for h in range(4):
            q = queries[b * 128 : b * 128 + 128, h * 64 : h * 64 + 64]
            score = lax.dot_general(q, keys, nt, preferred_element_type=jnp.float32) * 0.125
            score = jnp.where(allowed, score, -1e30)
            sink = sinks[h]
            top = jnp.maximum(jnp.max(score, axis=-1, keepdims=True), sink)
            expd = jnp.exp(score - top)
            total = jnp.exp(sink - top) + jnp.sum(expd, axis=-1, keepdims=True)
            probs = (expd / total).astype(jnp.bfloat16)
            mixed = jnp.dot(probs, values, preferred_element_type=jnp.float32)
            attended[b * 128 : b * 128 + 128, h * 64 : h * 64 + 64] = mixed.astype(jnp.bfloat16)

    loads[2].wait()
    for lo, n in ((0, 1024), (1024, 1024), (2048, 832)):
        got = lax.dot_general(
            attended[...], outw_w[lo : lo + n, :], nt, preferred_element_type=jnp.float32
        ).astype(jnp.bfloat16)
        part[:, :, :, :, lo : lo + n] = got.reshape(2, 4, 2, 16, n)

    def piece(by, half=None):
        cols = slice(None) if half is None else halves_of[half]
        return part.at[:, shifted[2][by % 4], core, :, cols]

    def landed(slot, half):
        return part_in.at[slot, :, :, halves_of[half]]

    def from_sibling(by):
        return part_sib.at[:, shifted[2][by % 4]]

    def tr_wait(k, v):
        copy(v, v, tr_send.at[k], tr_recv.at[k], sibling).wait_recv()

    def plus(dst, *others):
        for i in range(2):
            total = dst[i].astype(jnp.float32)
            for o in others:
                total = total + o[i].astype(jnp.float32)
            dst[i] = total.astype(jnp.bfloat16)

    for k, by in enumerate((2, 1, -1, 0)):
        send(
            part.at[:, shifted[2][by % 4], 1 - core], from_sibling(by),
            tr_send.at[k], tr_recv.at[k], sibling,
        )
    turn_weights(1)
    tr_wait(0, from_sibling(2))
    plus(piece(2), from_sibling(2))
    send(piece(2, 0), landed(2, 0), tr_send.at[4], tr_recv.at[4], right)
    send(piece(2, 1), landed(2, 1), tr_send.at[5], tr_recv.at[5], left)
    tr_wait(1, from_sibling(1))
    plus(piece(1), from_sibling(1))
    send(piece(1, 1), landed(0, 1), tr_send.at[6], tr_recv.at[6], right)
    tr_wait(2, from_sibling(-1))
    plus(piece(-1), from_sibling(-1))
    send(piece(-1, 0), landed(1, 0), tr_send.at[7], tr_recv.at[7], left)
    turn_weights(2)
    tr_wait(4, landed(2, 0))
    plus(piece(1, 0), landed(2, 0))
    send(piece(1, 0), landed(0, 0), tr_send.at[8], tr_recv.at[8], right)
    tr_wait(5, landed(2, 1))
    plus(piece(-1, 1), landed(2, 1))
    send(piece(-1, 1), landed(1, 1), tr_send.at[9], tr_recv.at[9], left)
    tr_wait(3, from_sibling(0))
    plus(piece(0), from_sibling(0))
    turn_weights(2)
    tr_wait(6, landed(0, 1))
    tr_wait(7, landed(1, 0))
    tr_wait(8, landed(0, 0))
    tr_wait(9, landed(1, 1))
    plus(piece(0), part_in.at[0], part_in.at[1])
    send(part.at[1 - yh, me[2], core], part_last, tr_send.at[10], tr_recv.at[10], across)
    turn_weights(12)
    tr_wait(10, part_last)
    total = part[yh, me[2], core].astype(jnp.float32) + part_last[...].astype(jnp.float32)
    resid[:, 2816:2944] = jnp.zeros((16, 128), jnp.float32)
    resid[:, 0:2880] = tokens[...].astype(jnp.float32) + total
    v = resid[...]
    scale = lax.rsqrt(jnp.sum(v * v, axis=-1, keepdims=True) * (1.0 / 2880.0) + 1e-05)
    gain_pad[...] = jnp.zeros((1, 2944), jnp.float32)
    gain_pad[:, 0:2880] = mlp_gain[...].reshape(1, 2880)
    v = v * scale * gain_pad[...]
    high = fixed[...] // 256
    low = fixed[...] - high * 256
    meta = jnp.concatenate([routes[...], high, low, jnp.zeros((4, 16), jnp.int32)], axis=0)
    meta = meta.astype(jnp.float32).T.astype(jnp.bfloat16)
    spot = lax.broadcasted_iota(jnp.int32, (16, 128), 0) + 64 == lax.broadcasted_iota(jnp.int32, (16, 128), 1)
    meta = jnp.dot(meta, jnp.where(spot, 1.0, 0.0).astype(jnp.bfloat16), preferred_element_type=jnp.float32)
    for p, (lo, n, wide) in enumerate(PARTS):
        w = v[:, lo : lo + wide]
        if p == 2:
            w = jnp.concatenate([w[:, :768], w[:, 768:] + meta], axis=1)
        xs[p][me[0], me[1], me[2], core] = w.astype(jnp.bfloat16)
    v = gathered.at[:, :, core]
    copy(v, v, ta_send.at[1], ta_recv.at[8], sibling).wait_send()
    for v in (gathered.at[yh, :, core], gathered.at[yh, pl.ds(0, 3), core]):
        copy(v, v, ta_send.at[0], ta_recv.at[8], sibling).wait_send()
    for cp in started:
        cp.wait_send()

    ALL = "all"

    def where_(p, offsets, drop=()):
        idx = [None] * 3
        for s, o in enumerate(offsets):
            a = ORDERS[p][s]
            idx[a] = slice(None) if o is ALL else shifted[a][o % 4]
        return tuple(idx[a] for a in range(3) if a not in [ORDERS[p][s] for s in drop])

    def cols_of(p, half):
        if half is None:
            return pl.ds(0, PARTS[p][2])
        return (pl.ds(0, HALF), pl.ds(HALF, PARTS[p][2] - HALF))[half]

    def mine(p, offsets, half=None, which=None):
        which = core if which is None else which
        return xs[p].at[where_(p, offsets) + (which, slice(None), cols_of(p, half))]

    def ways(p, s):
        return neighbour(ORDERS[p][s], 1), neighbour(ORDERS[p][s], -1)

    def ag(p, k, v, to):
        copy(v, v, ag_send.at[p], ag_recv.at[p, k], to).start()

    def ag_wait(p, k, v):
        copy(v, v, ag_send.at[p], ag_recv.at[p, k], sibling).wait_recv()

    def forward(p, offsets):
        v = mine(p, offsets)
        copy(v, v, sib_send.at[p], sib_recv.at[p], sibling).start()

    def wait_sent(p, sem):
        some = pl.ds(0, 3)
        for idx in ((some,), (0, some), (0, 0, some)):
            v = xs[p].at[idx + (slice(None),) * (3 - len(idx)) + (core,)]
            copy(v, v, sem, ag_recv.at[p, 0], sibling).wait_send()

    def third(p, j):
        up, dn = ways(p, 2)
        k = 9 + (j % 4) * 4
        ag(p, k, mine(p, (ALL, j, 0)), up)
        ag(p, k + 1, mine(p, (ALL, j, 0)), dn)

    def third_relay(p, j):
        up, dn = ways(p, 2)
        k = 9 + (j % 4) * 4
        ag_wait(p, k, mine(p, (ALL, j, -1)))
        ag(p, k + 2, mine(p, (ALL, j, -1), 0), up)
        ag_wait(p, k + 1, mine(p, (ALL, j, 1)))
        ag(p, k + 3, mine(p, (ALL, j, 1), 1), dn)
        forward(p, (ALL, j, -1))
        forward(p, (ALL, j, 1))

    def third_end(p, j):
        k = 9 + (j % 4) * 4
        ag_wait(p, k + 2, mine(p, (ALL, j, 2), 0))
        ag_wait(p, k + 3, mine(p, (ALL, j, 2), 1))
        forward(p, (ALL, j, 2))

    for p in range(3):
        own = mine(p, (0, 0, 0))
        up, dn = ways(p, 0)
        ag(p, 0, own, up)
        ag(p, 1, own, dn)
        ag(p, 2, own, neighbour(ORDERS[p][0], 2))
    for p in range(3):
        ag_wait(p, 0, mine(p, (-1, 0, 0)))
        ag_wait(p, 1, mine(p, (1, 0, 0)))
        ag_wait(p, 2, mine(p, (2, 0, 0)))
        up, dn = ways(p, 1)
        ag(p, 3, mine(p, (ALL, 0, 0), 0), up)
        ag(p, 4, mine(p, (ALL, 0, 0), 1), dn)
        ag(p, 5, mine(p, (ALL, 0, 0), 1), up)
        ag(p, 6, mine(p, (ALL, 0, 0), 0), dn)
        third(p, 0)
        forward(p, (ALL, 0, 0))
    for p in range(3):
        up, dn = ways(p, 1)
        ag_wait(p, 3, mine(p, (ALL, -1, 0), 0))
        ag(p, 7, mine(p, (ALL, -1, 0), 0), up)
        ag_wait(p, 4, mine(p, (ALL, 1, 0), 1))
        ag(p, 8, mine(p, (ALL, 1, 0), 1), dn)
    for p in range(3):
        ag_wait(p, 5, mine(p, (ALL, -1, 0), 1))
        third(p, -1)
        ag_wait(p, 6, mine(p, (ALL, 1, 0), 0))
        third(p, 1)
        forward(p, (ALL, -1, 0))
        forward(p, (ALL, 1, 0))
    for p in range(3):
        third_relay(p, 0)
    for p in range(3):
        ag_wait(p, 7, mine(p, (ALL, 2, 0), 0))
        ag_wait(p, 8, mine(p, (ALL, 2, 0), 1))
        third(p, 2)
        forward(p, (ALL, 2, 0))
    for p in range(3):
        third_end(p, 0)
        third_relay(p, -1)
    for p in range(3):
        third_relay(p, 1)
        third_end(p, -1)
    for p in range(3):
        third_relay(p, 2)
        third_end(p, 1)
    for p in range(3):
        third_end(p, 2)
    for p in range(3):
        v = mine(p, (ALL, ALL, ALL), None, 1 - core)
        copy(v, v, sib_send.at[p], sib_recv.at[p], sibling).wait_recv()

    first_expert = fsdp * 4
    lane = lax.broadcasted_iota(jnp.int32, (256, 128), 1)
    row = lax.broadcasted_iota(jnp.int32, (256, 128), 0)
    lane_expert = (first_expert + lane // 32).astype(jnp.float32)
    lane_slot = ((lane % 32) // 16).astype(jnp.float32)
    same_source = row // 16 == lane % 16

    def dispatch(g, _):
        z, yh = g // 2, g % 2

        def rows(p):
            return xs[p][z, pl.ds(yh * 2, 2)].reshape(256, PARTS[p][2])

        last = rows(2)
        ids = last[:, 768:896].astype(jnp.float32)
        hit = jnp.zeros((256, 128), jnp.float32)
        for k in range(4):
            hit = hit + jnp.where(ids[:, 64 + k : 65 + k] == lane_expert, 1.0, 0.0)
        rank = jnp.dot(lower[...], hit.astype(jnp.bfloat16), preferred_element_type=jnp.float32)
        t = jnp.where((rank == lane_slot) & same_source, hit, 0.0)
        table[g] = t.astype(jnp.bfloat16)
        pick = t.T.astype(jnp.bfloat16)
        for p in range(3):
            src = last if p == 2 else rows(p)
            got = jnp.dot(pick, src, preferred_element_type=jnp.float32).astype(jnp.bfloat16)
            for e in range(4):
                ds[p][e, pl.ds(g * 32, 32), :] = got[e * 32 : (e + 1) * 32]
        return 0

    lax.fori_loop(0, GROUPS, dispatch, 0)

    def expert(e, _):
        gate = jnp.zeros((256, 192), jnp.float32)
        upv = jnp.zeros((256, 192), jnp.float32)
        for p, (lo, n, held) in enumerate(PARTS):
            y = ds[p][e, :, 0:n]
            gate = gate + lax.dot_general(y, gate_w[e, :, lo : lo + n], nt, preferred_element_type=jnp.float32)
            upv = upv + lax.dot_general(y, up_w[e, :, lo : lo + n], nt, preferred_element_type=jnp.float32)
        about = ds[2][e, :, 768:896].astype(jnp.float32)
        weight = jnp.zeros((256, 1), jnp.float32)
        number = (first_expert + e).astype(jnp.float32)
        for k in range(4):
            value = about[:, 68 + k : 69 + k] * 256.0 + about[:, 72 + k : 73 + k]
            weight = weight + jnp.where(about[:, 64 + k : 65 + k] == number, value, 0.0)
        hidden = gate * jax.nn.sigmoid(GLU * gate) * (upv + 1.0)
        hidden_all[e] = (hidden * (weight * (1.0 / 65536.0))).astype(jnp.bfloat16)
        return 0

    lax.fori_loop(0, 4, expert, 0)

    turns = (2, 1, -1, 0)

    def other(p, offsets):
        return ss[p].at[where_(p, offsets)]

    def land3(p, slot, j, half=None):
        return rbufs[p][2].at[(slot,) + where_(p, (ALL, j, 0), (2,)) + (slice(None), cols_of(p, half))]

    def land2(p, slot, half=None):
        return rbufs[p][1].at[slot, :, :, cols_of(p, half)]

    def rs(p, k, src, dst, to):
        copy(src, dst, rs_send.at[p], rs_recv.at[p, k], to).start()

    def rs_wait(p, k, dst):
        copy(dst, dst, rs_send.at[p], rs_recv.at[p, k], sibling).wait_recv()

    def add(dst, *others):
        for i in range(4):
            total = dst[i]
            for o in others:
                total = total + o[i]
            dst[i] = total

    def half_of(ref, p, half):
        return ref.at[:, :, cols_of(p, half)]

    def first(p, j):
        v = other(p, (ALL, j, ALL))
        copy(v, v, sx_send.at[p], sx_recv.at[p, j % 4], sibling).wait_recv()
        up, dn = ways(p, 2)
        k = 9 + (j % 4) * 4
        add(mine(p, (ALL, j, 2)), other(p, (ALL, j, 2)))
        rs(p, k, mine(p, (ALL, j, 2), 0), land3(p, 2, j, 0), up)
        rs(p, k + 1, mine(p, (ALL, j, 2), 1), land3(p, 2, j, 1), dn)

    def mid(p, j):
        up, dn = ways(p, 2)
        k = 9 + (j % 4) * 4
        add(mine(p, (ALL, j, 1), 1), half_of(other(p, (ALL, j, 1)), p, 1))
        add(mine(p, (ALL, j, -1), 0), half_of(other(p, (ALL, j, -1)), p, 0))
        rs_wait(p, k, land3(p, 2, j, 0))
        add(mine(p, (ALL, j, 1), 0), half_of(other(p, (ALL, j, 1)), p, 0), land3(p, 2, j, 0))
        rs(p, k + 2, mine(p, (ALL, j, 1)), land3(p, 0, j), up)
        rs_wait(p, k + 1, land3(p, 2, j, 1))
        add(mine(p, (ALL, j, -1), 1), half_of(other(p, (ALL, j, -1)), p, 1), land3(p, 2, j, 1))
        rs(p, k + 3, mine(p, (ALL, j, -1)), land3(p, 1, j), dn)

    def last(p, j):
        k = 9 + (j % 4) * 4
        rs_wait(p, k + 2, land3(p, 0, j))
        rs_wait(p, k + 3, land3(p, 1, j))
        add(mine(p, (ALL, j, 0)), other(p, (ALL, j, 0)), land3(p, 0, j), land3(p, 1, j))
        up, dn = ways(p, 1)
        if j == 2:
            rs(p, 3, mine(p, (ALL, 2, 0), 0), land2(p, 2, 0), up)
            rs(p, 4, mine(p, (ALL, 2, 0), 1), land2(p, 2, 1), dn)
        if j == 1:
            rs(p, 5, mine(p, (ALL, 1, 0), 1), land2(p, 0, 1), up)
        if j == -1:
            rs(p, 6, mine(p, (ALL, -1, 0), 0), land2(p, 1, 0), dn)

    def second(p):
        up, dn = ways(p, 1)
        rs_wait(p, 3, land2(p, 2, 0))
        add(mine(p, (ALL, 1, 0), 0), land2(p, 2, 0))
        rs(p, 7, mine(p, (ALL, 1, 0), 0), land2(p, 0, 0), up)
        rs_wait(p, 4, land2(p, 2, 1))
        add(mine(p, (ALL, -1, 0), 1), land2(p, 2, 1))
        rs(p, 8, mine(p, (ALL, -1, 0), 1), land2(p, 1, 1), dn)

    def second_end(p):
        rs_wait(p, 5, land2(p, 0, 1))
        rs_wait(p, 6, land2(p, 1, 0))
        rs_wait(p, 7, land2(p, 0, 0))
        rs_wait(p, 8, land2(p, 1, 1))
        add(mine(p, (ALL, 0, 0)), land2(p, 0), land2(p, 1))
        up, dn = ways(p, 0)
        rs(p, 0, mine(p, (1, 0, 0)), rbufs[p][0].at[0], up)
        rs(p, 1, mine(p, (-1, 0, 0)), rbufs[p][0].at[1], dn)
        rs(p, 2, mine(p, (2, 0, 0)), rbufs[p][0].at[2], neighbour(ORDERS[p][0], 2))

    def produce(p):
        lo, n, wide = PARTS[p]
        wait_sent(p, ag_send.at[p])
        v = mine(p, (ALL, ALL, ALL))
        copy(v, v, sib_send.at[p], sib_recv.at[p], sibling).wait_send()

        def down(e, _):
            ds[p][e, :, 0:n] = jnp.dot(
                hidden_all[e], down_w[e, :, lo : lo + n], preferred_element_type=jnp.float32
            ).astype(jnp.bfloat16)
            return 0

        lax.fori_loop(0, 4, down, 0)

        def combine(g, _):
            z, yh_ = g // 2, g % 2
            y = jnp.concatenate([ds[p][e, pl.ds(g * 32, 32), :] for e in range(4)], axis=0)
            got = jnp.dot(table[g], y, preferred_element_type=jnp.float32).astype(jnp.bfloat16)
            xs[p][z, pl.ds(yh_ * 2, 2)] = got.reshape(2, 4, 2, 16, wide)
            return 0

        lax.fori_loop(0, GROUPS, combine, 0)
        for j in turns:
            copy(
                mine(p, (ALL, j, ALL), None, 1 - core), other(p, (ALL, j, ALL)),
                sx_send.at[p], sx_recv.at[p, j % 4], sibling,
            ).start()

    produce(0)
    produce(1)
    first(0, 2)
    first(0, 1)
    produce(2)
    first(1, 2)
    first(1, 1)
    first(0, -1)
    first(0, 0)
    mid(0, 2)
    first(2, 2)
    first(2, 1)
    mid(1, 2)
    first(1, -1)
    first(1, 0)
    mid(0, 1)
    mid(2, 2)
    first(2, -1)
    first(2, 0)
    mid(1, 1)
    mid(2, 1)
    for p in range(3):
        last(p, 2)
        mid(p, -1)
    for p in range(3):
        last(p, 1)
        mid(p, 0)
    for p in range(3):
        last(p, -1)
        second(p)
    for p in range(3):
        last(p, 0)
    for p in range(3):
        second_end(p)
    for p, (lo, n, wide) in enumerate(PARTS):
        total = mine(p, (0, 0, 0))[...].astype(jnp.float32)
        for s in range(3):
            rs_wait(p, s, rbufs[p][0].at[s])
            total = total + rbufs[p][0][s].astype(jnp.float32)
        out[:, lo : lo + n] = (resid[:, lo : lo + n] + total[:, :n]).astype(jnp.bfloat16)
    for p in range(3):
        wait_sent(p, rs_send.at[p])
        v = other(p, (ALL, ALL, ALL))
        copy(v, v, sx_send.at[p], sx_recv.at[p, 0], sibling).wait_send()


def layer(tokens, attn_gain, mlp_gain, sinks, routes, fixed, weights):
    bf = jnp.bfloat16
    wide = [p[2] for p in PARTS]
    width = tokens.shape[1]
    dma = pltpu.SemaphoreType.DMA
    scratch = (
        [pltpu.VMEM((4, 4, 4, 2, 16, h), bf) for h in wide]
        + [pltpu.VMEM((4, 256, h), bf) for h in wide]
        + [pltpu.VMEM((4, 4, 4, 16, h), bf) for h in wide]
        + [pltpu.VMEM((4, 192, width), bf)] * 3
        + [
            pltpu.VMEM((2, 48, 4, width), bf),
            pltpu.VMEM((4, 256, 192), bf),
            pltpu.VMEM((1, 2944), jnp.float32),
        ]
        + [pltpu.VMEM((GROUPS, 256, 128), bf), pltpu.VMEM((256, 256), bf)]
        + [pltpu.VMEM((3,) + (4,) * s + (16, h), bf) for h in wide for s in range(3)]
        + [pltpu.VMEM(w.shape, bf) for w in (weights[0], weights[1], weights[2])]
        + [
            pltpu.VMEM((2, 4, 2, 16, width), bf),
            pltpu.VMEM((256, width), bf),
            pltpu.VMEM((256, 64), bf),
            pltpu.VMEM((2, 384, 64), bf),
            pltpu.VMEM((256, 256), bf),
            pltpu.VMEM((256, 256), bf),
            pltpu.VMEM((2, 4, 2, 16, width), bf),
            pltpu.VMEM((2, 4, 16, width), bf),
            pltpu.VMEM((3, 2, 16, width), bf),
            pltpu.VMEM((16, width), bf),
            pltpu.VMEM((16, 2944), jnp.float32),
        ]
        + [
            dma((5,)), dma((3,)), dma((3, 25)), dma((3,)), dma((3,)),
            dma((3,)), dma((3, 25)), dma((3,)), dma((3, 4)),
            dma((2,)), dma((9,)), dma((4,)), dma((4,)), dma((11,)), dma((11,)),
        ]
    )
    vm = pl.BlockSpec(memory_space=pltpu.VMEM)
    sm = pl.BlockSpec(memory_space=pltpu.SMEM)
    anym = pl.BlockSpec(memory_space=pl.ANY)
    return pl.pallas_call(
        layer_kernel,
        out_shape=jax.ShapeDtypeStruct(tokens.shape, bf),
        in_specs=[vm] * 3 + [sm] + [vm] * 2 + [anym] * 6,
        out_specs=vm,
        scratch_shapes=scratch,
        compiler_params=pltpu.CompilerParams(
            collective_id=1, has_side_effects=True, vmem_limit_bytes=62 * 1024 * 1024
        ),
        name="layer",
    )(tokens, attn_gain, mlp_gain, sinks, routes, fixed, *weights)


def shards(
    tokens, attn_gain, query_weight, keyval_weight, sink_logits, out_weight,
    mlp_gain, routes, gate_fixed, gate_weight, up_weight, down_weight,
):
    experts = [jnp.transpose(w, (1, 0, 2)) for w in (gate_weight, up_weight, down_weight)]
    weights = (query_weight, keyval_weight, out_weight.T, *experts)
    return layer(tokens, attn_gain, mlp_gain, sink_logits, routes.T, gate_fixed.T, weights)


def solution(mesh):
    in_specs = (
        P(("ctx", "fsdp"), None),
        P(),
        P(None, "fsdp"),
        P("fsdp", None),
        P("fsdp"),
        P("fsdp", None),
        P(),
        P(("ctx", "fsdp"), None),
        P(("ctx", "fsdp"), None),
        P("fsdp", "ctx", None),
        P("fsdp", "ctx", None),
        P("fsdp", "ctx", None),
    )
    out_specs = P(("ctx", "fsdp"), None)
    return jax.shard_map(shards, mesh=mesh, in_specs=in_specs, out_specs=out_specs, check_vma=False)
```

```python
import math
import jax
import jax.numpy as jnp
from jax import lax
from jax.experimental import pallas as pl
from jax.experimental.pallas import tpu as pltpu
from jax.sharding import PartitionSpec as P

PARTS = ((0, 1024, 1024), (1024, 1024, 1024), (2048, 832, 896))
ORDERS = ((0, 1, 2), (1, 2, 0), (2, 0, 1))
HALF = 512
GROUPS = 8
GLU = 1.702


def layer_kernel(
    tokens, attn_gain, mlp_gain, sinks, routes, fixed,
    query_hbm, keyval_hbm, outw_hbm, gate_hbm, up_hbm, down_hbm, out,
    x0, x1, x2, d0, d1, d2, s0, s1, s2,
    gate_w, up_w, down_w, stage, hidden_all, gain_pad, table, picks, slot_weight, metas, lower,
    ra0, ra1, ra2, rb0, rb1, rb2, rc0, rc1, rc2,
    query_w, keyval_w, outw_w, gathered, normed, kv_mine, kv_all, queries, attended,
    part, part_sib, part_in, part_last, resid,
    wsem, ag_send, ag_recv, sib_send, sib_recv,
    rs_send, rs_recv, sx_send, sx_recv,
    mt_send, mt_recv, ta_send, ta_recv, kv_send, kv_recv, tr_send, tr_recv,
):
    xs, ds, ss = (x0, x1, x2), (d0, d1, d2), (s0, s1, s2)
    rbufs = ((ra0, ra1, ra2), (rb0, rb1, rb2), (rc0, rc1, rc2))
    ctx = lax.axis_index("ctx")
    fsdp = lax.axis_index("fsdp")
    core = lax.rem(fsdp, 2)
    me = (lax.div(ctx, 2), lax.div(fsdp, 8) * 2 + lax.rem(ctx, 2), lax.rem(lax.div(fsdp, 2), 4))
    shifted = [[me[a]] + [lax.rem(me[a] + by, 4) for by in (1, 2, 3)] for a in range(3)]

    def device(z, y, x, c):
        return (z * 2 + lax.rem(y, 2), (lax.div(y, 2) * 4 + x) * 2 + c)

    def neighbour(axis, by):
        at = list(me)
        at[axis] = shifted[axis][by % 4]
        return device(*at, core)

    sibling = device(*me, 1 - core)

    def copy(src, dst, ss_, rs_, to):
        return pltpu.make_async_remote_copy(
            src_ref=src, dst_ref=dst, send_sem=ss_, recv_sem=rs_,
            device_id=to, device_id_type=pl.DeviceIdType.MESH,
        )

    loads = [
        pltpu.make_async_copy(h, v, wsem.at[i])
        for i, (h, v) in enumerate(((keyval_hbm, keyval_w), (query_hbm, query_w), (outw_hbm, outw_w)))
    ]
    for w in loads:
        w.start()

    def chunk(i):
        src = (gate_hbm, up_hbm, down_hbm)[i // 4]
        n = 36 if i % 4 == 3 else 48
        return pltpu.make_async_copy(
            src.at[pl.ds((i % 4) * 48, n)], stage.at[i % 2, pl.ds(0, n)], wsem.at[3 + i % 2]
        )

    turned = [0]

    def turn_weights(count):
        for i in range(turned[0], min(turned[0] + count, 12)):
            chunk(i).wait()
            dst = (gate_w, up_w, down_w)[i // 4]
            rows = pl.ds((i % 4) * 48, 48)
            if i % 4 == 3:
                stage[i % 2, 36:48] = jnp.zeros((12, 4, 2880), jnp.bfloat16)

            def tile(t, _):
                cols = pl.ds(pl.multiple_of(t * 256, 256), 256)
                dst[:, rows, cols] = jnp.swapaxes(stage[i % 2, :, :, cols], 0, 1)
                return 0

            lax.fori_loop(0, 11, tile, 0)
            dst[:, rows, 2816:2880] = jnp.swapaxes(stage[i % 2, :, :, 2816:2880], 0, 1)
            if i + 2 < 12:
                chunk(i + 2).start()
            turned[0] = i + 1

    chunk(0).start()
    chunk(1).start()

    def signal(to):
        pl.semaphore_signal(barrier, inc=1, device_id=to, device_id_type=pl.DeviceIdType.MESH)

    barrier = pltpu.get_barrier_semaphore()
    across = neighbour(1, 2)
    diagonal = [device(me[0], shifted[1][2], shifted[2][by % 4], core) for by in range(4)]
    partners = [neighbour(a, b) for a in range(3) for b in (1, -1, 2)] + [sibling] + diagonal[1:]
    for to in partners:
        signal(to)
    behind = (ctx + 7) % 8
    ahead = (ctx + 1) % 8
    key_from, value_from = fsdp // 2, 8 + fsdp // 2
    signal((behind, key_from))
    signal((behind, value_from))

    @pl.when(fsdp != 0)
    def _():
        signal((ctx, key_from))

    @pl.when(fsdp != 15)
    def _():
        signal((ctx, value_from))

    yh = lax.div(me[1], 2)
    ys = (yh, 1 - yh)
    gathered[yh, me[2], core] = tokens[...]
    high = fixed[...] // 256
    low = fixed[...] - high * 256
    about = jnp.concatenate([routes[...], high, low, jnp.zeros((4, 16), jnp.int32)], axis=0)
    about = about.astype(jnp.float32).T.astype(jnp.bfloat16)
    spot = lax.broadcasted_iota(jnp.int32, (16, 128), 0) == lax.broadcasted_iota(jnp.int32, (16, 128), 1)
    about = jnp.dot(about, jnp.where(spot, 1.0, 0.0).astype(jnp.bfloat16), preferred_element_type=jnp.float32)
    metas[me[0], me[1], me[2], core] = about.astype(jnp.bfloat16)

    r = lax.broadcasted_iota(jnp.int32, (256, 256), 0)
    c = lax.broadcasted_iota(jnp.int32, (256, 256), 1)
    lower[...] = jnp.where((r // 16 == c // 16) & (c < r), 1.0, 0.0).astype(jnp.bfloat16)
    alone = jnp.where((fsdp == 0) | (fsdp == 15), 1, 0)
    pl.semaphore_wait(barrier, len(partners) + 4 - alone)

    started = []

    def send(src, dst, send_sem, recv_sem, to):
        cp = copy(src, dst, send_sem, recv_sem, to)
        cp.start()
        started.append(cp)

    left, right = neighbour(2, -1), neighbour(2, 1)
    halves_of = (pl.ds(0, 1408), pl.ds(1408, 1472))

    def held(b, by, which):
        return gathered.at[ys[b], shifted[2][by % 4], which]

    def norm_block(b, by, which):
        y_, x_ = ys[b], shifted[2][by % 4]
        v = gathered[y_, x_, which].astype(jnp.float32)
        scale = lax.rsqrt(jnp.sum(v * v, axis=-1, keepdims=True) * (1.0 / 2880.0) + 1e-05)
        row = ((y_ * 4 + x_) * 2 + which) * 16
        normed[pl.ds(pl.multiple_of(row, 16), 16), :] = (v * scale * attn_gain[...].reshape(1, 2880)).astype(jnp.bfloat16)

    lanes = lax.broadcasted_iota(jnp.int32, (256, 128), 1)
    early = lanes % 64 < 32
    freqs = jnp.exp((lanes % 32).astype(jnp.float32) * (-2.0 / 64 * math.log(150000.0)))
    angles = (ctx * 256 + lax.broadcasted_iota(jnp.int32, (256, 128), 0)).astype(jnp.float32) * freqs

    def meta_view(stage, by):
        idx = tuple(slice(None) if a < stage else (shifted[a][by % 4] if a == stage else me[a]) for a in range(3))
        return metas.at[idx + (core,)]

    def meta_send(stage):
        v = meta_view(stage, 0)
        for by in (2, 1, -1):
            copy(v, v, mt_send.at[0], mt_recv.at[stage * 4 + by % 4], neighbour(stage, by)).start()

    def meta_wait(stage):
        for by in (2, 1, -1):
            v = meta_view(stage, by)
            copy(v, v, mt_send.at[0], mt_recv.at[stage * 4 + -by % 4], sibling).wait_recv()

    mates = ((1, 2), (1, 1), (1, -1), (0, 2), (1, 0), (0, 1), (0, -1))
    own = held(0, 0, core)
    for b, by in mates:
        to = diagonal[by % 4] if b else neighbour(2, by)
        copy(own, own, ta_send.at[0], ta_recv.at[b * 4 + by % 4], to).start()
    copy(own, own, ta_send.at[1], ta_recv.at[8], sibling).start()
    meta_send(0)
    norm_block(0, 0, core)
    cosine = jnp.cos(angles)
    sine = jnp.sin(angles)
    sine = jnp.where(early, -sine, sine)
    turn_weights(6)
    for b, by in ((0, -1), (0, 1), (1, 0), (0, 2), (1, -1), (1, 1), (1, 2)):
        v = held(b, by, core)
        copy(v, v, ta_send.at[0], ta_recv.at[b * 4 + -by % 4], sibling).wait_recv()
        copy(v, v, ta_send.at[1], ta_recv.at[8], sibling).start()
        norm_block(b, by, core)
    meta_wait(0)
    meta_send(1)
    v = gathered.at[:, :, 1 - core]
    copy(v, v, ta_send.at[1], ta_recv.at[8], sibling).wait_recv()
    for b in range(2):
        for by in range(4):
            norm_block(b, by, 1 - core)

    nt = (((1,), (1,)), ((), ()))

    def turn(v, c_, s_):
        return v * c_ + jnp.where(early, pltpu.roll(v, 96, 1), pltpu.roll(v, 32, 1)) * s_

    loads[0].wait()
    kv = lax.dot_general(normed[...], keyval_w[...], nt, preferred_element_type=jnp.float32)
    kv = jnp.concatenate([kv, kv], axis=1)
    kv = jnp.where(fsdp < 8, turn(kv, cosine, sine), kv)
    kv_mine[...] = kv[:, :64].astype(jnp.bfloat16)
    which = fsdp // 8
    main, rim = pl.ds(128, 256), pl.ds(0, 128)
    wait_main = []
    for i in range(2):
        to = 2 * (fsdp % 8) + i
        cp = copy(kv_mine, kv_all.at[which, main], kv_send.at[i], kv_recv.at[which * 2], (ctx, to))
        own = fsdp == 15 * i

        @pl.when(jnp.logical_not(own))
        def _(cp=cp):
            cp.start()

        @pl.when(own)
        def _():
            kv_all[which, main] = kv_mine[...]

        wait_main.append((own, cp))
        send(
            kv_mine.at[pl.ds(128, 128)], kv_all.at[which, rim],
            kv_send.at[2 + i], kv_recv.at[which * 2 + 1], (ahead, to),
        )
    meta_wait(1)
    meta_send(2)
    loads[1].wait()
    query = jnp.dot(normed[...], query_w[...], preferred_element_type=jnp.float32)
    for i in range(2):
        cols = slice(i * 128, i * 128 + 128)
        queries[:, cols] = turn(query[:, cols], cosine, sine).astype(jnp.bfloat16)
    turn_weights(1)
    for w in range(2):
        v = kv_all.at[w, main]

        @pl.when(fsdp != 15 * w)
        def _(v=v, w=w):
            copy(v, v, kv_send.at[0], kv_recv.at[w * 2], sibling).wait_recv()

        v = kv_all.at[w, rim]
        copy(v, v, kv_send.at[0], kv_recv.at[w * 2 + 1], sibling).wait_recv()
    for own, cp in wait_main:

        @pl.when(jnp.logical_not(own))
        def _(cp=cp):
            cp.wait_send()

    row = lax.broadcasted_iota(jnp.int32, (128, 256), 0)
    col = lax.broadcasted_iota(jnp.int32, (128, 256), 1)
    for b in range(2):
        allowed = (col <= row + 128) & (col > row) & (ctx * 256 + b * 128 - 128 + col >= 0)
        keys = kv_all[0, b * 128 : b * 128 + 256]
        values = kv_all[1, b * 128 : b * 128 + 256]
        for h in range(4):
            q = queries[b * 128 : b * 128 + 128, h * 64 : h * 64 + 64]
            score = lax.dot_general(q, keys, nt, preferred_element_type=jnp.float32) * 0.125
            score = jnp.where(allowed, score, -1e30)
            sink = sinks[h]
            top = jnp.maximum(jnp.max(score, axis=-1, keepdims=True), sink)
            expd = jnp.exp(score - top)
            total = jnp.exp(sink - top) + jnp.sum(expd, axis=-1, keepdims=True)
            probs = (expd / total).astype(jnp.bfloat16)
            mixed = jnp.dot(probs, values, preferred_element_type=jnp.float32)
            attended[b * 128 : b * 128 + 128, h * 64 : h * 64 + 64] = mixed.astype(jnp.bfloat16)

    meta_wait(2)
    v = metas.at[:, :, :, core]
    copy(v, v, mt_send.at[1], mt_recv.at[12], sibling).start()
    loads[2].wait()
    for lo, n in ((0, 1024), (1024, 1024), (2048, 832)):
        got = lax.dot_general(
            attended[...], outw_w[lo : lo + n, :], nt, preferred_element_type=jnp.float32
        ).astype(jnp.bfloat16)
        part[:, :, :, :, lo : lo + n] = got.reshape(2, 4, 2, 16, n)

    def octant(zh, yh_, xh):
        return pl.ds(zh * 2, 2), pl.ds(yh_ * 2, 2), pl.ds(xh * 2, 2)

    first_expert = fsdp * 4
    lane = lax.broadcasted_iota(jnp.int32, (256, 128), 1)
    row = lax.broadcasted_iota(jnp.int32, (256, 128), 0)
    lane_expert = (first_expert + lane // 32).astype(jnp.float32)
    lane_slot = ((lane % 32) // 16).astype(jnp.float32)
    same_source = row // 16 == lane % 16
    slot_expert = (first_expert + row[:128] // 32).astype(jnp.float32)

    def tables(lo, hi):
        def one(o, _):
            known = metas[octant(o // 4, (o // 2) % 2, o % 2)].reshape(256, 128)
            ids = known.astype(jnp.float32)
            hit = jnp.zeros((256, 128), jnp.float32)
            for k in range(4):
                hit = hit + jnp.where(ids[:, k : k + 1] == lane_expert, 1.0, 0.0)
            rank = jnp.dot(lower[...], hit.astype(jnp.bfloat16), preferred_element_type=jnp.float32)
            t = jnp.where((rank == lane_slot) & same_source, hit, 0.0)
            table[o] = t.astype(jnp.bfloat16)
            pick = t.T.astype(jnp.bfloat16)
            picks[o] = pick
            got = jnp.dot(pick, known, preferred_element_type=jnp.float32)
            weight = jnp.zeros((128, 128), jnp.float32)
            for k in range(4):
                value = got[:, 4 + k : 5 + k] * 256.0 + got[:, 8 + k : 9 + k]
                weight = weight + jnp.where(got[:, k : k + 1] == slot_expert, value, 0.0)
            weight = weight * (1.0 / 65536.0)
            at = pl.ds(pl.multiple_of(o * 32, 32), 32)
            for e in range(4):
                slot_weight[e, at, :] = weight[e * 32 : e * 32 + 32]
            return 0

        lax.fori_loop(lo, hi, one, 0)

    def piece(by, half=None):
        cols = slice(None) if half is None else halves_of[half]
        return part.at[:, shifted[2][by % 4], core, :, cols]

    def landed(slot, half):
        return part_in.at[slot, :, :, halves_of[half]]

    def from_sibling(by):
        return part_sib.at[:, shifted[2][by % 4]]

    def tr_wait(k, v):
        copy(v, v, tr_send.at[k], tr_recv.at[k], sibling).wait_recv()

    def plus(dst, *others):
        for i in range(2):
            total = dst[i].astype(jnp.float32)
            for o in others:
                total = total + o[i].astype(jnp.float32)
            dst[i] = total.astype(jnp.bfloat16)

    for k, by in enumerate((2, 1, -1, 0)):
        send(
            part.at[:, shifted[2][by % 4], 1 - core], from_sibling(by),
            tr_send.at[k], tr_recv.at[k], sibling,
        )
    tr_wait(0, from_sibling(2))
    plus(piece(2), from_sibling(2))
    send(piece(2, 0), landed(2, 0), tr_send.at[4], tr_recv.at[4], right)
    send(piece(2, 1), landed(2, 1), tr_send.at[5], tr_recv.at[5], left)
    tr_wait(1, from_sibling(1))
    plus(piece(1), from_sibling(1))
    send(piece(1, 1), landed(0, 1), tr_send.at[6], tr_recv.at[6], right)
    tr_wait(2, from_sibling(-1))
    plus(piece(-1), from_sibling(-1))
    send(piece(-1, 0), landed(1, 0), tr_send.at[7], tr_recv.at[7], left)
    v = metas.at[:, :, :, 1 - core]
    copy(v, v, mt_send.at[1], mt_recv.at[12], sibling).wait_recv()
    tables(0, 5)
    tr_wait(4, landed(2, 0))
    plus(piece(1, 0), landed(2, 0))
    send(piece(1, 0), landed(0, 0), tr_send.at[8], tr_recv.at[8], right)
    tr_wait(5, landed(2, 1))
    plus(piece(-1, 1), landed(2, 1))
    send(piece(-1, 1), landed(1, 1), tr_send.at[9], tr_recv.at[9], left)
    tr_wait(3, from_sibling(0))
    plus(piece(0), from_sibling(0))
    tables(5, 8)
    turn_weights(2)
    tr_wait(6, landed(0, 1))
    tr_wait(7, landed(1, 0))
    tr_wait(8, landed(0, 0))
    tr_wait(9, landed(1, 1))
    plus(piece(0), part_in.at[0], part_in.at[1])
    send(part.at[1 - yh, me[2], core], part_last, tr_send.at[10], tr_recv.at[10], across)
    turn_weights(12)
    tr_wait(10, part_last)
    total = part[yh, me[2], core].astype(jnp.float32) + part_last[...].astype(jnp.float32)
    resid[:, 2816:2944] = jnp.zeros((16, 128), jnp.float32)
    resid[:, 0:2880] = tokens[...].astype(jnp.float32) + total
    v = resid[...]
    scale = lax.rsqrt(jnp.sum(v * v, axis=-1, keepdims=True) * (1.0 / 2880.0) + 1e-05)
    gain_pad[...] = jnp.zeros((1, 2944), jnp.float32)
    gain_pad[:, 0:2880] = mlp_gain[...].reshape(1, 2880)
    v = v * scale * gain_pad[...]
    for p, (lo, n, wide) in enumerate(PARTS):
        w = v[:, lo : lo + wide]
        xs[p][me[0], me[1], me[2], core] = w.astype(jnp.bfloat16)
    v = gathered.at[:, :, core]
    copy(v, v, ta_send.at[1], ta_recv.at[8], sibling).wait_send()
    for v in (gathered.at[yh, :, core], gathered.at[yh, pl.ds(0, 3), core]):
        copy(v, v, ta_send.at[0], ta_recv.at[8], sibling).wait_send()
    for v in (metas.at[pl.ds(0, 3), :, :, core], metas.at[0, pl.ds(0, 3), :, core], metas.at[0, 0, pl.ds(0, 3), core]):
        copy(v, v, mt_send.at[0], mt_recv.at[12], sibling).wait_send()
    v = metas.at[:, :, :, core]
    copy(v, v, mt_send.at[1], mt_recv.at[12], sibling).wait_send()
    for cp in started:
        cp.wait_send()

    ALL = "all"

    def where_(p, offsets, drop=()):
        idx = [None] * 3
        for s, o in enumerate(offsets):
            a = ORDERS[p][s]
            idx[a] = slice(None) if o is ALL else shifted[a][o % 4]
        return tuple(idx[a] for a in range(3) if a not in [ORDERS[p][s] for s in drop])

    def cols_of(p, half):
        if half is None:
            return pl.ds(0, PARTS[p][2])
        return (pl.ds(0, HALF), pl.ds(HALF, PARTS[p][2] - HALF))[half]

    def mine(p, offsets, half=None, which=None):
        which = core if which is None else which
        return xs[p].at[where_(p, offsets) + (which, slice(None), cols_of(p, half))]

    def ways(p, s):
        return neighbour(ORDERS[p][s], 1), neighbour(ORDERS[p][s], -1)

    def ag(p, k, v, to):
        copy(v, v, ag_send.at[p], ag_recv.at[p, k], to).start()

    def ag_wait(p, k, v):
        copy(v, v, ag_send.at[p], ag_recv.at[p, k], sibling).wait_recv()

    def forward(p, offsets):
        v = mine(p, offsets)
        group = 2 * (offsets[1] == 2) + (offsets[2] == 2)
        copy(v, v, sib_send.at[p], sib_recv.at[p, group], sibling).start()

    some = pl.ds(0, 3)
    near = [lax.div(me[a], 2) for a in range(3)]
    far = [1 - h for h in near]

    def pair(p, two, three):
        for i in range(2):
            half = [None] * 3
            for s, h in enumerate((i, two, three)):
                half[ORDERS[p][s]] = h
            yield half[0] * 4 + half[1] * 2 + half[2], octant(*half)

    def halves_at(p, group):
        a2, a3 = ORDERS[p][1:]
        return (far if group >= 2 else near)[a2], (far if group % 2 else near)[a3]

    def dispatch(p, group):
        idx = ((some, some, slice(None)), (0, some, slice(None)), (0, some, slice(None)), (0, 0, slice(None)))[group]
        v = xs[p].at[idx + (1 - core,)]
        copy(v, v, sib_send.at[p], sib_recv.at[p, group], sibling).wait_recv()
        for o, at in pair(p, *halves_at(p, group)):
            src = xs[p][at].reshape(256, PARTS[p][2])
            got = jnp.dot(picks[o], src, preferred_element_type=jnp.float32).astype(jnp.bfloat16)
            to = pl.ds(pl.multiple_of(o * 32, 32), 32)
            for e in range(4):
                ds[p][e, to, :] = got[e * 32 : (e + 1) * 32]

    def wait_sent(p, sem):
        for idx in ((some,), (0, some), (0, 0, some)):
            v = xs[p].at[idx + (slice(None),) * (3 - len(idx)) + (core,)]
            copy(v, v, sem, ag_recv.at[p, 0], sibling).wait_send()

    def third(p, j):
        up, dn = ways(p, 2)
        k = 9 + (j % 4) * 4
        ag(p, k, mine(p, (ALL, j, 0)), up)
        ag(p, k + 1, mine(p, (ALL, j, 0)), dn)

    def third_relay(p, j):
        up, dn = ways(p, 2)
        k = 9 + (j % 4) * 4
        ag_wait(p, k, mine(p, (ALL, j, -1)))
        ag(p, k + 2, mine(p, (ALL, j, -1), 0), up)
        ag_wait(p, k + 1, mine(p, (ALL, j, 1)))
        ag(p, k + 3, mine(p, (ALL, j, 1), 1), dn)
        forward(p, (ALL, j, -1))
        forward(p, (ALL, j, 1))

    def third_end(p, j):
        k = 9 + (j % 4) * 4
        ag_wait(p, k + 2, mine(p, (ALL, j, 2), 0))
        ag_wait(p, k + 3, mine(p, (ALL, j, 2), 1))
        forward(p, (ALL, j, 2))

    for p in range(3):
        own = mine(p, (0, 0, 0))
        up, dn = ways(p, 0)
        ag(p, 0, own, up)
        ag(p, 1, own, dn)
        ag(p, 2, own, neighbour(ORDERS[p][0], 2))
    for p in range(3):
        ag_wait(p, 0, mine(p, (-1, 0, 0)))
        ag_wait(p, 1, mine(p, (1, 0, 0)))
        ag_wait(p, 2, mine(p, (2, 0, 0)))
        up, dn = ways(p, 1)
        ag(p, 3, mine(p, (ALL, 0, 0), 0), up)
        ag(p, 4, mine(p, (ALL, 0, 0), 1), dn)
        ag(p, 5, mine(p, (ALL, 0, 0), 1), up)
        ag(p, 6, mine(p, (ALL, 0, 0), 0), dn)
        third(p, 0)
        forward(p, (ALL, 0, 0))
    for p in range(3):
        up, dn = ways(p, 1)
        ag_wait(p, 3, mine(p, (ALL, -1, 0), 0))
        ag(p, 7, mine(p, (ALL, -1, 0), 0), up)
        ag_wait(p, 4, mine(p, (ALL, 1, 0), 1))
        ag(p, 8, mine(p, (ALL, 1, 0), 1), dn)
    for p in range(3):
        ag_wait(p, 5, mine(p, (ALL, -1, 0), 1))
        third(p, -1)
        ag_wait(p, 6, mine(p, (ALL, 1, 0), 0))
        third(p, 1)
        forward(p, (ALL, -1, 0))
        forward(p, (ALL, 1, 0))
    for p in range(3):
        third_relay(p, 0)
    for p in range(3):
        ag_wait(p, 7, mine(p, (ALL, 2, 0), 0))
        ag_wait(p, 8, mine(p, (ALL, 2, 0), 1))
        third(p, 2)
        forward(p, (ALL, 2, 0))
    for p in range(3):
        third_end(p, 0)
        third_relay(p, -1)
    for p in range(3):
        third_relay(p, 1)
        third_end(p, -1)
    for p in range(3):
        dispatch(p, 0)
    for p in range(3):
        third_relay(p, 2)
        third_end(p, 1)
    for p in range(3):
        dispatch(p, 1)
    for p in range(3):
        dispatch(p, 2)
    for p in range(3):
        third_end(p, 2)
    for p in range(3):
        dispatch(p, 3)

    def expert(e, _):
        gate = jnp.zeros((256, 192), jnp.float32)
        upv = jnp.zeros((256, 192), jnp.float32)
        for p, (lo, n, held) in enumerate(PARTS):
            y = ds[p][e, :, 0:n]
            gate = gate + lax.dot_general(y, gate_w[e, :, lo : lo + n], nt, preferred_element_type=jnp.float32)
            upv = upv + lax.dot_general(y, up_w[e, :, lo : lo + n], nt, preferred_element_type=jnp.float32)
        hidden = gate * jax.nn.sigmoid(GLU * gate) * (upv + 1.0)
        hidden_all[e] = (hidden * slot_weight[e][:, 0:1]).astype(jnp.bfloat16)
        return 0

    lax.fori_loop(0, 4, expert, 0)

    turns = (2, 1, -1, 0)

    def other(p, offsets):
        return ss[p].at[where_(p, offsets)]

    def land3(p, slot, j, half=None):
        return rbufs[p][2].at[(slot,) + where_(p, (ALL, j, 0), (2,)) + (slice(None), cols_of(p, half))]

    def land2(p, slot, half=None):
        return rbufs[p][1].at[slot, :, :, cols_of(p, half)]

    def rs(p, k, src, dst, to):
        copy(src, dst, rs_send.at[p], rs_recv.at[p, k], to).start()

    def rs_wait(p, k, dst):
        copy(dst, dst, rs_send.at[p], rs_recv.at[p, k], sibling).wait_recv()

    def add(dst, *others):
        for i in range(4):
            total = dst[i]
            for o in others:
                total = total + o[i]
            dst[i] = total

    def half_of(ref, p, half):
        return ref.at[:, :, cols_of(p, half)]

    def first(p, j):
        up, dn = ways(p, 2)
        k = 9 + (j % 4) * 4
        add(mine(p, (ALL, j, 2)), other(p, (ALL, j, 2)))
        rs(p, k, mine(p, (ALL, j, 2), 0), land3(p, 2, j, 0), up)
        rs(p, k + 1, mine(p, (ALL, j, 2), 1), land3(p, 2, j, 1), dn)

    def mid(p, j):
        up, dn = ways(p, 2)
        k = 9 + (j % 4) * 4
        add(mine(p, (ALL, j, 1), 1), half_of(other(p, (ALL, j, 1)), p, 1))
        add(mine(p, (ALL, j, -1), 0), half_of(other(p, (ALL, j, -1)), p, 0))
        rs_wait(p, k, land3(p, 2, j, 0))
        add(mine(p, (ALL, j, 1), 0), half_of(other(p, (ALL, j, 1)), p, 0), land3(p, 2, j, 0))
        rs(p, k + 2, mine(p, (ALL, j, 1)), land3(p, 0, j), up)
        rs_wait(p, k + 1, land3(p, 2, j, 1))
        add(mine(p, (ALL, j, -1), 1), half_of(other(p, (ALL, j, -1)), p, 1), land3(p, 2, j, 1))
        rs(p, k + 3, mine(p, (ALL, j, -1)), land3(p, 1, j), dn)

    def last(p, j):
        k = 9 + (j % 4) * 4
        rs_wait(p, k + 2, land3(p, 0, j))
        rs_wait(p, k + 3, land3(p, 1, j))
        add(mine(p, (ALL, j, 0)), other(p, (ALL, j, 0)), land3(p, 0, j), land3(p, 1, j))
        up, dn = ways(p, 1)
        if j == 2:
            rs(p, 3, mine(p, (ALL, 2, 0), 0), land2(p, 2, 0), up)
            rs(p, 4, mine(p, (ALL, 2, 0), 1), land2(p, 2, 1), dn)
        if j == 1:
            rs(p, 5, mine(p, (ALL, 1, 0), 1), land2(p, 0, 1), up)
        if j == -1:
            rs(p, 6, mine(p, (ALL, -1, 0), 0), land2(p, 1, 0), dn)

    def second(p):
        up, dn = ways(p, 1)
        rs_wait(p, 3, land2(p, 2, 0))
        add(mine(p, (ALL, 1, 0), 0), land2(p, 2, 0))
        rs(p, 7, mine(p, (ALL, 1, 0), 0), land2(p, 0, 0), up)
        rs_wait(p, 4, land2(p, 2, 1))
        add(mine(p, (ALL, -1, 0), 1), land2(p, 2, 1))
        rs(p, 8, mine(p, (ALL, -1, 0), 1), land2(p, 1, 1), dn)

    def second_end(p):
        rs_wait(p, 5, land2(p, 0, 1))
        rs_wait(p, 6, land2(p, 1, 0))
        rs_wait(p, 7, land2(p, 0, 0))
        rs_wait(p, 8, land2(p, 1, 1))
        add(mine(p, (ALL, 0, 0)), land2(p, 0), land2(p, 1))
        up, dn = ways(p, 0)
        rs(p, 0, mine(p, (1, 0, 0)), rbufs[p][0].at[0], up)
        rs(p, 1, mine(p, (-1, 0, 0)), rbufs[p][0].at[1], dn)
        rs(p, 2, mine(p, (2, 0, 0)), rbufs[p][0].at[2], neighbour(ORDERS[p][0], 2))

    def down(p):
        lo, n, wide = PARTS[p]

        def one(e, _):
            ds[p][e, :, 0:n] = jnp.dot(
                hidden_all[e], down_w[e, :, lo : lo + n], preferred_element_type=jnp.float32
            ).astype(jnp.bfloat16)
            return 0

        lax.fori_loop(0, 4, one, 0)
        wait_sent(p, ag_send.at[p])
        v = mine(p, (ALL, ALL, ALL))
        copy(v, v, sib_send.at[p], sib_recv.at[p, 0], sibling).wait_send()

    def swap(p, group):
        idx = [slice(None)] * 3
        for s, h in zip((1, 2), halves_at(p, group)):
            idx[ORDERS[p][s]] = pl.ds(h * 2, 2)
        idx = tuple(idx)
        return copy(
            xs[p].at[idx + (1 - core,)], ss[p].at[idx], sx_send.at[p], sx_recv.at[p, group], sibling
        )

    def combine(p, group):
        for o, at in pair(p, *halves_at(p, group)):
            rows = pl.ds(pl.multiple_of(o * 32, 32), 32)
            y = jnp.concatenate([ds[p][e, rows, :] for e in range(4)], axis=0)
            got = jnp.dot(table[o], y, preferred_element_type=jnp.float32).astype(jnp.bfloat16)
            xs[p][at] = got.reshape(2, 2, 2, 2, 16, PARTS[p][2])
        swap(p, group).start()

    down(0)
    combine(0, 3)
    down(1)
    combine(1, 3)
    swap(0, 3).wait_recv()
    first(0, 2)
    down(2)
    combine(2, 3)
    swap(1, 3).wait_recv()
    first(1, 2)
    combine(0, 2)
    swap(2, 3).wait_recv()
    first(2, 2)
    combine(1, 2)
    combine(2, 2)
    for p in range(3):
        swap(p, 2).wait_recv()
        mid(p, 2)
        combine(p, 1)
        combine(p, 0)
    for p in range(3):
        swap(p, 1).wait_recv()
        swap(p, 0).wait_recv()
        first(p, 1)
        first(p, -1)
        first(p, 0)
    for p in range(3):
        mid(p, 1)
    for p in range(3):
        last(p, 2)
        mid(p, -1)
    for p in range(3):
        last(p, 1)
        mid(p, 0)
    for p in range(3):
        last(p, -1)
        second(p)
    for p in range(3):
        last(p, 0)
    for p in range(3):
        second_end(p)
    for p, (lo, n, wide) in enumerate(PARTS):
        total = mine(p, (0, 0, 0))[...].astype(jnp.float32)
        for s in range(3):
            rs_wait(p, s, rbufs[p][0].at[s])
            total = total + rbufs[p][0][s].astype(jnp.float32)
        out[:, lo : lo + n] = (resid[:, lo : lo + n] + total[:, :n]).astype(jnp.bfloat16)
    for p in range(3):
        wait_sent(p, rs_send.at[p])
        v = other(p, (ALL, ALL, ALL))
        copy(v, v, sx_send.at[p], sx_recv.at[p, 0], sibling).wait_send()


def layer(tokens, attn_gain, mlp_gain, sinks, routes, fixed, weights):
    bf = jnp.bfloat16
    wide = [p[2] for p in PARTS]
    width = tokens.shape[1]
    dma = pltpu.SemaphoreType.DMA
    scratch = (
        [pltpu.VMEM((4, 4, 4, 2, 16, h), bf) for h in wide]
        + [pltpu.VMEM((4, 256, h), bf) for h in wide]
        + [pltpu.VMEM((4, 4, 4, 16, h), bf) for h in wide]
        + [pltpu.VMEM((4, 192, width), bf)] * 3
        + [
            pltpu.VMEM((2, 48, 4, width), bf),
            pltpu.VMEM((4, 256, 192), bf),
            pltpu.VMEM((1, 2944), jnp.float32),
        ]
        + [
            pltpu.VMEM((GROUPS, 256, 128), bf),
            pltpu.VMEM((GROUPS, 128, 256), bf),
            pltpu.VMEM((4, 256, 128), jnp.float32),
            pltpu.VMEM((4, 4, 4, 2, 16, 128), bf),
            pltpu.VMEM((256, 256), bf),
        ]
        + [pltpu.VMEM((3,) + (4,) * s + (16, h), bf) for h in wide for s in range(3)]
        + [pltpu.VMEM(w.shape, bf) for w in (weights[0], weights[1], weights[2])]
        + [
            pltpu.VMEM((2, 4, 2, 16, width), bf),
            pltpu.VMEM((256, width), bf),
            pltpu.VMEM((256, 64), bf),
            pltpu.VMEM((2, 384, 64), bf),
            pltpu.VMEM((256, 256), bf),
            pltpu.VMEM((256, 256), bf),
            pltpu.VMEM((2, 4, 2, 16, width), bf),
            pltpu.VMEM((2, 4, 16, width), bf),
            pltpu.VMEM((3, 2, 16, width), bf),
            pltpu.VMEM((16, width), bf),
            pltpu.VMEM((16, 2944), jnp.float32),
        ]
        + [
            dma((5,)), dma((3,)), dma((3, 25)), dma((3,)), dma((3, 4)),
            dma((3,)), dma((3, 25)), dma((3,)), dma((3, 4)),
            dma((2,)), dma((13,)), dma((2,)), dma((9,)), dma((4,)), dma((4,)), dma((11,)), dma((11,)),
        ]
    )
    vm = pl.BlockSpec(memory_space=pltpu.VMEM)
    sm = pl.BlockSpec(memory_space=pltpu.SMEM)
    anym = pl.BlockSpec(memory_space=pl.ANY)
    return pl.pallas_call(
        layer_kernel,
        out_shape=jax.ShapeDtypeStruct(tokens.shape, bf),
        in_specs=[vm] * 3 + [sm] + [vm] * 2 + [anym] * 6,
        out_specs=vm,
        scratch_shapes=scratch,
        compiler_params=pltpu.CompilerParams(
            collective_id=1, has_side_effects=True, vmem_limit_bytes=62 * 1024 * 1024
        ),
        name="layer",
    )(tokens, attn_gain, mlp_gain, sinks, routes, fixed, *weights)


def shards(
    tokens, attn_gain, query_weight, keyval_weight, sink_logits, out_weight,
    mlp_gain, routes, gate_fixed, gate_weight, up_weight, down_weight,
):
    experts = [jnp.transpose(w, (1, 0, 2)) for w in (gate_weight, up_weight, down_weight)]
    weights = (query_weight, keyval_weight, out_weight.T, *experts)
    return layer(tokens, attn_gain, mlp_gain, sink_logits, routes.T, gate_fixed.T, weights)


def solution(mesh):
    in_specs = (
        P(("ctx", "fsdp"), None),
        P(),
        P(None, "fsdp"),
        P("fsdp", None),
        P("fsdp"),
        P("fsdp", None),
        P(),
        P(("ctx", "fsdp"), None),
        P(("ctx", "fsdp"), None),
        P("fsdp", "ctx", None),
        P("fsdp", "ctx", None),
        P("fsdp", "ctx", None),
    )
    out_specs = P(("ctx", "fsdp"), None)
    return jax.shard_map(shards, mesh=mesh, in_specs=in_specs, out_specs=out_specs, check_vma=False)
```

```python
import math
import jax
import jax.numpy as jnp
from jax import lax
from jax.experimental import pallas as pl
from jax.experimental.pallas import tpu as pltpu
from jax.sharding import PartitionSpec as P

PARTS = ((0, 1024, 1024), (1024, 1024, 1024), (2048, 832, 896))
ORDERS = ((0, 1, 2), (1, 2, 0), (2, 0, 1))
HALF = 512
GROUPS = 8
GLU = 1.702


def layer_kernel(
    tokens, attn_gain, mlp_gain, sinks, routes, fixed,
    query_hbm, keyval_hbm, outw_hbm, gate_hbm, up_hbm, down_hbm, out,
    x0, x1, x2, d0, d1, d2, s0, s1, s2,
    gate_w, up_w, down_w, stage, hidden_all, gain_pad, table, picks, slot_weight, metas, lower,
    ra0, ra1, ra2, rb0, rb1, rb2, rc0, rc1, rc2,
    query_w, keyval_w, outw_w, gathered, normed, kv_mine, kv_all, queries, attended,
    part, part_sib, part_in, part_last, resid,
    wsem, ag_send, ag_recv, sib_send, sib_recv,
    rs_send, rs_recv, sx_send, sx_recv,
    mt_send, mt_recv, ta_send, ta_recv, kv_send, kv_recv, tr_send, tr_recv,
):
    xs, ds, ss = (x0, x1, x2), (d0, d1, d2), (s0, s1, s2)
    rbufs = ((ra0, ra1, ra2), (rb0, rb1, rb2), (rc0, rc1, rc2))
    ctx = lax.axis_index("ctx")
    fsdp = lax.axis_index("fsdp")
    core = lax.rem(fsdp, 2)
    me = (lax.div(ctx, 2), lax.div(fsdp, 8) * 2 + lax.rem(ctx, 2), lax.rem(lax.div(fsdp, 2), 4))
    shifted = [[me[a]] + [lax.rem(me[a] + by, 4) for by in (1, 2, 3)] for a in range(3)]

    def device(z, y, x, c):
        return (z * 2 + lax.rem(y, 2), (lax.div(y, 2) * 4 + x) * 2 + c)

    def neighbour(axis, by):
        at = list(me)
        at[axis] = shifted[axis][by % 4]
        return device(*at, core)

    sibling = device(*me, 1 - core)

    def copy(src, dst, ss_, rs_, to):
        return pltpu.make_async_remote_copy(
            src_ref=src, dst_ref=dst, send_sem=ss_, recv_sem=rs_,
            device_id=to, device_id_type=pl.DeviceIdType.MESH,
        )

    loads = [
        pltpu.make_async_copy(h, v, wsem.at[i])
        for i, (h, v) in enumerate(((keyval_hbm, keyval_w), (query_hbm, query_w), (outw_hbm, outw_w)))
    ]
    for w in loads:
        w.start()

    def chunk(i):
        src = (gate_hbm, up_hbm, down_hbm)[i // 4]
        n = 36 if i % 4 == 3 else 48
        return pltpu.make_async_copy(
            src.at[pl.ds((i % 4) * 48, n)], stage.at[i % 2, pl.ds(0, n)], wsem.at[3 + i % 2]
        )

    turned = [0]

    def turn_weights(count):
        for i in range(turned[0], min(turned[0] + count, 12)):
            chunk(i).wait()
            dst = (gate_w, up_w, down_w)[i // 4]
            rows = pl.ds((i % 4) * 48, 48)
            if i % 4 == 3:
                stage[i % 2, 36:48] = jnp.zeros((12, 4, 2880), jnp.bfloat16)

            def tile(t, _):
                cols = pl.ds(pl.multiple_of(t * 256, 256), 256)
                dst[:, rows, cols] = jnp.swapaxes(stage[i % 2, :, :, cols], 0, 1)
                return 0

            lax.fori_loop(0, 11, tile, 0)
            dst[:, rows, 2816:2880] = jnp.swapaxes(stage[i % 2, :, :, 2816:2880], 0, 1)
            if i + 2 < 12:
                chunk(i + 2).start()
            turned[0] = i + 1

    chunk(0).start()
    chunk(1).start()

    def signal(to):
        pl.semaphore_signal(barrier, inc=1, device_id=to, device_id_type=pl.DeviceIdType.MESH)

    barrier = pltpu.get_barrier_semaphore()
    across = neighbour(1, 2)
    diagonal = [device(me[0], shifted[1][2], shifted[2][by % 4], core) for by in range(4)]
    partners = [neighbour(a, b) for a in range(3) for b in (1, -1, 2)] + [sibling] + diagonal[1:]
    for to in partners:
        signal(to)
    behind = (ctx + 7) % 8
    ahead = (ctx + 1) % 8
    key_from, value_from = fsdp // 2, 8 + fsdp // 2
    signal((behind, key_from))
    signal((behind, value_from))

    @pl.when(fsdp != 0)
    def _():
        signal((ctx, key_from))

    @pl.when(fsdp != 15)
    def _():
        signal((ctx, value_from))

    yh = lax.div(me[1], 2)
    ys = (yh, 1 - yh)
    gathered[yh, me[2], core] = tokens[...]
    high = fixed[...] // 256
    low = fixed[...] - high * 256
    about = jnp.concatenate([routes[...], high, low, jnp.zeros((4, 16), jnp.int32)], axis=0)
    about = about.astype(jnp.float32).T.astype(jnp.bfloat16)
    spot = lax.broadcasted_iota(jnp.int32, (16, 128), 0) == lax.broadcasted_iota(jnp.int32, (16, 128), 1)
    about = jnp.dot(about, jnp.where(spot, 1.0, 0.0).astype(jnp.bfloat16), preferred_element_type=jnp.float32)
    metas[me[0], me[1], me[2], core] = about.astype(jnp.bfloat16)

    r = lax.broadcasted_iota(jnp.int32, (256, 256), 0)
    c = lax.broadcasted_iota(jnp.int32, (256, 256), 1)
    lower[...] = jnp.where((r // 16 == c // 16) & (c < r), 1.0, 0.0).astype(jnp.bfloat16)
    alone = jnp.where((fsdp == 0) | (fsdp == 15), 1, 0)
    pl.semaphore_wait(barrier, len(partners) + 4 - alone)

    started = []

    def send(src, dst, send_sem, recv_sem, to):
        cp = copy(src, dst, send_sem, recv_sem, to)
        cp.start()
        started.append(cp)

    left, right = neighbour(2, -1), neighbour(2, 1)
    halves_of = (pl.ds(0, 1408), pl.ds(1408, 1472))

    def held(b, by, which):
        return gathered.at[ys[b], shifted[2][by % 4], which]

    def norm_block(b, by, which):
        y_, x_ = ys[b], shifted[2][by % 4]
        v = gathered[y_, x_, which].astype(jnp.float32)
        scale = lax.rsqrt(jnp.sum(v * v, axis=-1, keepdims=True) * (1.0 / 2880.0) + 1e-05)
        row = ((y_ * 4 + x_) * 2 + which) * 16
        normed[pl.ds(pl.multiple_of(row, 16), 16), :] = (v * scale * attn_gain[...].reshape(1, 2880)).astype(jnp.bfloat16)

    lanes = lax.broadcasted_iota(jnp.int32, (256, 128), 1)
    early = lanes % 64 < 32
    freqs = jnp.exp((lanes % 32).astype(jnp.float32) * (-2.0 / 64 * math.log(150000.0)))
    angles = (ctx * 256 + lax.broadcasted_iota(jnp.int32, (256, 128), 0)).astype(jnp.float32) * freqs

    def meta_view(stage, by):
        idx = tuple(slice(None) if a < stage else (shifted[a][by % 4] if a == stage else me[a]) for a in range(3))
        return metas.at[idx + (core,)]

    def meta_send(stage):
        v = meta_view(stage, 0)
        for by in (2, 1, -1):
            copy(v, v, mt_send.at[0], mt_recv.at[stage * 4 + by % 4], neighbour(stage, by)).start()

    def meta_wait(stage):
        for by in (2, 1, -1):
            v = meta_view(stage, by)
            copy(v, v, mt_send.at[0], mt_recv.at[stage * 4 + -by % 4], sibling).wait_recv()

    mates = ((1, 2), (1, 1), (1, -1), (0, 2), (1, 0), (0, 1), (0, -1))
    own = held(0, 0, core)
    for b, by in mates:
        to = diagonal[by % 4] if b else neighbour(2, by)
        copy(own, own, ta_send.at[0], ta_recv.at[b * 4 + by % 4], to).start()
    copy(own, own, ta_send.at[1], ta_recv.at[8], sibling).start()
    meta_send(0)
    norm_block(0, 0, core)
    cosine = jnp.cos(angles)
    sine = jnp.sin(angles)
    sine = jnp.where(early, -sine, sine)
    turn_weights(6)
    for b, by in ((0, -1), (0, 1), (1, 0), (0, 2), (1, -1), (1, 1), (1, 2)):
        v = held(b, by, core)
        copy(v, v, ta_send.at[0], ta_recv.at[b * 4 + -by % 4], sibling).wait_recv()
        copy(v, v, ta_send.at[1], ta_recv.at[8], sibling).start()
        norm_block(b, by, core)
    meta_wait(0)
    meta_send(1)
    v = gathered.at[:, :, 1 - core]
    copy(v, v, ta_send.at[1], ta_recv.at[8], sibling).wait_recv()
    for b in range(2):
        for by in range(4):
            norm_block(b, by, 1 - core)

    nt = (((1,), (1,)), ((), ()))

    def turn(v, c_, s_):
        return v * c_ + jnp.where(early, pltpu.roll(v, 96, 1), pltpu.roll(v, 32, 1)) * s_

    loads[0].wait()
    kv = lax.dot_general(normed[...], keyval_w[...], nt, preferred_element_type=jnp.float32)
    kv = jnp.concatenate([kv, kv], axis=1)
    kv = jnp.where(fsdp < 8, turn(kv, cosine, sine), kv)
    kv_mine[...] = kv[:, :64].astype(jnp.bfloat16)
    which = fsdp // 8
    main, rim = pl.ds(128, 256), pl.ds(0, 128)
    wait_main = []
    for i in range(2):
        to = 2 * (fsdp % 8) + i
        cp = copy(kv_mine, kv_all.at[which, main], kv_send.at[i], kv_recv.at[which * 2], (ctx, to))
        own = fsdp == 15 * i

        @pl.when(jnp.logical_not(own))
        def _(cp=cp):
            cp.start()

        @pl.when(own)
        def _():
            kv_all[which, main] = kv_mine[...]

        wait_main.append((own, cp))
        send(
            kv_mine.at[pl.ds(128, 128)], kv_all.at[which, rim],
            kv_send.at[2 + i], kv_recv.at[which * 2 + 1], (ahead, to),
        )
    meta_wait(1)
    meta_send(2)
    loads[1].wait()
    query = jnp.dot(normed[...], query_w[...], preferred_element_type=jnp.float32)
    for i in range(2):
        cols = slice(i * 128, i * 128 + 128)
        queries[:, cols] = turn(query[:, cols], cosine, sine).astype(jnp.bfloat16)
    turn_weights(1)
    for w in range(2):
        v = kv_all.at[w, main]

        @pl.when(fsdp != 15 * w)
        def _(v=v, w=w):
            copy(v, v, kv_send.at[0], kv_recv.at[w * 2], sibling).wait_recv()

        v = kv_all.at[w, rim]
        copy(v, v, kv_send.at[0], kv_recv.at[w * 2 + 1], sibling).wait_recv()
    for own, cp in wait_main:

        @pl.when(jnp.logical_not(own))
        def _(cp=cp):
            cp.wait_send()

    row = lax.broadcasted_iota(jnp.int32, (128, 256), 0)
    col = lax.broadcasted_iota(jnp.int32, (128, 256), 1)
    for b in range(2):
        allowed = (col <= row + 128) & (col > row) & (ctx * 256 + b * 128 - 128 + col >= 0)
        keys = kv_all[0, b * 128 : b * 128 + 256]
        values = kv_all[1, b * 128 : b * 128 + 256]
        for h in range(4):
            q = queries[b * 128 : b * 128 + 128, h * 64 : h * 64 + 64]
            score = lax.dot_general(q, keys, nt, preferred_element_type=jnp.float32) * 0.125
            score = jnp.where(allowed, score, -1e30)
            sink = sinks[h]
            top = jnp.maximum(jnp.max(score, axis=-1, keepdims=True), sink)
            expd = jnp.exp(score - top)
            total = jnp.exp(sink - top) + jnp.sum(expd, axis=-1, keepdims=True)
            probs = (expd / total).astype(jnp.bfloat16)
            mixed = jnp.dot(probs, values, preferred_element_type=jnp.float32)
            attended[b * 128 : b * 128 + 128, h * 64 : h * 64 + 64] = mixed.astype(jnp.bfloat16)

    meta_wait(2)
    v = metas.at[:, :, :, core]
    copy(v, v, mt_send.at[1], mt_recv.at[12], sibling).start()
    loads[2].wait()
    for lo, n in ((0, 1024), (1024, 1024), (2048, 832)):
        got = lax.dot_general(
            attended[...], outw_w[lo : lo + n, :], nt, preferred_element_type=jnp.float32
        ).astype(jnp.bfloat16)
        part[:, :, :, :, lo : lo + n] = got.reshape(2, 4, 2, 16, n)

    def octant(zh, yh_, xh):
        return pl.ds(zh * 2, 2), pl.ds(yh_ * 2, 2), pl.ds(xh * 2, 2)

    first_expert = fsdp * 4
    lane = lax.broadcasted_iota(jnp.int32, (256, 128), 1)
    row = lax.broadcasted_iota(jnp.int32, (256, 128), 0)
    lane_expert = (first_expert + lane // 32).astype(jnp.float32)
    lane_slot = ((lane % 32) // 16).astype(jnp.float32)
    same_source = row // 16 == lane % 16
    slot_expert = (first_expert + row[:128] // 32).astype(jnp.float32)

    def tables(lo, hi):
        def one(o, _):
            known = metas[octant(o // 4, (o // 2) % 2, o % 2)].reshape(256, 128)
            ids = known.astype(jnp.float32)
            hit = jnp.zeros((256, 128), jnp.float32)
            for k in range(4):
                hit = hit + jnp.where(ids[:, k : k + 1] == lane_expert, 1.0, 0.0)
            rank = jnp.dot(lower[...], hit.astype(jnp.bfloat16), preferred_element_type=jnp.float32)
            t = jnp.where((rank == lane_slot) & same_source, hit, 0.0)
            table[o] = t.astype(jnp.bfloat16)
            pick = t.T.astype(jnp.bfloat16)
            picks[o] = pick
            got = jnp.dot(pick, known, preferred_element_type=jnp.float32)
            weight = jnp.zeros((128, 128), jnp.float32)
            for k in range(4):
                value = got[:, 4 + k : 5 + k] * 256.0 + got[:, 8 + k : 9 + k]
                weight = weight + jnp.where(got[:, k : k + 1] == slot_expert, value, 0.0)
            weight = weight * (1.0 / 65536.0)
            at = pl.ds(pl.multiple_of(o * 32, 32), 32)
            for e in range(4):
                slot_weight[e, at, :] = weight[e * 32 : e * 32 + 32]
            return 0

        lax.fori_loop(lo, hi, one, 0)

    def piece(by, half=None):
        cols = slice(None) if half is None else halves_of[half]
        return part.at[:, shifted[2][by % 4], core, :, cols]

    def landed(slot, half):
        return part_in.at[slot, :, :, halves_of[half]]

    def from_sibling(by):
        return part_sib.at[:, shifted[2][by % 4]]

    def tr_wait(k, v):
        copy(v, v, tr_send.at[k], tr_recv.at[k], sibling).wait_recv()

    def plus(dst, *others):
        for i in range(2):
            total = dst[i].astype(jnp.float32)
            for o in others:
                total = total + o[i].astype(jnp.float32)
            dst[i] = total.astype(jnp.bfloat16)

    for k, by in enumerate((2, 1, -1, 0)):
        send(
            part.at[:, shifted[2][by % 4], 1 - core], from_sibling(by),
            tr_send.at[k], tr_recv.at[k], sibling,
        )
    tr_wait(0, from_sibling(2))
    plus(piece(2), from_sibling(2))
    send(piece(2, 0), landed(2, 0), tr_send.at[4], tr_recv.at[4], right)
    send(piece(2, 1), landed(2, 1), tr_send.at[5], tr_recv.at[5], left)
    tr_wait(1, from_sibling(1))
    plus(piece(1), from_sibling(1))
    send(piece(1, 1), landed(0, 1), tr_send.at[6], tr_recv.at[6], right)
    tr_wait(2, from_sibling(-1))
    plus(piece(-1), from_sibling(-1))
    send(piece(-1, 0), landed(1, 0), tr_send.at[7], tr_recv.at[7], left)
    v = metas.at[:, :, :, 1 - core]
    copy(v, v, mt_send.at[1], mt_recv.at[12], sibling).wait_recv()
    tables(0, 5)
    tr_wait(4, landed(2, 0))
    plus(piece(1, 0), landed(2, 0))
    send(piece(1, 0), landed(0, 0), tr_send.at[8], tr_recv.at[8], right)
    tr_wait(5, landed(2, 1))
    plus(piece(-1, 1), landed(2, 1))
    send(piece(-1, 1), landed(1, 1), tr_send.at[9], tr_recv.at[9], left)
    tr_wait(3, from_sibling(0))
    plus(piece(0), from_sibling(0))
    tables(5, 8)
    turn_weights(2)
    tr_wait(6, landed(0, 1))
    tr_wait(7, landed(1, 0))
    tr_wait(8, landed(0, 0))
    tr_wait(9, landed(1, 1))
    plus(piece(0), part_in.at[0], part_in.at[1])
    send(part.at[1 - yh, me[2], core], part_last, tr_send.at[10], tr_recv.at[10], across)
    turn_weights(12)
    tr_wait(10, part_last)
    total = part[yh, me[2], core].astype(jnp.float32) + part_last[...].astype(jnp.float32)
    resid[:, 2816:2944] = jnp.zeros((16, 128), jnp.float32)
    resid[:, 0:2880] = tokens[...].astype(jnp.float32) + total
    v = resid[...]
    scale = lax.rsqrt(jnp.sum(v * v, axis=-1, keepdims=True) * (1.0 / 2880.0) + 1e-05)
    gain_pad[...] = jnp.zeros((1, 2944), jnp.float32)
    gain_pad[:, 0:2880] = mlp_gain[...].reshape(1, 2880)
    v = v * scale * gain_pad[...]
    for p, (lo, n, wide) in enumerate(PARTS):
        w = v[:, lo : lo + wide]
        xs[p][me[0], me[1], me[2], core] = w.astype(jnp.bfloat16)
    v = gathered.at[:, :, core]
    copy(v, v, ta_send.at[1], ta_recv.at[8], sibling).wait_send()
    for v in (gathered.at[yh, :, core], gathered.at[yh, pl.ds(0, 3), core]):
        copy(v, v, ta_send.at[0], ta_recv.at[8], sibling).wait_send()
    for v in (metas.at[pl.ds(0, 3), :, :, core], metas.at[0, pl.ds(0, 3), :, core], metas.at[0, 0, pl.ds(0, 3), core]):
        copy(v, v, mt_send.at[0], mt_recv.at[12], sibling).wait_send()
    v = metas.at[:, :, :, core]
    copy(v, v, mt_send.at[1], mt_recv.at[12], sibling).wait_send()
    for cp in started:
        cp.wait_send()

    ALL = "all"

    def where_(p, offsets, drop=()):
        idx = [None] * 3
        for s, o in enumerate(offsets):
            a = ORDERS[p][s]
            idx[a] = slice(None) if o is ALL else shifted[a][o % 4]
        return tuple(idx[a] for a in range(3) if a not in [ORDERS[p][s] for s in drop])

    def cols_of(p, half):
        if half is None:
            return pl.ds(0, PARTS[p][2])
        return (pl.ds(0, HALF), pl.ds(HALF, PARTS[p][2] - HALF))[half]

    def mine(p, offsets, half=None, which=None):
        which = core if which is None else which
        return xs[p].at[where_(p, offsets) + (which, slice(None), cols_of(p, half))]

    def ways(p, s):
        return neighbour(ORDERS[p][s], 1), neighbour(ORDERS[p][s], -1)

    def ag(p, k, v, to):
        copy(v, v, ag_send.at[p], ag_recv.at[p, k], to).start()

    def ag_wait(p, k, v):
        copy(v, v, ag_send.at[p], ag_recv.at[p, k], sibling).wait_recv()

    def forward(p, offsets):
        v = mine(p, offsets)
        group = 2 * (offsets[1] == 2) + (offsets[2] == 2)
        copy(v, v, sib_send.at[p], sib_recv.at[p, group], sibling).start()

    some = pl.ds(0, 3)
    near = [lax.div(me[a], 2) for a in range(3)]
    far = [1 - h for h in near]

    def pair(p, two, three):
        for i in range(2):
            half = [None] * 3
            for s, h in enumerate((i, two, three)):
                half[ORDERS[p][s]] = h
            yield half[0] * 4 + half[1] * 2 + half[2], octant(*half)

    def halves_at(p, group):
        a2, a3 = ORDERS[p][1:]
        return (far if group >= 2 else near)[a2], (far if group % 2 else near)[a3]

    def dispatch(p, group):
        idx = ((some, some, slice(None)), (0, some, slice(None)), (0, some, slice(None)), (0, 0, slice(None)))[group]
        v = xs[p].at[idx + (1 - core,)]
        copy(v, v, sib_send.at[p], sib_recv.at[p, group], sibling).wait_recv()
        for o, at in pair(p, *halves_at(p, group)):
            src = xs[p][at].reshape(256, PARTS[p][2])
            got = jnp.dot(picks[o], src, preferred_element_type=jnp.float32).astype(jnp.bfloat16)
            to = pl.ds(pl.multiple_of(o * 32, 32), 32)
            for e in range(4):
                ds[p][e, to, :] = got[e * 32 : (e + 1) * 32]

    def wait_sent(p, sem):
        for idx in ((some,), (0, some), (0, 0, some)):
            v = xs[p].at[idx + (slice(None),) * (3 - len(idx)) + (core,)]
            copy(v, v, sem, ag_recv.at[p, 0], sibling).wait_send()

    def third(p, j):
        up, dn = ways(p, 2)
        k = 9 + (j % 4) * 4
        ag(p, k, mine(p, (ALL, j, 0)), up)
        ag(p, k + 1, mine(p, (ALL, j, 0)), dn)

    def third_relay(p, j):
        up, dn = ways(p, 2)
        k = 9 + (j % 4) * 4
        ag_wait(p, k, mine(p, (ALL, j, -1)))
        ag(p, k + 2, mine(p, (ALL, j, -1), 0), up)
        ag_wait(p, k + 1, mine(p, (ALL, j, 1)))
        ag(p, k + 3, mine(p, (ALL, j, 1), 1), dn)
        forward(p, (ALL, j, -1))
        forward(p, (ALL, j, 1))

    def third_end(p, j):
        k = 9 + (j % 4) * 4
        ag_wait(p, k + 2, mine(p, (ALL, j, 2), 0))
        ag_wait(p, k + 3, mine(p, (ALL, j, 2), 1))
        forward(p, (ALL, j, 2))

    def spread(p, by):
        v = mine(p, (by, 0, 0))
        for s, k in ((1, 3), (2, 9)):
            up, dn = ways(p, s)
            ag(p, k, v, up)
            ag(p, k + 1, v, dn)

    for p in range(3):
        own = mine(p, (0, 0, 0))
        up, dn = ways(p, 0)
        ag(p, 2, own, neighbour(ORDERS[p][0], 2))
        ag(p, 0, own, up)
        ag(p, 1, own, dn)
    for p in range(3):
        spread(p, 0)
    for p in range(3):
        ag_wait(p, 0, mine(p, (-1, 0, 0)))
        spread(p, -1)
        ag_wait(p, 1, mine(p, (1, 0, 0)))
        spread(p, 1)
    for p in range(3):
        ag_wait(p, 2, mine(p, (2, 0, 0)))
        spread(p, 2)
        forward(p, (ALL, 0, 0))
    for p in range(3):
        up, dn = ways(p, 1)
        ag_wait(p, 3, mine(p, (ALL, -1, 0)))
        ag(p, 5, mine(p, (ALL, -1, 0), 0), up)
        third(p, -1)
        ag_wait(p, 4, mine(p, (ALL, 1, 0)))
        ag(p, 6, mine(p, (ALL, 1, 0), 1), dn)
        third(p, 1)
        forward(p, (ALL, -1, 0))
        forward(p, (ALL, 1, 0))
    for p in range(3):
        third_relay(p, 0)
    for p in range(3):
        ag_wait(p, 5, mine(p, (ALL, 2, 0), 0))
        ag_wait(p, 6, mine(p, (ALL, 2, 0), 1))
        third(p, 2)
        forward(p, (ALL, 2, 0))
    for p in range(3):
        third_end(p, 0)
        third_relay(p, -1)
    for p in range(3):
        third_relay(p, 1)
        third_end(p, -1)
    for p in range(3):
        dispatch(p, 0)
    for p in range(3):
        third_relay(p, 2)
        third_end(p, 1)
    for p in range(3):
        dispatch(p, 1)
    for p in range(3):
        dispatch(p, 2)
    for p in range(3):
        third_end(p, 2)
    for p in range(3):
        dispatch(p, 3)

    def expert(e, _):
        gate = jnp.zeros((256, 192), jnp.float32)
        upv = jnp.zeros((256, 192), jnp.float32)
        for p, (lo, n, held) in enumerate(PARTS):
            y = ds[p][e, :, 0:n]
            gate = gate + lax.dot_general(y, gate_w[e, :, lo : lo + n], nt, preferred_element_type=jnp.float32)
            upv = upv + lax.dot_general(y, up_w[e, :, lo : lo + n], nt, preferred_element_type=jnp.float32)
        hidden = gate * jax.nn.sigmoid(GLU * gate) * (upv + 1.0)
        hidden_all[e] = (hidden * slot_weight[e][:, 0:1]).astype(jnp.bfloat16)
        return 0

    lax.fori_loop(0, 4, expert, 0)

    turns = (2, 1, -1, 0)

    def other(p, offsets):
        return ss[p].at[where_(p, offsets)]

    def land3(p, slot, j, half=None):
        return rbufs[p][2].at[(slot,) + where_(p, (ALL, j, 0), (2,)) + (slice(None), cols_of(p, half))]

    def land2(p, slot, half=None):
        return rbufs[p][1].at[slot, :, :, cols_of(p, half)]

    def rs(p, k, src, dst, to):
        copy(src, dst, rs_send.at[p], rs_recv.at[p, k], to).start()

    def rs_wait(p, k, dst):
        copy(dst, dst, rs_send.at[p], rs_recv.at[p, k], sibling).wait_recv()

    def add(dst, *others):
        for i in range(4):
            total = dst[i]
            for o in others:
                total = total + o[i]
            dst[i] = total

    def half_of(ref, p, half):
        return ref.at[:, :, cols_of(p, half)]

    def first(p, j):
        up, dn = ways(p, 2)
        k = 9 + (j % 4) * 4
        add(mine(p, (ALL, j, 2)), other(p, (ALL, j, 2)))
        rs(p, k, mine(p, (ALL, j, 2), 0), land3(p, 2, j, 0), up)
        rs(p, k + 1, mine(p, (ALL, j, 2), 1), land3(p, 2, j, 1), dn)

    def mid(p, j):
        up, dn = ways(p, 2)
        k = 9 + (j % 4) * 4
        add(mine(p, (ALL, j, 1), 1), half_of(other(p, (ALL, j, 1)), p, 1))
        add(mine(p, (ALL, j, -1), 0), half_of(other(p, (ALL, j, -1)), p, 0))
        rs_wait(p, k, land3(p, 2, j, 0))
        add(mine(p, (ALL, j, 1), 0), half_of(other(p, (ALL, j, 1)), p, 0), land3(p, 2, j, 0))
        rs(p, k + 2, mine(p, (ALL, j, 1)), land3(p, 0, j), up)
        rs_wait(p, k + 1, land3(p, 2, j, 1))
        add(mine(p, (ALL, j, -1), 1), half_of(other(p, (ALL, j, -1)), p, 1), land3(p, 2, j, 1))
        rs(p, k + 3, mine(p, (ALL, j, -1)), land3(p, 1, j), dn)

    def last(p, j):
        k = 9 + (j % 4) * 4
        rs_wait(p, k + 2, land3(p, 0, j))
        rs_wait(p, k + 3, land3(p, 1, j))
        add(mine(p, (ALL, j, 0)), other(p, (ALL, j, 0)), land3(p, 0, j), land3(p, 1, j))
        up, dn = ways(p, 1)
        if j == 2:
            rs(p, 3, mine(p, (ALL, 2, 0), 0), land2(p, 2, 0), up)
            rs(p, 4, mine(p, (ALL, 2, 0), 1), land2(p, 2, 1), dn)
        if j == 1:
            rs(p, 5, mine(p, (ALL, 1, 0), 1), land2(p, 0, 1), up)
        if j == -1:
            rs(p, 6, mine(p, (ALL, -1, 0), 0), land2(p, 1, 0), dn)

    def second(p):
        up, dn = ways(p, 1)
        rs_wait(p, 3, land2(p, 2, 0))
        add(mine(p, (ALL, 1, 0), 0), land2(p, 2, 0))
        rs(p, 7, mine(p, (ALL, 1, 0), 0), land2(p, 0, 0), up)
        rs_wait(p, 4, land2(p, 2, 1))
        add(mine(p, (ALL, -1, 0), 1), land2(p, 2, 1))
        rs(p, 8, mine(p, (ALL, -1, 0), 1), land2(p, 1, 1), dn)

    def second_end(p):
        rs_wait(p, 5, land2(p, 0, 1))
        rs_wait(p, 6, land2(p, 1, 0))
        rs_wait(p, 7, land2(p, 0, 0))
        rs_wait(p, 8, land2(p, 1, 1))
        add(mine(p, (ALL, 0, 0)), land2(p, 0), land2(p, 1))
        up, dn = ways(p, 0)
        rs(p, 0, mine(p, (1, 0, 0)), rbufs[p][0].at[0], up)
        rs(p, 1, mine(p, (-1, 0, 0)), rbufs[p][0].at[1], dn)
        rs(p, 2, mine(p, (2, 0, 0)), rbufs[p][0].at[2], neighbour(ORDERS[p][0], 2))

    def down(p):
        lo, n, wide = PARTS[p]

        def one(e, _):
            ds[p][e, :, 0:n] = jnp.dot(
                hidden_all[e], down_w[e, :, lo : lo + n], preferred_element_type=jnp.float32
            ).astype(jnp.bfloat16)
            return 0

        lax.fori_loop(0, 4, one, 0)
        wait_sent(p, ag_send.at[p])
        v = mine(p, (ALL, ALL, ALL))
        copy(v, v, sib_send.at[p], sib_recv.at[p, 0], sibling).wait_send()

    def swap(p, group):
        idx = [slice(None)] * 3
        for s, h in zip((1, 2), halves_at(p, group)):
            idx[ORDERS[p][s]] = pl.ds(h * 2, 2)
        idx = tuple(idx)
        return copy(
            xs[p].at[idx + (1 - core,)], ss[p].at[idx], sx_send.at[p], sx_recv.at[p, group], sibling
        )

    def combine(p, group):
        for o, at in pair(p, *halves_at(p, group)):
            rows = pl.ds(pl.multiple_of(o * 32, 32), 32)
            y = jnp.concatenate([ds[p][e, rows, :] for e in range(4)], axis=0)
            got = jnp.dot(table[o], y, preferred_element_type=jnp.float32).astype(jnp.bfloat16)
            xs[p][at] = got.reshape(2, 2, 2, 2, 16, PARTS[p][2])
        swap(p, group).start()

    down(0)
    combine(0, 3)
    down(1)
    combine(1, 3)
    swap(0, 3).wait_recv()
    first(0, 2)
    down(2)
    combine(2, 3)
    swap(1, 3).wait_recv()
    first(1, 2)
    combine(0, 2)
    swap(2, 3).wait_recv()
    first(2, 2)
    combine(1, 2)
    combine(2, 2)
    for p in range(3):
        swap(p, 2).wait_recv()
        mid(p, 2)
        combine(p, 1)
        combine(p, 0)
    for p in range(3):
        swap(p, 1).wait_recv()
        swap(p, 0).wait_recv()
        first(p, 1)
        first(p, -1)
        first(p, 0)
    for p in range(3):
        mid(p, 1)
    for p in range(3):
        last(p, 2)
        mid(p, -1)
    for p in range(3):
        last(p, 1)
        mid(p, 0)
    for p in range(3):
        last(p, -1)
        second(p)
    for p in range(3):
        last(p, 0)
    for p in range(3):
        second_end(p)
    for p, (lo, n, wide) in enumerate(PARTS):
        total = mine(p, (0, 0, 0))[...].astype(jnp.float32)
        for s in range(3):
            rs_wait(p, s, rbufs[p][0].at[s])
            total = total + rbufs[p][0][s].astype(jnp.float32)
        out[:, lo : lo + n] = (resid[:, lo : lo + n] + total[:, :n]).astype(jnp.bfloat16)
    for p in range(3):
        wait_sent(p, rs_send.at[p])
        v = other(p, (ALL, ALL, ALL))
        copy(v, v, sx_send.at[p], sx_recv.at[p, 0], sibling).wait_send()


def layer(tokens, attn_gain, mlp_gain, sinks, routes, fixed, weights):
    bf = jnp.bfloat16
    wide = [p[2] for p in PARTS]
    width = tokens.shape[1]
    dma = pltpu.SemaphoreType.DMA
    scratch = (
        [pltpu.VMEM((4, 4, 4, 2, 16, h), bf) for h in wide]
        + [pltpu.VMEM((4, 256, h), bf) for h in wide]
        + [pltpu.VMEM((4, 4, 4, 16, h), bf) for h in wide]
        + [pltpu.VMEM((4, 192, width), bf)] * 3
        + [
            pltpu.VMEM((2, 48, 4, width), bf),
            pltpu.VMEM((4, 256, 192), bf),
            pltpu.VMEM((1, 2944), jnp.float32),
        ]
        + [
            pltpu.VMEM((GROUPS, 256, 128), bf),
            pltpu.VMEM((GROUPS, 128, 256), bf),
            pltpu.VMEM((4, 256, 128), jnp.float32),
            pltpu.VMEM((4, 4, 4, 2, 16, 128), bf),
            pltpu.VMEM((256, 256), bf),
        ]
        + [pltpu.VMEM((3,) + (4,) * s + (16, h), bf) for h in wide for s in range(3)]
        + [pltpu.VMEM(w.shape, bf) for w in (weights[0], weights[1], weights[2])]
        + [
            pltpu.VMEM((2, 4, 2, 16, width), bf),
            pltpu.VMEM((256, width), bf),
            pltpu.VMEM((256, 64), bf),
            pltpu.VMEM((2, 384, 64), bf),
            pltpu.VMEM((256, 256), bf),
            pltpu.VMEM((256, 256), bf),
            pltpu.VMEM((2, 4, 2, 16, width), bf),
            pltpu.VMEM((2, 4, 16, width), bf),
            pltpu.VMEM((3, 2, 16, width), bf),
            pltpu.VMEM((16, width), bf),
            pltpu.VMEM((16, 2944), jnp.float32),
        ]
        + [
            dma((5,)), dma((3,)), dma((3, 25)), dma((3,)), dma((3, 4)),
            dma((3,)), dma((3, 25)), dma((3,)), dma((3, 4)),
            dma((2,)), dma((13,)), dma((2,)), dma((9,)), dma((4,)), dma((4,)), dma((11,)), dma((11,)),
        ]
    )
    vm = pl.BlockSpec(memory_space=pltpu.VMEM)
    sm = pl.BlockSpec(memory_space=pltpu.SMEM)
    anym = pl.BlockSpec(memory_space=pl.ANY)
    return pl.pallas_call(
        layer_kernel,
        out_shape=jax.ShapeDtypeStruct(tokens.shape, bf),
        in_specs=[vm] * 3 + [sm] + [vm] * 2 + [anym] * 6,
        out_specs=vm,
        scratch_shapes=scratch,
        compiler_params=pltpu.CompilerParams(
            collective_id=1, has_side_effects=True, vmem_limit_bytes=62 * 1024 * 1024
        ),
        name="layer",
    )(tokens, attn_gain, mlp_gain, sinks, routes, fixed, *weights)


def shards(
    tokens, attn_gain, query_weight, keyval_weight, sink_logits, out_weight,
    mlp_gain, routes, gate_fixed, gate_weight, up_weight, down_weight,
):
    experts = [jnp.transpose(w, (1, 0, 2)) for w in (gate_weight, up_weight, down_weight)]
    weights = (query_weight, keyval_weight, out_weight.T, *experts)
    return layer(tokens, attn_gain, mlp_gain, sink_logits, routes.T, gate_fixed.T, weights)


def solution(mesh):
    in_specs = (
        P(("ctx", "fsdp"), None),
        P(),
        P(None, "fsdp"),
        P("fsdp", None),
        P("fsdp"),
        P("fsdp", None),
        P(),
        P(("ctx", "fsdp"), None),
        P(("ctx", "fsdp"), None),
        P("fsdp", "ctx", None),
        P("fsdp", "ctx", None),
        P("fsdp", "ctx", None),
    )
    out_specs = P(("ctx", "fsdp"), None)
    return jax.shard_map(shards, mesh=mesh, in_specs=in_specs, out_specs=out_specs, check_vma=False)
```
